256 devices in a mesh: gx: 8 (over z), gy: 8 (over y, x_hi), col: 4 (over x_lo, core).
Axes of the slice: x: 4 (x_hi: 2, x_lo: 2; x = x_hi * 2 + x_lo), y: 4, z: 8, core: 2. Of those that a mesh axis runs over, the one named last changes fastest.
Arguments:
- pre_bottom: bfloat16 [8, 16, 16, 1024], P(None, None, 'col', 'gy'), may hold values from -6 to 6
- bottom_input: bfloat16 [8, 16, 16, 1024], P(None, None, 'col', 'gx'), may hold values from -6 to 6
- bottom_weight: bfloat16 [1024, 27, 1024], P('gx', None, 'gy'), may hold values from -0.0390625 to 0.0390625
- up_weight: bfloat16 [1024, 512], P('gy'), may hold values from -0.09375 to 0.09375
- level_input: bfloat16 [16, 32, 32, 512], P('gx', 'gy', None, 'col'), may hold values from -6 to 6
- pre_level: bfloat16 [16, 32, 32, 512], P('gx', 'gy', None, 'col'), may hold values from -6 to 6
- level_cotangent: bfloat16 [16, 32, 32, 512], P('gx', 'gy', None, 'col'), may hold values from -6 to 6
- labels: int32 [16, 32, 32], P('gx', 'gy'), may hold values from 0 to 13
- level_weight: bfloat16 [512, 13824], P('col'), may hold values from -0.0546875 to 0.0546875
- aux_weight: bfloat16 [512, 14], P('col'), may hold values from -2 to 2
Outputs:
- level_input_grad: bfloat16 [16, 32, 32, 512], P('gx', 'gy', None, 'col')
- bottom_input_grad: bfloat16 [8, 16, 16, 1024], P('gy', None, 'col', 'gx')
- level_weight_grad: float32 [512, 13824], P('col', ('gx', 'gy'))
- bottom_weight_grad: float32 [1024, 27, 1024], P(('gx', 'col'), None, 'gy')
- up_weight_grad: float32 [1024, 512], P('gy', 'col')
- aux_weight_grad: float32 [512, 14], P('col')
The draws below stay inside these ranges and needn't reach their ends.
All inputs are finite; a program needn't handle non-finite values.
Results may differ from the reference program's by a relative error of at most 0.011.
Values may be sent and summed in bfloat16 or wider, within the bound.
No kernel may reach another device: no remote copies, remote signals or barrier semaphores. Data moves between devices by JAX's collectives and lax.ppermute only.
A program may use at most 64 MiB of HBM per device.

```python
import jax
import jax.numpy as jnp
from jax import lax

CU = 512
CB = 1024
CLASSES = 14
TAPS = 27
WIDTH = 32
NU_D = 16
NU_H = 32
DB = 8
HB = 16
WB = 16


def draw_pre_level(key, part):
    key = jax.random.fold_in(key, 11)
    full_shape = (NU_D, NU_H, WIDTH, CU)
    values = jnp.clip(jax.random.normal(key, full_shape, jnp.float32), -6.0, 6.0)
    return values.astype(jnp.bfloat16)


def draw_aux_weight(key, part):
    key = jax.random.fold_in(key, 23)
    spread = 5.6 / CU ** 0.5
    values = jnp.clip(jax.random.normal(key, (CU, CLASSES), jnp.float32) * spread, -1.0, 1.0)
    return values.astype(jnp.bfloat16)


def set_ends(result, key, smallest, top_value):
    dims = result.shape
    index_at = [jax.random.randint(jax.random.fold_in(key, axis), (), 0, dims[axis]) for axis in range(len(dims))]
    result = result.at[tuple(index_at)].set(smallest)
    longest = dims.index(max(dims))
    index_at[longest] = (index_at[longest] + 1) % dims[longest]
    return result.at[tuple(index_at)].set(top_value)


def steps_of(own_key, dims, split, low, largest):
    factor_of = 1.0
    for position, shards_of in split:
        heights = jax.random.uniform(jax.random.fold_in(jax.random.fold_in(own_key, 6), position), (shards_of,), jnp.float32, low / len(split), largest / len(split))
        factor_of = factor_of * jnp.repeat(jnp.exp(heights), dims[position] // shards_of).reshape((-1,) + (1,) * (len(dims) - 1 - position))
    return factor_of


def centred(own_key, dims, scale, reach, cuts=(), kind=jnp.bfloat16):
    gain = steps_of(own_key, dims, cuts, -0.22, 0.18) if cuts else 1.0
    result = jax.random.normal(own_key, dims, jnp.float32) * scale * gain
    return jnp.minimum(jnp.maximum(result, -reach), reach).astype(kind)


def setup_inputs(seed: int = 0) -> dict:
    splits = jax.random.split(jax.random.key(seed), 11)
    pre_bottom = centred(splits[0], (DB, HB, WB, CB), 1.0, 6.0, ((2, 4), (3, 8)))
    bottom_input = centred(splits[1], (DB, HB, WB, CB), 1.0, 6.0, ((2, 4), (3, 8)))
    bottom_weight = centred(splits[2], (CB, TAPS, CB), (TAPS * CB) ** -0.5, 0.0390625, ((0, 8), (2, 8)))
    up_weight = centred(splits[3], (CB, CU), (8 * CU) ** -0.5, 0.09375, ((0, 8),))
    level_input = centred(splits[4], (NU_D, NU_H, WIDTH, CU), 1.0, 6.0, ((0, 8), (1, 8), (3, 4)))
    pre_level = draw_pre_level(jax.random.fold_in(splits[10], 71), 0)
    level_cotangent = centred(splits[6], (NU_D, NU_H, WIDTH, CU), 1.0, 6.0, ((0, 8), (1, 8), (3, 4)))
    labels = set_ends(jax.random.randint(splits[7], (NU_D, NU_H, WIDTH), 0, CLASSES), jax.random.fold_in(splits[7], 1), 0, CLASSES - 1).astype(jnp.int32)
    level_weight = centred(splits[8], (CU, TAPS * CU), (TAPS * CU) ** -0.5, 0.0546875, ((0, 4),))
    aux_weight = draw_aux_weight(jax.random.fold_in(splits[10], 71), 0)
    return dict(pre_bottom=pre_bottom, bottom_input=bottom_input, bottom_weight=bottom_weight, up_weight=up_weight, level_input=level_input, pre_level=pre_level, level_cotangent=level_cotangent, labels=labels, level_weight=level_weight, aux_weight=aux_weight)


def tap_offsets():
    return [(depth_step, height_step, width_step) for depth_step in (-1, 0, 1) for height_step in (-1, 0, 1) for width_step in (-1, 0, 1)]


def taps_back(source, padded, weight):
    depth_size, height_size, width_size, inner_width = source.shape
    outer_width = padded.shape[3]
    row_count = depth_size * height_size * width_size
    flat_source = source.reshape(row_count, inner_width)
    input_grad = jnp.zeros((row_count, inner_width), jnp.float32)
    pieces = []
    for tap_index, (depth_step, height_step, width_step) in enumerate(tap_offsets()):
        shifted = lax.slice(padded, (1 - depth_step, 1 - height_step, 1 - width_step, 0), (1 - depth_step + depth_size, 1 - height_step + height_size, 1 - width_step + width_size, outer_width)).reshape(row_count, outer_width)
        tap_weight = weight[:, tap_index * outer_width:(tap_index + 1) * outer_width]
        input_grad = input_grad + lax.dot_general(shifted, tap_weight, (((1,), (1,)), ((), ())), preferred_element_type=jnp.float32)
        pieces.append(lax.dot_general(flat_source, shifted, (((0,), (0,)), ((), ())), preferred_element_type=jnp.float32))
    return input_grad.reshape(depth_size, height_size, width_size, inner_width), jnp.concatenate(pieces, axis=1)


def reference(pre_bottom, bottom_input, bottom_weight, up_weight, level_input, pre_level, level_cotangent, labels, level_weight, aux_weight):
    active_rows = jnp.maximum(pre_level, 0).reshape(-1, CU)
    logits = jnp.dot(active_rows, aux_weight, preferred_element_type=jnp.float32)
    probabilities = jax.nn.softmax(logits, axis=-1)
    onehot = (labels.reshape(-1)[:, None] == jnp.arange(CLASSES, dtype=jnp.int32)[None, :]).astype(jnp.float32)
    logit_grad = (probabilities - onehot).astype(jnp.bfloat16)
    aux_weight_grad = lax.dot_general(active_rows, logit_grad, (((0,), (0,)), ((), ())), preferred_element_type=jnp.float32)
    aux_back = lax.dot_general(logit_grad, aux_weight, (((1,), (1,)), ((), ())), preferred_element_type=jnp.float32)
    total_grad = level_cotangent.reshape(-1, CU).astype(jnp.float32) + aux_back
    level_pre_grad = jnp.where(pre_level.reshape(-1, CU) > 0, total_grad, jnp.zeros_like(total_grad)).astype(jnp.bfloat16).reshape(pre_level.shape)
    padded = jnp.pad(level_pre_grad, ((1, 1), (1, 1), (1, 1), (0, 0)))
    skip_grad, level_weight_grad = taps_back(level_input, padded, level_weight)
    level_input_grad = skip_grad.astype(jnp.bfloat16)
    down_grad = skip_grad.reshape(DB, 2, HB, 2, WB, 2, CU).sum(axis=(1, 3, 5)).astype(jnp.bfloat16)
    flat_down = down_grad.reshape(-1, CU)
    bottom_active = jnp.maximum(pre_bottom, 0).reshape(-1, CB)
    up_weight_grad = lax.dot_general(bottom_active, flat_down, (((0,), (0,)), ((), ())), preferred_element_type=jnp.float32)
    bottom_back = lax.dot_general(flat_down, up_weight, (((1,), (1,)), ((), ())), preferred_element_type=jnp.float32).reshape(pre_bottom.shape)
    bottom_pre_grad = jnp.where(pre_bottom > 0, bottom_back, jnp.zeros_like(bottom_back)).astype(jnp.bfloat16)
    bottom_padded = jnp.pad(bottom_pre_grad, ((1, 1), (1, 1), (1, 1), (0, 0)))
    flat_weight = bottom_weight.reshape(CB, TAPS * CB)
    bottom_part, bottom_weight_part = taps_back(bottom_input, bottom_padded, flat_weight)
    bottom_input_grad = bottom_part.astype(jnp.bfloat16)
    bottom_weight_grad = bottom_weight_part.reshape(CB, TAPS, CB)
    return level_input_grad, bottom_input_grad, level_weight_grad, bottom_weight_grad, up_weight_grad, aux_weight_grad
```

```python
import jax
import jax.numpy as jnp
from jax import lax
from jax.sharding import PartitionSpec as P

CLASSES = 14
TAPS = 27


def tap_offsets():
    return [
        (depth_step, height_step, width_step)
        for depth_step in (-1, 0, 1)
        for height_step in (-1, 0, 1)
        for width_step in (-1, 0, 1)
    ]


def shifted(padded, step, dims):
    starts = tuple(1 - s for s in step)
    return lax.slice(
        padded,
        starts + (0,),
        tuple(a + n for a, n in zip(starts, dims)) + (padded.shape[3],),
    ).reshape(-1, padded.shape[3])


def exchange(x, axis):
    return lax.all_to_all(x, axis, split_axis=0, concat_axis=0, tiled=False)


def spread(x, axis):
    size = lax.axis_size(axis)
    return exchange(jnp.broadcast_to(x[None], (size,) + x.shape), axis)


def neighbour(x, depth, height):
    nx, ny = lax.axis_size("gx"), lax.axis_size("gy")
    pairs = [
        (i * ny + j, (i + depth) * ny + j + height)
        for i in range(nx)
        for j in range(ny)
        if 0 <= i + depth < nx and 0 <= j + height < ny
    ]
    return lax.ppermute(x, ("gx", "gy"), pairs)


def with_halo(x):
    lines = []
    for depth in (1, 0, -1):
        part = {1: x[-1:], 0: x, -1: x[:1]}[depth]
        cells = []
        for height in (1, 0, -1):
            piece = {1: part[:, -1:], 0: part, -1: part[:, :1]}[height]
            cells.append(piece if depth == 0 and height == 0 else neighbour(piece, depth, height))
        lines.append(jnp.concatenate(cells, axis=1))
    return jnp.concatenate(lines, axis=0)


def dot_rows(a, b):
    return lax.dot_general(a, b, (((0,), (0,)), ((), ())), preferred_element_type=jnp.float32)


def dot_lanes(a, b):
    return lax.dot_general(a, b, (((1,), (1,)), ((), ())), preferred_element_type=jnp.float32)


def per_device(
    pre_bottom,
    bottom_input,
    bottom_weight,
    up_weight,
    level_input,
    pre_level,
    level_cotangent,
    labels,
    level_weight,
    aux_weight,
):
    nx, ny, nc = (lax.axis_size(a) for a in ("gx", "gy", "col"))
    depth, height, width, inner = level_input.shape
    full = inner * nc
    rows = depth * height * width
    bf16, f32 = jnp.bfloat16, jnp.float32

    ups = [(i, i + 1) for i in range(nc - 1)]
    downs = [(j, i) for i, j in ups]
    pre_before = lax.ppermute(pre_bottom[:, :, -1:], "col", ups)
    pre_after = lax.ppermute(pre_bottom[:, :, :1], "col", downs)
    pre_wide = lax.optimization_barrier(
        jnp.concatenate([pre_before, pre_bottom, pre_after], axis=2)
    )

    own_pre = pre_level.reshape(rows, inner)
    payload = jnp.concatenate(
        [own_pre, level_cotangent.reshape(rows, inner), jnp.pad(aux_weight.T, ((0, 2), (0, 0)))]
    )
    gathered = lax.all_gather(payload, "col")

    def channels(x):
        return x.transpose(1, 0, 2).reshape(x.shape[1], full)

    pre = channels(gathered[:, :rows])
    cotangent = channels(gathered[:, rows : 2 * rows])
    aux = channels(gathered[:, 2 * rows : 2 * rows + CLASSES])
    logits = dot_lanes(jnp.maximum(pre, 0), aux)
    probabilities = jax.nn.softmax(logits, axis=-1)
    onehot = (labels.reshape(-1)[:, None] == jnp.arange(CLASSES, dtype=jnp.int32)[None, :]).astype(f32)
    logit_grad = (probabilities - onehot).astype(bf16)
    aux_back = lax.dot_general(
        logit_grad, aux, (((1,), (0,)), ((), ())), preferred_element_type=f32
    )
    total_grad = cotangent.astype(f32) + aux_back
    level_pre_grad = (
        jnp.where(pre > 0, total_grad, 0.0).astype(bf16).reshape(depth, height, width, full)
    )
    aux_part = dot_rows(logit_grad, jnp.maximum(own_pre, 0)).astype(bf16)

    extended = jnp.pad(with_halo(level_pre_grad), ((0, 0), (0, 0), (1, 1), (0, 0)))
    skip_grad = jnp.zeros((rows, inner), f32)
    for tap, step in enumerate(tap_offsets()):
        piece = shifted(extended, step, (depth, height, width))
        skip_grad = skip_grad + dot_lanes(piece, level_weight[:, tap * full : (tap + 1) * full])
    level_input_grad = skip_grad.astype(bf16).reshape(level_input.shape)

    half_d, half_h, half_w = depth // 2, height // 2, width // 2
    down_local = (
        skip_grad.reshape(half_d, 2, half_h, 2, half_w, 2, inner).sum(axis=(1, 3, 5)).astype(bf16)
    )
    block = half_w // nc
    wide = block + 2
    down_padded = jnp.pad(down_local, ((0, 0), (0, 0), (1, 1), (0, 0)))
    cells = half_d * half_h * wide
    parts = jnp.stack(
        [down_padded[:, :, c * block : c * block + wide].reshape(cells, inner) for c in range(nc)]
    )
    relayed = exchange(parts, "col").reshape(nc * cells, inner)

    flat_input = level_input.reshape(rows, inner)
    pieces = [
        dot_rows(shifted(extended, step, (depth, height, width)), flat_input).astype(bf16)
        for step in tap_offsets()
    ]
    chunk = TAPS * full // (nx * ny)
    level_part = jnp.concatenate(pieces).reshape(nx, ny, chunk, inner).transpose(1, 0, 2, 3)
    level_part = exchange(level_part, "gy").astype(f32).sum(axis=0).astype(bf16)

    tail = jnp.pad(aux_part, ((0, 2), (0, 0)))
    by_depth = spread(jnp.concatenate([relayed, tail]), "gx")
    aux_sum = by_depth[:, nc * cells :].astype(f32).sum(axis=0).astype(bf16)
    line = jnp.concatenate([by_depth[:, : nc * cells].reshape(-1, inner), aux_sum])
    by_height = spread(line, "gy")
    split = nx * nc * cells
    aux_weight_grad = by_height[:, split : split + CLASSES].astype(f32).sum(axis=0).T
    down_wide = (
        by_height[:, :split]
        .reshape(ny, nx, nc, half_d, half_h, wide, inner)
        .transpose(1, 3, 0, 4, 5, 2, 6)
        .reshape(nx * half_d, ny * half_h, wide, full)
    )

    level_part = exchange(level_part, "gx").astype(f32).sum(axis=0)
    level_weight_grad = level_part.T

    bottom_d, bottom_h = pre_bottom.shape[:2]
    filters = pre_bottom.shape[3]
    bottom_back = dot_lanes(down_wide.reshape(-1, full), up_weight).reshape(pre_wide.shape)
    bottom_pre_grad = jnp.where(pre_wide > 0, bottom_back, 0.0).astype(bf16)
    flat_down = down_wide[:, :, 1:-1].reshape(-1, full)
    up_part = dot_rows(jnp.maximum(pre_bottom, 0).reshape(-1, filters), flat_down).astype(bf16)
    padded = jnp.pad(bottom_pre_grad, ((1, 1), (1, 1), (0, 0), (0, 0)))
    bottom_rows = bottom_d * bottom_h * block
    channel_width = bottom_weight.shape[0]
    source = bottom_input.reshape(bottom_rows, channel_width)
    bottom_part = jnp.zeros((bottom_rows, channel_width), f32)
    weight_parts = []
    for tap, step in enumerate(tap_offsets()):
        piece = shifted(padded, step, (bottom_d, bottom_h, block))
        bottom_part = bottom_part + dot_lanes(piece, bottom_weight[:, tap])
        weight_parts.append(dot_rows(source, piece).astype(bf16))

    share = bottom_d // ny
    bottom_part = exchange(
        bottom_part.astype(bf16).reshape(ny, share * bottom_h * block, channel_width), "gy"
    )
    bottom_input_grad = (
        bottom_part.astype(f32).sum(axis=0).astype(bf16).reshape(share, bottom_h, block, channel_width)
    )
    thin = channel_width // nc
    weight_parts = (
        jnp.stack(weight_parts)
        .reshape(TAPS, nc, thin, filters)
        .transpose(1, 0, 2, 3)
        .reshape(nc, TAPS * thin, filters)
    )
    up_parts = up_part.reshape(filters, nc, inner).transpose(1, 0, 2)
    both = exchange(jnp.concatenate([weight_parts, up_parts], axis=1), "col").astype(f32).sum(axis=0)
    bottom_weight_grad = both[: TAPS * thin].reshape(TAPS, thin, filters).transpose(1, 0, 2)
    up_weight_grad = both[TAPS * thin :]
    return (
        level_input_grad,
        bottom_input_grad,
        level_weight_grad,
        bottom_weight_grad,
        up_weight_grad,
        aux_weight_grad,
    )


def solution(mesh):
    return jax.shard_map(
        per_device,
        mesh=mesh,
        in_specs=(
            P(None, None, "col", "gy"),
            P(None, None, "col", "gx"),
            P("gx", None, "gy"),
            P("gy", None),
            P("gx", "gy", None, "col"),
            P("gx", "gy", None, "col"),
            P("gx", "gy", None, "col"),
            P("gx", "gy", None),
            P("col", None),
            P("col", None),
        ),
        out_specs=(
            P("gx", "gy", None, "col"),
            P("gy", None, "col", "gx"),
            P("col", ("gx", "gy")),
            P(("gx", "col"), None, "gy"),
            P("gy", "col"),
            P("col", None),
        ),
        check_vma=False,
    )
```

```python
import functools

import jax
import jax.numpy as jnp
from jax import lax
from jax.experimental import pallas as pl
from jax.experimental.pallas import tpu as pltpu
from jax.sharding import PartitionSpec as P

CLASSES = 14
CLASS_ROWS = 16
TAPS = 27
VMEM_LIMIT = 48 * 1024 * 1024
STEPS = (-1, 0, 1)


def exchange(x, axis):
    return lax.all_to_all(x, axis, split_axis=0, concat_axis=0, tiled=False)


def spread(x, axis):
    size = lax.axis_size(axis)
    return exchange(jnp.broadcast_to(x[None], (size,) + x.shape), axis)


def neighbour(x, depth, height):
    nx, ny = lax.axis_size("gx"), lax.axis_size("gy")
    pairs = [
        (i * ny + j, (i + depth) * ny + j + height)
        for i in range(nx)
        for j in range(ny)
        if 0 <= i + depth < nx and 0 <= j + height < ny
    ]
    return lax.ppermute(x, ("gx", "gy"), pairs)


def dot_nn(a, b):
    return lax.dot_general(a, b, (((1,), (0,)), ((), ())), preferred_element_type=jnp.float32)


def dot_tn(a, b):
    return lax.dot_general(a, b, (((0,), (0,)), ((), ())), preferred_element_type=jnp.float32)


def dot_nt(a, b):
    return lax.dot_general(a, b, (((1,), (1,)), ((), ())), preferred_element_type=jnp.float32)


def moved(x, step, period):
    if step == 0:
        return x
    rows = x.shape[0]
    place = lax.rem(lax.broadcasted_iota(jnp.int32, x.shape, 0), period)
    edge = 0 if step == 1 else period - 1
    return jnp.where(place == edge, 0.0, pltpu.roll(x, step % rows, 0))


def local_call(body, out_shapes, scratch, flops, moved_bytes, *args):
    return pl.pallas_call(
        body,
        out_shape=out_shapes,
        in_specs=[pl.BlockSpec(memory_space=pltpu.VMEM)] * len(args),
        out_specs=jax.tree.map(lambda _: pl.BlockSpec(memory_space=pltpu.VMEM), out_shapes),
        scratch_shapes=scratch,
        cost_estimate=pl.CostEstimate(flops=flops, bytes_accessed=moved_bytes, transcendentals=0),
        compiler_params=pltpu.CompilerParams(vmem_limit_bytes=VMEM_LIMIT),
    )(*args)


def class_kernel(gathered_ref, own_ref, label_ref, grad_ref, aux_ref):
    groups, rows, inner = gathered_ref.shape[0], own_ref.shape[0], own_ref.shape[1]
    logits = jnp.zeros((CLASS_ROWS, rows), jnp.float32)
    for c in range(groups):
        weight = gathered_ref[c, 2 * rows : 2 * rows + CLASS_ROWS]
        logits += dot_nt(weight, jnp.maximum(gathered_ref[c, :rows], 0))
    place = lax.broadcasted_iota(jnp.int32, logits.shape, 0)
    real = place < CLASSES
    logits = jnp.where(real, logits, -jnp.inf)
    powers = jnp.exp(logits - jnp.max(logits, axis=0, keepdims=True))
    probabilities = powers / jnp.sum(powers, axis=0, keepdims=True)
    onehot = jnp.where(place == label_ref[...], 1.0, 0.0)
    logit_grad = jnp.where(real, probabilities - onehot, 0.0).astype(jnp.bfloat16)
    for c in range(groups):
        weight = gathered_ref[c, 2 * rows : 2 * rows + CLASS_ROWS]
        total = gathered_ref[c, rows : 2 * rows].astype(jnp.float32) + dot_tn(logit_grad, weight)
        active = gathered_ref[c, :rows].astype(jnp.float32) > 0
        grad_ref[:, c * inner : (c + 1) * inner] = jnp.where(active, total, 0.0).astype(jnp.bfloat16)
    aux_ref[...] = dot_nn(logit_grad, jnp.maximum(own_ref[...], 0)).astype(jnp.bfloat16)


def conv_kernel(grad_ref, weight_ref, low_ref, mid_ref, high_ref, acc_ref):
    _, far_d, far_h, width, inner = acc_ref.shape
    depth, height = far_d - 2, far_h - 2
    full = grad_ref.shape[1]
    acc_ref[...] = jnp.zeros_like(acc_ref)
    for a in STEPS:
        for b in STEPS:
            for c in STEPS:
                tap = 9 * (a + 1) + 3 * (b + 1) + c + 1
                term = dot_nt(grad_ref[...], weight_ref[:, tap * full : (tap + 1) * full])
                acc_ref[c + 1, 1 + a : 1 + a + depth, 1 + b : 1 + b + height] += term.reshape(
                    depth, height, width, inner
                )
    for d in range(far_d):
        lines = sum(
            moved(acc_ref[c + 1, d].reshape(far_h * width, inner), c, width) for c in STEPS
        ).reshape(far_h, width, inner)
        if d == 0:
            low_ref[...] = lines.astype(jnp.bfloat16)
        elif d == far_d - 1:
            high_ref[...] = lines.astype(jnp.bfloat16)
        else:
            mid_ref[d - 1] = lines


def kernel_grad_kernel(chunk, grad_ref, input_ref, out_ref, shift_ref):
    far_d, far_h, width, inner = input_ref.shape
    depth, height = far_d - 2, far_h - 2
    rows, full = grad_ref.shape
    by_height, by_depth, window, _ = out_ref.shape
    flat = input_ref[...].astype(jnp.float32).reshape(far_d * far_h * width, inner)
    for c in STEPS:
        shift_ref[c + 1] = moved(flat, -c, width).astype(jnp.bfloat16).reshape(input_ref.shape)
    turned = grad_ref[...].T
    for a in STEPS:
        for b in STEPS:
            piece = jnp.concatenate(
                [
                    shift_ref[c, 1 + a : 1 + a + depth, 1 + b : 1 + b + height].reshape(rows, inner)
                    for c in range(3)
                ],
                axis=1,
            )
            terms = dot_nn(turned, piece).astype(jnp.bfloat16)
            for c in range(3):
                first = (9 * (a + 1) + 3 * (b + 1) + c) * full
                for owner in range(by_depth * by_height):
                    start = owner * chunk // 16 * 16
                    low, high = max(start, first), min(start + window, first + full)
                    if low < high:
                        out_ref[owner % by_height, owner // by_height, low - start : high - start] = terms[
                            low - first : high - first, c * inner : (c + 1) * inner
                        ]


def bottom_kernel(
    down_ref, up_ref, pre_ref, source_ref, weight_ref, part_ref, both_ref, shift_ref
):
    _, far_d, far_w, height, filters = shift_ref.shape
    depth, width = far_d - 2, far_w - 2
    rows = depth * width * height
    channels = source_ref.shape[1]
    groups = both_ref.shape[0]
    thin = channels // groups
    full = down_ref.shape[1]
    inner = full // groups
    back = dot_nt(down_ref[...], up_ref[...])
    saved = pre_ref[...]
    grad = jnp.where(saved.astype(jnp.float32) > 0, back, 0.0)
    shift_ref[:, :1] = jnp.zeros((3, 1) + shift_ref.shape[2:], jnp.bfloat16)
    shift_ref[:, far_d - 1 :] = jnp.zeros((3, 1) + shift_ref.shape[2:], jnp.bfloat16)
    for b in STEPS:
        shift_ref[b + 1, 1 : 1 + depth] = (
            moved(grad, b, height).astype(jnp.bfloat16).reshape(depth, far_w, height, filters)
        )
    own_down = down_ref[...].reshape(depth, far_w, height, full)[:, 1 : 1 + width].reshape(rows, full)
    own_saved = saved.reshape(depth, far_w, height, filters)[:, 1 : 1 + width].reshape(rows, filters)
    up_part = dot_tn(jnp.maximum(own_saved, 0), own_down).astype(jnp.bfloat16)
    for cc in range(groups):
        both_ref[cc, TAPS * thin :] = up_part[:, cc * inner : (cc + 1) * inner]
    turned = source_ref[...].T
    total = jnp.zeros((rows, channels), jnp.float32)
    for a in STEPS:
        for b in STEPS:
            tap = 9 * (a + 1) + 3 * (b + 1)
            piece = jnp.concatenate(
                [
                    shift_ref[b + 1, 1 - a : 1 - a + depth, 1 - c : 1 - c + width].reshape(rows, filters)
                    for c in STEPS
                ],
                axis=1,
            )
            weight = jnp.concatenate([weight_ref[tap + c] for c in range(3)], axis=1)
            total += dot_nt(piece, weight)
            terms = dot_nn(turned, piece).astype(jnp.bfloat16)
            for c in range(3):
                for cc in range(groups):
                    both_ref[cc, (tap + c) * thin : (tap + c + 1) * thin] = terms[
                        cc * thin : (cc + 1) * thin, c * filters : (c + 1) * filters
                    ]
    part_ref[...] = total.astype(jnp.bfloat16)


def per_device(
    pre_bottom,
    bottom_input,
    bottom_weight,
    up_weight,
    level_input,
    pre_level,
    level_cotangent,
    labels,
    level_weight,
    aux_weight,
):
    nx, ny, nc = (lax.axis_size(a) for a in ("gx", "gy", "col"))
    depth, height, width, inner = level_input.shape
    full = inner * nc
    rows = depth * height * width
    far_d, far_h = depth + 2, height + 2
    bf16, f32 = jnp.bfloat16, jnp.float32
    struct = jax.ShapeDtypeStruct

    own_pre = pre_level.reshape(rows, inner)
    payload = jnp.concatenate(
        [
            own_pre,
            level_cotangent.reshape(rows, inner),
            jnp.pad(aux_weight.T, ((0, CLASS_ROWS - CLASSES), (0, 0))),
        ]
    )
    gathered = spread(payload, "col")

    lines = jnp.concatenate(
        [neighbour(level_input[-1:], 1, 0), level_input, neighbour(level_input[:1], -1, 0)], axis=0
    )
    input_far = jnp.concatenate(
        [neighbour(lines[:, -1:], 0, 1), lines, neighbour(lines[:, :1], 0, -1)], axis=1
    )

    turned_pre = pre_bottom.transpose(0, 2, 1, 3)
    ups = [(i, i + 1) for i in range(nc - 1)]
    downs = [(j, i) for i, j in ups]
    pre_wide = jnp.concatenate(
        [
            lax.ppermute(turned_pre[:, -1:], "col", ups),
            turned_pre,
            lax.ppermute(turned_pre[:, :1], "col", downs),
        ],
        axis=1,
    )

    level_pre_grad, aux_part = local_call(
        class_kernel,
        (struct((rows, full), bf16), struct((CLASS_ROWS, inner), bf16)),
        [],
        6 * rows * full * CLASS_ROWS,
        2 * gathered.size,
        gathered,
        own_pre,
        labels.reshape(1, rows),
    )

    low, mid, high = local_call(
        conv_kernel,
        (
            struct((far_h, width, inner), bf16),
            struct((depth, far_h, width, inner), f32),
            struct((far_h, width, inner), bf16),
        ),
        [pltpu.VMEM((3, far_d, far_h, width, inner), f32)],
        2 * rows * full * TAPS * inner,
        2 * level_weight.size,
        level_pre_grad,
        level_weight,
    )
    from_low = neighbour(high, 1, 0)
    from_high = neighbour(low, -1, 0)
    mid = jnp.concatenate([(mid[0] + from_low)[None], mid[1:-1], (mid[-1] + from_high)[None]], axis=0)
    before = neighbour(mid[:, -1].astype(bf16), 0, 1)
    after = neighbour(mid[:, 0].astype(bf16), 0, -1)

    chunk = TAPS * full // (nx * ny)
    window = chunk + 8 if chunk % 16 else chunk
    level_part = local_call(
        functools.partial(kernel_grad_kernel, chunk),
        struct((ny, nx, window, inner), bf16),
        [pltpu.VMEM((3, far_d, far_h, width, inner), bf16)],
        2 * rows * full * TAPS * inner,
        2 * nx * ny * window * inner,
        level_pre_grad,
        input_far,
    )
    level_part = exchange(level_part, "gy").astype(f32).sum(axis=0).astype(bf16)
    level_part = exchange(level_part, "gx").astype(f32).sum(axis=0)
    if window != chunk:
        odd = lax.rem(lax.axis_index("gy") + lax.axis_index("gx") * ny, 2)
        level_part = jnp.where(odd == 1, level_part[window - chunk :], level_part[:chunk])
    level_weight_grad = level_part.T

    skip_grad = jnp.concatenate(
        [
            (mid[:, 1] + before)[:, None],
            mid[:, 2 : far_h - 2],
            (mid[:, far_h - 2] + after)[:, None],
        ],
        axis=1,
    )
    level_input_grad = skip_grad.astype(bf16)

    half_d, half_h, half_w = depth // 2, height // 2, width // 2
    down_local = (
        skip_grad.reshape(half_d, 2, half_h, 2, half_w, 2, inner).sum(axis=(1, 3, 5)).astype(bf16)
    )
    block = half_w // nc
    wide = block + 2
    down_padded = jnp.pad(down_local, ((0, 0), (0, 0), (1, 1), (0, 0)))
    cells = half_d * half_h * wide
    parts = jnp.stack(
        [down_padded[:, :, c * block : c * block + wide].reshape(cells, inner) for c in range(nc)]
    )
    relayed = exchange(parts, "col").reshape(nc * cells, inner)

    by_depth = spread(jnp.concatenate([relayed, aux_part]), "gx")
    aux_sum = by_depth[:, nc * cells :].astype(f32).sum(axis=0).astype(bf16)
    line = jnp.concatenate([by_depth[:, : nc * cells].reshape(-1, inner), aux_sum])
    by_height = spread(line, "gy")
    split = nx * nc * cells
    aux_weight_grad = by_height[:, split : split + CLASSES].astype(f32).sum(axis=0).T
    bottom_d, bottom_h, _, filters = pre_bottom.shape
    down_wide = (
        by_height[:, :split]
        .reshape(ny, nx, nc, half_d, half_h, wide, inner)
        .transpose(1, 3, 5, 0, 4, 2, 6)
        .reshape(bottom_d * wide * bottom_h, full)
    )

    bottom_rows = bottom_d * block * bottom_h
    channel_width = bottom_weight.shape[0]
    thin = channel_width // nc
    part, both = local_call(
        bottom_kernel,
        (
            struct((bottom_rows, channel_width), bf16),
            struct((nc, TAPS * thin + filters, inner), bf16),
        ),
        [pltpu.VMEM((3, bottom_d + 2, wide, bottom_h, filters), bf16)],
        4 * bottom_rows * channel_width * TAPS * filters,
        2 * bottom_weight.size,
        down_wide,
        up_weight,
        pre_wide.reshape(-1, filters),
        bottom_input.transpose(0, 2, 1, 3).reshape(bottom_rows, channel_width),
        bottom_weight.transpose(1, 0, 2),
    )
    share = bottom_d // ny
    bottom_input_grad = (
        exchange(part.reshape(ny, bottom_rows // ny, channel_width), "gy")
        .astype(f32)
        .sum(axis=0)
        .astype(bf16)
        .reshape(share, block, bottom_h, channel_width)
        .transpose(0, 2, 1, 3)
    )
    both = exchange(both, "col").astype(f32).sum(axis=0)
    bottom_weight_grad = both[: TAPS * thin].reshape(TAPS, thin, filters).transpose(1, 0, 2)
    up_weight_grad = both[TAPS * thin :]
    return (
        level_input_grad,
        bottom_input_grad,
        level_weight_grad,
        bottom_weight_grad,
        up_weight_grad,
        aux_weight_grad,
    )


def solution(mesh):
    return jax.shard_map(
        per_device,
        mesh=mesh,
        in_specs=(
            P(None, None, "col", "gy"),
            P(None, None, "col", "gx"),
            P("gx", None, "gy"),
            P("gy", None),
            P("gx", "gy", None, "col"),
            P("gx", "gy", None, "col"),
            P("gx", "gy", None, "col"),
            P("gx", "gy", None),
            P("col", None),
            P("col", None),
        ),
        out_specs=(
            P("gx", "gy", None, "col"),
            P("gy", None, "col", "gx"),
            P("col", ("gx", "gy")),
            P(("gx", "col"), None, "gy"),
            P("gy", "col"),
            P("col", None),
        ),
        check_vma=False,
    )
```

```python
import functools

import jax
import jax.numpy as jnp
from jax import lax
from jax.experimental import pallas as pl
from jax.experimental.pallas import tpu as pltpu
from jax.sharding import PartitionSpec as P

CLASSES = 14
CLASS_ROWS = 16
TAPS = 27
VMEM_LIMIT = 48 * 1024 * 1024
STEPS = (-1, 0, 1)


def exchange(x, axis):
    return lax.all_to_all(x, axis, split_axis=0, concat_axis=0, tiled=False)


def spread(x, axis):
    size = lax.axis_size(axis)
    return exchange(jnp.broadcast_to(x[None], (size,) + x.shape), axis)


def behind(x, *others):
    return lax.optimization_barrier((x,) + others)[0]


def neighbour(x, depth, height):
    nx, ny = lax.axis_size("gx"), lax.axis_size("gy")
    pairs = [
        (i * ny + j, (i + depth) * ny + j + height)
        for i in range(nx)
        for j in range(ny)
        if 0 <= i + depth < nx and 0 <= j + height < ny
    ]
    return lax.ppermute(x, ("gx", "gy"), pairs)


def bits_of(axis):
    return [1 << k for k in reversed(range(lax.axis_size(axis).bit_length() - 1))]


def swap(x, axis, bit):
    return lax.ppermute(x, axis, [(i, i ^ bit) for i in range(lax.axis_size(axis))])


def mine_and_other(x, axis, bit, dim):
    own = lax.axis_index(axis) // bit % 2
    take = functools.partial(lax.dynamic_index_in_dim, x, axis=dim, keepdims=False)
    return take(own), take(1 - own)


def in_order(own, other, axis, bit, dim):
    flag = lax.axis_index(axis) // bit % 2 == 1
    first = jnp.where(flag, other, own)
    second = jnp.where(flag, own, other)
    return jnp.stack([first, second], axis=dim)


def gathered_by_pairs(x, axis):
    steps = [x]
    for k, bit in enumerate(bits_of(axis)):
        x = in_order(x, swap(x, axis, bit), axis, bit, k)
        steps.append(x)
    size = lax.axis_size(axis)
    return x.reshape((size,) + x.shape[len(steps) - 1 :]), steps


def exchanged_by_pairs(x, axis):
    shape = x.shape
    bits = bits_of(axis)
    x = x.reshape((2,) * len(bits) + shape[1:])
    steps = []
    for k, bit in reversed(list(enumerate(bits))):
        own, other = mine_and_other(x, axis, bit, k)
        x = in_order(own, swap(other, axis, bit), axis, bit, k)
        steps.append(x)
    return x.reshape(shape), steps


def summed_by_pairs(x, axis, bits):
    names = bits_of(axis)
    x = x.reshape((2,) * len(names) + x.shape[1:])
    left = list(names)
    steps = []
    for bit in bits:
        own, other = mine_and_other(x, axis, bit, left.index(bit))
        left.remove(bit)
        x = own.astype(jnp.float32) + swap(other.astype(jnp.bfloat16), axis, bit).astype(jnp.float32)
        steps.append(x)
    return x, steps


def dot_nn(a, b):
    return lax.dot_general(a, b, (((1,), (0,)), ((), ())), preferred_element_type=jnp.float32)


def dot_tn(a, b):
    return lax.dot_general(a, b, (((0,), (0,)), ((), ())), preferred_element_type=jnp.float32)


def dot_nt(a, b):
    return lax.dot_general(a, b, (((1,), (1,)), ((), ())), preferred_element_type=jnp.float32)


def moved(x, step, period):
    if step == 0:
        return x
    rows = x.shape[0]
    place = lax.rem(lax.broadcasted_iota(jnp.int32, x.shape, 0), period)
    edge = 0 if step == 1 else period - 1
    return jnp.where(place == edge, 0.0, pltpu.roll(x, step % rows, 0))


def local_call(body, out_shapes, scratch, flops, moved_bytes, *args):
    return pl.pallas_call(
        body,
        out_shape=out_shapes,
        in_specs=[
            pl.BlockSpec(memory_space=pltpu.SMEM if a.ndim == 1 else pltpu.VMEM) for a in args
        ],
        out_specs=jax.tree.map(lambda _: pl.BlockSpec(memory_space=pltpu.VMEM), out_shapes),
        scratch_shapes=scratch,
        cost_estimate=pl.CostEstimate(flops=flops, bytes_accessed=moved_bytes, transcendentals=0),
        compiler_params=pltpu.CompilerParams(vmem_limit_bytes=VMEM_LIMIT),
    )(*args)


def class_kernel(gathered_ref, own_ref, label_ref, grad_ref, turned_ref, aux_ref):
    groups, rows, inner = gathered_ref.shape[0], own_ref.shape[0], own_ref.shape[1]
    owners, piece_rows, lanes = turned_ref.shape
    logits = jnp.zeros((CLASS_ROWS, rows), jnp.float32)
    for c in range(groups):
        weight = gathered_ref[c, 2 * rows : 2 * rows + CLASS_ROWS]
        logits += dot_nt(weight, jnp.maximum(gathered_ref[c, :rows], 0))
    place = lax.broadcasted_iota(jnp.int32, logits.shape, 0)
    real = place < CLASSES
    logits = jnp.where(real, logits, -jnp.inf)
    powers = jnp.exp(logits - jnp.max(logits, axis=0, keepdims=True))
    probabilities = powers / jnp.sum(powers, axis=0, keepdims=True)
    onehot = jnp.where(place == label_ref[...], 1.0, 0.0)
    logit_grad = jnp.where(real, probabilities - onehot, 0.0).astype(jnp.bfloat16)
    granules = []
    for c in range(groups):
        weight = gathered_ref[c, 2 * rows : 2 * rows + CLASS_ROWS]
        total = gathered_ref[c, rows : 2 * rows].astype(jnp.float32) + dot_tn(logit_grad, weight)
        active = gathered_ref[c, :rows].astype(jnp.float32) > 0
        grad = jnp.where(active, total, 0.0)
        grad_ref[:, c * inner : (c + 1) * inner] = grad.astype(jnp.bfloat16)
        turned = grad.T
        granules += [turned[8 * q : 8 * q + 8] for q in range(inner // 8)]
    for i in range(owners):
        mine = jnp.concatenate(granules[i::owners], axis=0).astype(jnp.bfloat16)
        size = mine.shape[0]
        for k in range(rows // lanes):
            turned_ref[i, k * size : (k + 1) * size] = mine[:, k * lanes : (k + 1) * lanes]
    aux_ref[...] = dot_nn(logit_grad, jnp.maximum(own_ref[...], 0)).astype(jnp.bfloat16)


def conv_kernel(place_ref, grad_ref, weight_ref, edge_ref, mid_ref, part_ref, acc_ref, sum_ref, pool_ref):
    _, far_d, far_h, width, inner = acc_ref.shape
    depth, height = far_d - 2, far_h - 2
    full = grad_ref.shape[1]
    ny, nc = part_ref.shape[:2]
    at_y = place_ref[0]
    acc_ref[...] = jnp.zeros_like(acc_ref)
    for a in STEPS:
        for b in STEPS:
            for c in STEPS:
                tap = 9 * (a + 1) + 3 * (b + 1) + c + 1
                term = dot_nt(grad_ref[...], weight_ref[:, tap * full : (tap + 1) * full])
                acc_ref[c + 1, 1 + a : 1 + a + depth, 1 + b : 1 + b + height] += term.reshape(
                    depth, height, width, inner
                )
    planes = []
    for d in range(far_d):
        planes.append(
            sum(
                moved(acc_ref[c + 1, d].reshape(far_h * width, inner), c, width) for c in STEPS
            ).reshape(far_h, width, inner)
        )
    edge_ref[0] = planes[0].astype(jnp.bfloat16)
    edge_ref[1] = planes[-1].astype(jnp.bfloat16)
    for d in range(depth):
        mid_ref[d] = planes[d + 1]
    half_h, half_w = height // 2, width // 2
    block = half_w // nc
    blocks = [planes[0], sum(planes[1 : 1 + depth]), planes[-1]]
    pool_ref[...] = jnp.zeros_like(pool_ref)
    for k, lines in enumerate(blocks):
        rows = [lines[0]]
        rows += [lines[1 + 2 * h] + lines[2 + 2 * h] for h in range(half_h)]
        rows += [lines[far_h - 1]]
        for h, row in enumerate(rows):
            sum_ref[k, h] = row
            pool_ref[k, h, 8 : 8 + half_w] = (
                sum_ref[k, h, pl.ds(0, half_w, stride=2)] + sum_ref[k, h, pl.ds(1, half_w, stride=2)]
            )
    part_ref[...] = jnp.zeros_like(part_ref)
    window = part_ref.shape[2] // (3 * half_h)
    empty = jnp.zeros((window, inner), jnp.float32)

    def put(to, first):
        for c in range(nc):
            for k in range(3):
                cells = []
                for h in range(half_h):
                    line = first + h
                    if 0 <= line < half_h + 2:
                        start = 7 + c * block
                        cells.append(pool_ref[k, line, start : start + window])
                    else:
                        cells.append(empty)
                size = half_h * window
                part_ref[to, c, k * size : (k + 1) * size] = jnp.concatenate(cells, axis=0).astype(
                    jnp.bfloat16
                )

    put(at_y, 1)

    @pl.when(at_y > 0)
    def _():
        put(at_y - 1, 1 - half_h)

    @pl.when(at_y < ny - 1)
    def _():
        put(at_y + 1, 1 + half_h)


def kernel_grad_kernel(granules, turned_ref, input_ref, out_ref, shift_ref, all_ref):
    blocks, piece_rows, lanes = turned_ref.shape
    all_d, far_h, width, inner = input_ref.shape
    height = far_h - 2
    per_block = all_d // blocks
    size = piece_rows // per_block
    cells = all_d * height * width
    owners, window, _ = out_ref.shape
    empty = jnp.zeros((3, 1) + shift_ref.shape[2:], jnp.bfloat16)
    shift_ref[:, :1] = empty
    shift_ref[:, all_d + 1 :] = empty
    flat = input_ref[...].astype(jnp.float32).reshape(all_d * far_h * width, inner)
    for c in STEPS:
        shift_ref[c + 1, 1 : 1 + all_d] = (
            moved(flat, -c, width).astype(jnp.bfloat16).reshape(input_ref.shape)
        )
    turned = jnp.concatenate(
        [
            turned_ref[k, d * size : (d + 1) * size]
            for k in range(blocks)
            for d in range(per_block)
        ],
        axis=1,
    )
    for a in STEPS:
        for b in STEPS:
            piece = jnp.concatenate(
                [
                    shift_ref[c, 1 + a : 1 + a + all_d, 1 + b : 1 + b + height].reshape(cells, inner)
                    for c in range(3)
                ],
                axis=1,
            )
            terms = dot_nn(turned, piece)
            for c in range(3):
                tap = 9 * (a + 1) + 3 * (b + 1) + c
                all_ref[tap * size : (tap + 1) * size] = terms[:, c * inner : (c + 1) * inner]
    all_ref[TAPS * size :] = jnp.zeros((window, inner), jnp.float32)
    for owner in range(owners):
        start = owner * granules // blocks * 8
        out_ref[owner] = all_ref[start : start + window].astype(jnp.bfloat16)


def bottom_kernel(
    down_ref, up_ref, pre_ref, source_ref, weight_ref, part_ref, both_ref, shift_ref
):
    _, far_d, far_w, height, filters = shift_ref.shape
    depth, width = far_d - 2, far_w - 2
    rows = depth * width * height
    channels = source_ref.shape[1]
    groups = both_ref.shape[0]
    thin = channels // groups
    full = down_ref.shape[1]
    inner = full // groups
    back = dot_nt(down_ref[...], up_ref[...])
    saved = pre_ref[...]
    grad = jnp.where(saved.astype(jnp.float32) > 0, back, 0.0)
    shift_ref[:, :1] = jnp.zeros((3, 1) + shift_ref.shape[2:], jnp.bfloat16)
    shift_ref[:, far_d - 1 :] = jnp.zeros((3, 1) + shift_ref.shape[2:], jnp.bfloat16)
    for b in STEPS:
        shift_ref[b + 1, 1 : 1 + depth] = (
            moved(grad, b, height).astype(jnp.bfloat16).reshape(depth, far_w, height, filters)
        )
    own_down = down_ref[...].reshape(depth, far_w, height, full)[:, 1 : 1 + width].reshape(rows, full)
    own_saved = saved.reshape(depth, far_w, height, filters)[:, 1 : 1 + width].reshape(rows, filters)
    up_part = dot_tn(jnp.maximum(own_saved, 0), own_down).astype(jnp.bfloat16)
    for cc in range(groups):
        both_ref[cc, TAPS * thin :] = up_part[:, cc * inner : (cc + 1) * inner]
    turned = source_ref[...].T
    total = jnp.zeros((rows, channels), jnp.float32)
    for a in STEPS:
        for b in STEPS:
            tap = 9 * (a + 1) + 3 * (b + 1)
            piece = jnp.concatenate(
                [
                    shift_ref[b + 1, 1 - a : 1 - a + depth, 1 - c : 1 - c + width].reshape(rows, filters)
                    for c in STEPS
                ],
                axis=1,
            )
            weight = jnp.concatenate([weight_ref[tap + c] for c in range(3)], axis=1)
            total += dot_nt(piece, weight)
            terms = dot_nn(turned, piece).astype(jnp.bfloat16)
            for c in range(3):
                for cc in range(groups):
                    both_ref[cc, (tap + c) * thin : (tap + c + 1) * thin] = terms[
                        cc * thin : (cc + 1) * thin, c * filters : (c + 1) * filters
                    ]
    part_ref[...] = total.astype(jnp.bfloat16)


def per_device(
    pre_bottom,
    bottom_input,
    bottom_weight,
    up_weight,
    level_input,
    pre_level,
    level_cotangent,
    labels,
    level_weight,
    aux_weight,
):
    nx, ny, nc = (lax.axis_size(a) for a in ("gx", "gy", "col"))
    at_x, at_y, at_c = (lax.axis_index(a) for a in ("gx", "gy", "col"))
    depth, height, width, inner = level_input.shape
    full = inner * nc
    rows = depth * height * width
    far_d, far_h = depth + 2, height + 2
    half_d, half_h, half_w = depth // 2, height // 2, width // 2
    block = half_w // nc
    wide = block + 2
    bottom_d, bottom_h, _, filters = pre_bottom.shape
    bf16, f32 = jnp.bfloat16, jnp.float32
    struct = jax.ShapeDtypeStruct

    own_pre = pre_level.reshape(rows, inner)
    turned_pre = pre_bottom.transpose(0, 2, 1, 3)
    payload = jnp.concatenate(
        [
            own_pre,
            level_cotangent.reshape(rows, inner),
            jnp.pad(aux_weight.T, ((0, CLASS_ROWS - CLASSES), (0, 0))),
        ]
    )
    first_edge = turned_pre[:, 0].reshape(-1, filters)
    last_edge = turned_pre[:, -1].reshape(-1, filters)
    payload = jnp.stack(
        [
            jnp.concatenate([payload, jnp.where(at_c < c, last_edge, first_edge)], axis=0)
            for c in range(nc)
        ]
    )
    gathered = exchange(payload, "col")
    edges = gathered[:, 2 * rows + CLASS_ROWS :].reshape(nc, bottom_d, 1, bottom_h, filters)

    def edge_of(c):
        found = lax.dynamic_index_in_dim(edges, jnp.clip(c, 0, nc - 1), 0, keepdims=False)
        return jnp.where((c >= 0) & (c < nc), found, jnp.zeros_like(found))

    pre_wide = jnp.concatenate([edge_of(at_c - 1), turned_pre, edge_of(at_c + 1)], axis=1)

    size = full // nx
    lanes = height * width
    level_pre_grad, turned_grad, aux_part = local_call(
        class_kernel,
        (
            struct((rows, full), bf16),
            struct((nx, depth * size, lanes), bf16),
            struct((CLASS_ROWS, inner), bf16),
        ),
        [],
        6 * rows * full * CLASS_ROWS,
        2 * gathered.size,
        gathered,
        own_pre,
        labels.reshape(1, rows),
    )

    window = (wide + 7) // 8 * 8
    edge, mid, parts = local_call(
        conv_kernel,
        (
            struct((2, far_h, width, inner), bf16),
            struct((depth, far_h, width, inner), f32),
            struct((ny, nc, 3 * half_h * window, inner), bf16),
        ),
        [
            pltpu.VMEM((3, far_d, far_h, width, inner), f32),
            pltpu.VMEM((3, half_h + 2, width, inner), f32),
            pltpu.VMEM((3, half_h + 2, half_w + 24, inner), f32),
        ],
        2 * rows * full * TAPS * inner,
        2 * level_weight.size,
        jnp.full((1,), at_y, jnp.int32),
        level_pre_grad,
        level_weight,
    )

    near = behind(level_input, parts)
    input_far = jnp.concatenate(
        [neighbour(near[:, -1:], 0, 1), near, neighbour(near[:, :1], 0, -1)], axis=1
    )
    moved_grad, moved_steps = exchanged_by_pairs(behind(turned_grad, parts), "gx")

    relayed = exchange(parts.reshape(ny * nc, 3 * half_h * window, inner), ("gy", "col"))
    relayed = (
        relayed.reshape(ny, nc, 3 * half_h, window, inner)[:, :, :, :wide]
        .astype(f32)
        .sum(axis=0)
        .astype(bf16)
        .reshape(nc * 3 * half_h * wide, inner)
    )

    relayed = behind(relayed, input_far, moved_steps[1])
    input_all, input_steps = gathered_by_pairs(input_far, "gx")
    input_all = input_all.reshape(nx * depth, far_h, width, inner)

    by_depth = spread(jnp.concatenate([relayed, aux_part]), "gx")
    split = nc * 3 * half_h * wide
    aux_sum = by_depth[:, split:].astype(f32).sum(axis=0).astype(bf16)
    down = by_depth[:, :split].reshape(nx, nc, 3, half_h, wide, inner).astype(f32)
    line = (
        down[:, :, 1]
        + jnp.pad(down[1:, :, 0], ((0, 1), (0, 0), (0, 0), (0, 0), (0, 0)))
        + jnp.pad(down[:-1, :, 2], ((1, 0), (0, 0), (0, 0), (0, 0), (0, 0)))
    ).astype(bf16)

    line = behind(line, input_steps[2], moved_grad)
    split = nx * nc * half_h * wide
    by_height = spread(jnp.concatenate([line.reshape(split, inner), aux_sum]), "gy")
    aux_weight_grad = by_height[:, split : split + CLASSES].astype(f32).sum(axis=0).T
    down_wide = (
        by_height[:, :split]
        .reshape(ny, nx, nc, half_h, wide, inner)
        .transpose(1, 4, 0, 3, 2, 5)
        .reshape(bottom_d * wide * bottom_h, full)
    )

    chunk = TAPS * full // (nx * ny)
    granules = chunk // 8
    slots = max((granules * o % nx + granules - 1) // nx + 1 for o in range(nx * ny))
    slots += slots % 2
    level_part = local_call(
        functools.partial(kernel_grad_kernel, granules),
        struct((nx * ny, 8 * slots, inner), bf16),
        [
            pltpu.VMEM((3, nx * depth + 2, far_h, width, inner), bf16),
            pltpu.VMEM((TAPS * size + 8 * slots, inner), f32),
        ],
        2 * rows * full * TAPS * inner,
        2 * nx * ny * slots * 8 * inner,
        moved_grad,
        input_all,
    )
    level_part = level_part.reshape(nx, ny, slots * 8, inner).transpose(1, 0, 2, 3)
    summed, sum_steps = summed_by_pairs(level_part, "gy", (2, 4, 1) if ny == 8 else bits_of("gy"))
    down_wide = behind(down_wide, sum_steps[0])
    level_part, _ = exchanged_by_pairs(summed.astype(bf16), "gx")
    level_part = (
        level_part.reshape(nx, slots, 8, inner).transpose(1, 0, 2, 3).reshape(-1, inner).astype(f32)
    )
    begin = lax.rem((at_x * ny + at_y) * granules, nx) * 8
    level_weight_grad = lax.dynamic_slice_in_dim(level_part, begin, chunk, axis=0).T

    bottom_rows = bottom_d * block * bottom_h
    channel_width = bottom_weight.shape[0]
    thin = channel_width // nc
    part, both = local_call(
        bottom_kernel,
        (
            struct((bottom_rows, channel_width), bf16),
            struct((nc, TAPS * thin + filters, inner), bf16),
        ),
        [pltpu.VMEM((3, bottom_d + 2, wide, bottom_h, filters), bf16)],
        4 * bottom_rows * channel_width * TAPS * filters,
        2 * bottom_weight.size,
        down_wide,
        up_weight,
        pre_wide.reshape(-1, filters),
        bottom_input.transpose(0, 2, 1, 3).reshape(bottom_rows, channel_width),
        bottom_weight.transpose(1, 0, 2),
    )
    edge = behind(edge, down_wide)
    mid = jnp.concatenate(
        [
            (mid[0] + neighbour(edge[1], 1, 0))[None],
            mid[1:-1],
            (mid[-1] + neighbour(edge[0], -1, 0))[None],
        ],
        axis=0,
    )
    before = neighbour(mid[:, -1].astype(bf16), 0, 1)
    after = neighbour(mid[:, 0].astype(bf16), 0, -1)
    level_input_grad = jnp.concatenate(
        [
            (mid[:, 1] + before)[:, None],
            mid[:, 2 : far_h - 2],
            (mid[:, far_h - 2] + after)[:, None],
        ],
        axis=1,
    ).astype(bf16)
    share = bottom_d // ny
    bottom_input_grad = (
        exchange(part.reshape(ny, bottom_rows // ny, channel_width), "gy")
        .astype(f32)
        .sum(axis=0)
        .astype(bf16)
        .reshape(share, block, bottom_h, channel_width)
        .transpose(0, 2, 1, 3)
    )
    both, _ = summed_by_pairs(both, "col", bits_of("col")[::-1])
    bottom_weight_grad = both[: TAPS * thin].reshape(TAPS, thin, filters).transpose(1, 0, 2)
    up_weight_grad = both[TAPS * thin :]
    return (
        level_input_grad,
        bottom_input_grad,
        level_weight_grad,
        bottom_weight_grad,
        up_weight_grad,
        aux_weight_grad,
    )


def solution(mesh):
    return jax.shard_map(
        per_device,
        mesh=mesh,
        in_specs=(
            P(None, None, "col", "gy"),
            P(None, None, "col", "gx"),
            P("gx", None, "gy"),
            P("gy", None),
            P("gx", "gy", None, "col"),
            P("gx", "gy", None, "col"),
            P("gx", "gy", None, "col"),
            P("gx", "gy", None),
            P("col", None),
            P("col", None),
        ),
        out_specs=(
            P("gx", "gy", None, "col"),
            P("gy", None, "col", "gx"),
            P("col", ("gx", "gy")),
            P(("gx", "col"), None, "gy"),
            P("gy", "col"),
            P("col", None),
        ),
        check_vma=False,
    )
```

```python
import functools

import jax
import jax.numpy as jnp
from jax import lax
from jax.experimental import pallas as pl
from jax.experimental.pallas import tpu as pltpu
from jax.sharding import PartitionSpec as P

CLASSES = 14
CLASS_ROWS = 16
TAPS = 27
VMEM_LIMIT = 48 * 1024 * 1024
STEPS = (-1, 0, 1)


def exchange(x, axis):
    return lax.all_to_all(x, axis, split_axis=0, concat_axis=0, tiled=False)


def spread(x, axis):
    size = lax.axis_size(axis)
    return exchange(jnp.broadcast_to(x[None], (size,) + x.shape), axis)


def behind(x, *others):
    return lax.optimization_barrier((x,) + others)[0]


def neighbour(x, depth, height):
    nx, ny = lax.axis_size("gx"), lax.axis_size("gy")
    pairs = [
        (i * ny + j, (i + depth) * ny + j + height)
        for i in range(nx)
        for j in range(ny)
        if 0 <= i + depth < nx and 0 <= j + height < ny
    ]
    return lax.ppermute(x, ("gx", "gy"), pairs)


def bits_of(axis):
    return [1 << k for k in reversed(range(lax.axis_size(axis).bit_length() - 1))]


def swap(x, axis, bit):
    return lax.ppermute(x, axis, [(i, i ^ bit) for i in range(lax.axis_size(axis))])


def mine_and_other(x, axis, bit, dim):
    own = lax.axis_index(axis) // bit % 2
    take = functools.partial(lax.dynamic_index_in_dim, x, axis=dim, keepdims=False)
    return take(own), take(1 - own)


def summed_by_pairs(x, axis, bits):
    names = bits_of(axis)
    x = x.reshape((2,) * len(names) + x.shape[1:])
    left = list(names)
    steps = []
    for bit in bits:
        own, other = mine_and_other(x, axis, bit, left.index(bit))
        left.remove(bit)
        x = own.astype(jnp.float32) + swap(other.astype(jnp.bfloat16), axis, bit).astype(jnp.float32)
        steps.append(x)
    return x, steps


def dot_nn(a, b):
    return lax.dot_general(a, b, (((1,), (0,)), ((), ())), preferred_element_type=jnp.float32)


def dot_tn(a, b):
    return lax.dot_general(a, b, (((0,), (0,)), ((), ())), preferred_element_type=jnp.float32)


def dot_nt(a, b):
    return lax.dot_general(a, b, (((1,), (1,)), ((), ())), preferred_element_type=jnp.float32)


def moved(x, step, period):
    if step == 0:
        return x
    rows = x.shape[0]
    place = lax.rem(lax.broadcasted_iota(jnp.int32, x.shape, 0), period)
    edge = 0 if step == 1 else period - 1
    return jnp.where(place == edge, 0.0, pltpu.roll(x, step % rows, 0))


def local_call(body, out_shapes, scratch, flops, moved_bytes, *args):
    return pl.pallas_call(
        body,
        out_shape=list(out_shapes),
        in_specs=[
            pl.BlockSpec(memory_space=pltpu.SMEM if a.ndim == 1 else pltpu.VMEM) for a in args
        ],
        out_specs=[pl.BlockSpec(memory_space=pltpu.VMEM)] * len(out_shapes),
        scratch_shapes=scratch,
        cost_estimate=pl.CostEstimate(flops=flops, bytes_accessed=moved_bytes, transcendentals=0),
        compiler_params=pltpu.CompilerParams(vmem_limit_bytes=VMEM_LIMIT),
    )(*args)


def class_kernel(gathered_ref, own_ref, label_ref, *out_refs):
    plane_refs, aux_ref = out_refs[:-1], out_refs[-1]
    groups, rows, inner = gathered_ref.shape[0], own_ref.shape[0], own_ref.shape[1]
    logits = jnp.zeros((CLASS_ROWS, rows), jnp.float32)
    for c in range(groups):
        weight = gathered_ref[c, 2 * rows : 2 * rows + CLASS_ROWS]
        logits += dot_nt(weight, jnp.maximum(gathered_ref[c, :rows], 0))
    place = lax.broadcasted_iota(jnp.int32, logits.shape, 0)
    real = place < CLASSES
    logits = jnp.where(real, logits, -jnp.inf)
    powers = jnp.exp(logits - jnp.max(logits, axis=0, keepdims=True))
    probabilities = powers / jnp.sum(powers, axis=0, keepdims=True)
    onehot = jnp.where(place == label_ref[...], 1.0, 0.0)
    logit_grad = jnp.where(real, probabilities - onehot, 0.0).astype(jnp.bfloat16)
    for c in range(groups):
        weight = gathered_ref[c, 2 * rows : 2 * rows + CLASS_ROWS]
        total = gathered_ref[c, rows : 2 * rows].astype(jnp.float32) + dot_tn(logit_grad, weight)
        active = gathered_ref[c, :rows].astype(jnp.float32) > 0
        grad = jnp.where(active, total, 0.0).astype(jnp.bfloat16)
        size = rows // len(plane_refs)
        for d, plane_ref in enumerate(plane_refs):
            plane_ref[:, c * inner : (c + 1) * inner] = grad[d * size : (d + 1) * size]
    aux_ref[...] = dot_nn(logit_grad, jnp.maximum(own_ref[...], 0)).astype(jnp.bfloat16)


def conv_kernel(*refs):
    planes, (low_ref, high_ref, weight_ref) = refs[:-8], refs[-8:-5]
    far_ref, out_ref, part_ref, acc_ref, pool_ref = refs[-5:]
    far_d, far_h, width, full = far_ref.shape
    depth, height = far_d - 2, far_h - 2
    inner = out_ref.shape[1]
    rows = depth * height * width
    for d, plane_ref in enumerate(planes):
        far_ref[d, 1 : 1 + height] = plane_ref[...].reshape(height, width, full)
    far_ref[:, 0] = low_ref[...]
    far_ref[:, far_h - 1] = high_ref[...]
    total = jnp.zeros((rows, inner), jnp.float32)
    terms = [total] * 3
    for a in STEPS:
        for b in STEPS:
            piece = far_ref[1 - a : 1 - a + depth, 1 - b : 1 - b + height].reshape(rows, full)
            for c in STEPS:
                tap = 9 * (a + 1) + 3 * (b + 1) + c + 1
                terms[c + 1] += dot_nt(piece, weight_ref[:, tap * full : (tap + 1) * full])
    for c in STEPS:
        total += moved(terms[c + 1], c, width)
    out_ref[...] = total.astype(jnp.bfloat16)

    half_d, half_h, half_w = depth // 2, height // 2, width // 2
    nc = part_ref.shape[0]
    block = half_w // nc
    window = part_ref.shape[1] // (half_d * half_h)
    pool_ref[...] = jnp.zeros_like(pool_ref)
    lines = total.reshape(depth, height, width, inner)
    for d in range(half_d):
        for h in range(half_h):
            acc_ref[...] = (
                lines[2 * d, 2 * h]
                + lines[2 * d, 2 * h + 1]
                + lines[2 * d + 1, 2 * h]
                + lines[2 * d + 1, 2 * h + 1]
            )
            pool_ref[d, h, 8 : 8 + half_w] = (
                acc_ref[pl.ds(0, half_w, stride=2)] + acc_ref[pl.ds(1, half_w, stride=2)]
            )
    for c in range(nc):
        start = 7 + c * block
        part_ref[c] = jnp.concatenate(
            [pool_ref[d, h, start : start + window] for d in range(half_d) for h in range(half_h)],
            axis=0,
        ).astype(jnp.bfloat16)


def kernel_grad_kernel(chunk, place_ref, far_ref, input_ref, *refs):
    out_refs, all_ref, turn_ref = refs[:-2], refs[-2], refs[-1]
    far_d, far_h, width, full = far_ref.shape
    depth, height = far_d - 2, far_h - 2
    rows, inner = input_ref.shape
    by_height, by_depth, window, _ = all_ref.shape
    lanes = height * width
    flat = input_ref[...].astype(jnp.float32)
    wide = jnp.concatenate([moved(flat, -c, width).astype(jnp.bfloat16) for c in STEPS], axis=1)
    for d in range(far_d):
        for b in range(3):
            turn_ref[d, b] = far_ref[d, b : b + height].reshape(lanes, full).T
    for a in STEPS:
        for b in STEPS:
            turned = jnp.concatenate([turn_ref[1 - a + d, 1 - b] for d in range(depth)], axis=1)
            terms = dot_nn(turned, wide).astype(jnp.bfloat16)
            for c in range(3):
                first = (9 * (a + 1) + 3 * (b + 1) + c) * full
                for owner in range(by_depth * by_height):
                    start = owner * chunk // 16 * 16
                    low, high = max(start, first), min(start + window, first + full)
                    if low < high:
                        all_ref[owner % by_height, owner // by_height, low - start : high - start] = terms[
                            low - first : high - first, c * inner : (c + 1) * inner
                        ]
    for k, out_ref in enumerate(out_refs):
        out_ref[...] = all_ref[place_ref[0] ^ k]


def bottom_kernel(
    down_ref,
    up_ref,
    before_ref,
    pre_ref,
    after_ref,
    source_ref,
    weight_ref,
    part_ref,
    both_ref,
    shift_ref,
):
    _, far_d, far_w, height, filters = shift_ref.shape
    depth, width = far_d - 2, far_w - 2
    rows = depth * width * height
    channels = source_ref.shape[1]
    groups = both_ref.shape[0]
    thin = channels // groups
    full = down_ref.shape[1]
    inner = full // groups
    back = dot_nt(down_ref[...], up_ref[...])
    own_saved = pre_ref[...].reshape(rows, filters)
    saved = jnp.concatenate([before_ref[...], pre_ref[...], after_ref[...]], axis=1)
    saved = saved.reshape(depth * far_w * height, filters)
    grad = jnp.where(saved.astype(jnp.float32) > 0, back, 0.0)
    shift_ref[:, :1] = jnp.zeros((3, 1) + shift_ref.shape[2:], jnp.bfloat16)
    shift_ref[:, far_d - 1 :] = jnp.zeros((3, 1) + shift_ref.shape[2:], jnp.bfloat16)
    for b in STEPS:
        shift_ref[b + 1, 1 : 1 + depth] = (
            moved(grad, b, height).astype(jnp.bfloat16).reshape(depth, far_w, height, filters)
        )
    own_down = down_ref[...].reshape(depth, far_w, height, full)[:, 1 : 1 + width].reshape(rows, full)
    up_part = dot_tn(jnp.maximum(own_saved, 0), own_down).astype(jnp.bfloat16)
    for cc in range(groups):
        both_ref[cc, TAPS * thin :] = up_part[:, cc * inner : (cc + 1) * inner]
    turned = source_ref[...].T
    total = jnp.zeros((rows, channels), jnp.float32)
    for a in STEPS:
        for b in STEPS:
            tap = 9 * (a + 1) + 3 * (b + 1)
            piece = jnp.concatenate(
                [
                    shift_ref[b + 1, 1 - a : 1 - a + depth, 1 - c : 1 - c + width].reshape(rows, filters)
                    for c in STEPS
                ],
                axis=1,
            )
            weight = jnp.concatenate([weight_ref[tap + c] for c in range(3)], axis=1)
            total += dot_nt(piece, weight)
            terms = dot_nn(turned, piece).astype(jnp.bfloat16)
            for c in range(3):
                for cc in range(groups):
                    both_ref[cc, (tap + c) * thin : (tap + c + 1) * thin] = terms[
                        cc * thin : (cc + 1) * thin, c * filters : (c + 1) * filters
                    ]
    part_ref[...] = total.astype(jnp.bfloat16)


def per_device(
    pre_bottom,
    bottom_input,
    bottom_weight,
    up_weight,
    level_input,
    pre_level,
    level_cotangent,
    labels,
    level_weight,
    aux_weight,
):
    nx, ny, nc = (lax.axis_size(a) for a in ("gx", "gy", "col"))
    at_x, at_y = lax.axis_index("gx"), lax.axis_index("gy")
    depth, height, width, inner = level_input.shape
    full = inner * nc
    rows = depth * height * width
    far_d, far_h = depth + 2, height + 2
    half_d, half_h, half_w = depth // 2, height // 2, width // 2
    block = half_w // nc
    wide = block + 2
    bottom_d, bottom_h, _, filters = pre_bottom.shape
    bf16, f32 = jnp.bfloat16, jnp.float32
    struct = jax.ShapeDtypeStruct

    own_pre = pre_level.reshape(rows, inner)
    payload = jnp.concatenate(
        [
            own_pre,
            level_cotangent.reshape(rows, inner),
            jnp.pad(aux_weight.T, ((0, CLASS_ROWS - CLASSES), (0, 0))),
        ]
    )
    gathered = lax.all_gather(payload, "col")
    lanes = height * width
    *planes, aux_part = local_call(
        class_kernel,
        [struct((lanes, full), bf16)] * depth + [struct((CLASS_ROWS, inner), bf16)],
        [],
        6 * rows * full * CLASS_ROWS,
        2 * gathered.size,
        gathered,
        own_pre,
        labels.reshape(1, rows),
    )

    planes = [neighbour(planes[-1], 1, 0)] + planes + [neighbour(planes[0], -1, 0)]
    low = neighbour(jnp.stack([p[lanes - width :] for p in planes]), 0, 1)
    high = neighbour(jnp.stack([p[:width] for p in planes]), 0, -1)

    window = (wide + 7) // 8 * 8
    cells = half_d * half_h * window
    far, level_input_grad, parts = local_call(
        conv_kernel,
        (
            struct((far_d, far_h, width, full), bf16),
            struct((rows, inner), bf16),
            struct((nc, cells, inner), bf16),
        ),
        [
            pltpu.VMEM((width, inner), f32),
            pltpu.VMEM((half_d, half_h, half_w + 24, inner), f32),
        ],
        2 * rows * full * TAPS * inner,
        2 * level_weight.size,
        *planes,
        low,
        high,
        level_weight,
    )
    level_input_grad = level_input_grad.reshape(level_input.shape)

    relayed = exchange(parts, "col").reshape(nc * cells, inner)

    chunk = TAPS * full // (nx * ny)
    span = chunk + 8 if chunk % 16 else chunk
    level_parts = local_call(
        functools.partial(kernel_grad_kernel, chunk),
        [struct((nx, span, inner), bf16)] * ny,
        [
            pltpu.VMEM((ny, nx, span, inner), bf16),
            pltpu.VMEM((far_d, 3, full, lanes), bf16),
        ],
        2 * rows * full * TAPS * inner,
        2 * nx * ny * span * inner,
        jnp.full((1,), at_y, jnp.int32),
        far,
        level_input.reshape(rows, inner),
    )
    relayed = behind(relayed, level_parts[0])

    turned_pre = pre_bottom.transpose(0, 2, 1, 3)
    edges = behind(turned_pre, parts)
    ups = [(i, i + 1) for i in range(nc - 1)]
    downs = [(j, i) for i, j in ups]
    pre_before = lax.ppermute(edges[:, -1:], "col", ups)
    pre_after = lax.ppermute(edges[:, :1], "col", downs)

    by_depth = spread(jnp.concatenate([relayed, aux_part]), "gx")
    aux_sum = by_depth[:, nc * cells :].astype(f32).sum(axis=0).astype(bf16)
    line = by_depth[:, : nc * cells].reshape(nx, nc, half_d * half_h, window, inner)[:, :, :, :wide]
    split = nx * nc * half_d * half_h * wide
    by_height = spread(jnp.concatenate([line.reshape(split, inner), aux_sum]), "gy")
    aux_weight_grad = by_height[:, split : split + CLASSES].astype(f32).sum(axis=0).T
    down_wide = (
        by_height[:, :split]
        .reshape(ny, nx, nc, half_d, half_h, wide, inner)
        .transpose(1, 3, 5, 0, 4, 2, 6)
        .reshape(bottom_d * wide * bottom_h, full)
    )

    level_part = level_parts[0].astype(f32)
    for k in range(1, ny):
        level_part += swap(level_parts[k], "gy", k).astype(f32)
    level_part = exchange(level_part.astype(bf16), "gx").astype(f32).sum(axis=0)
    if span != chunk:
        odd = lax.rem(at_y + at_x * ny, 2)
        level_part = jnp.where(odd == 1, level_part[span - chunk :], level_part[:chunk])
    level_weight_grad = level_part.T

    bottom_rows = bottom_d * block * bottom_h
    channel_width = bottom_weight.shape[0]
    thin = channel_width // nc
    part, both = local_call(
        bottom_kernel,
        (
            struct((bottom_rows, channel_width), bf16),
            struct((nc, TAPS * thin + filters, inner), bf16),
        ),
        [pltpu.VMEM((3, bottom_d + 2, wide, bottom_h, filters), bf16)],
        4 * bottom_rows * channel_width * TAPS * filters,
        2 * bottom_weight.size,
        down_wide,
        up_weight,
        pre_before,
        turned_pre,
        pre_after,
        bottom_input.transpose(0, 2, 1, 3).reshape(bottom_rows, channel_width),
        bottom_weight.transpose(1, 0, 2),
    )
    share = bottom_d // ny
    bottom_input_grad = (
        exchange(part.reshape(ny, bottom_rows // ny, channel_width), "gy")
        .astype(f32)
        .sum(axis=0)
        .astype(bf16)
        .reshape(share, block, bottom_h, channel_width)
        .transpose(0, 2, 1, 3)
    )
    both, _ = summed_by_pairs(both, "col", bits_of("col")[::-1])
    bottom_weight_grad = both[: TAPS * thin].reshape(TAPS, thin, filters).transpose(1, 0, 2)
    up_weight_grad = both[TAPS * thin :]
    return (
        level_input_grad,
        bottom_input_grad,
        level_weight_grad,
        bottom_weight_grad,
        up_weight_grad,
        aux_weight_grad,
    )


def solution(mesh):
    return jax.shard_map(
        per_device,
        mesh=mesh,
        in_specs=(
            P(None, None, "col", "gy"),
            P(None, None, "col", "gx"),
            P("gx", None, "gy"),
            P("gy", None),
            P("gx", "gy", None, "col"),
            P("gx", "gy", None, "col"),
            P("gx", "gy", None, "col"),
            P("gx", "gy", None),
            P("col", None),
            P("col", None),
        ),
        out_specs=(
            P("gx", "gy", None, "col"),
            P("gy", None, "col", "gx"),
            P("col", ("gx", "gy")),
            P(("gx", "col"), None, "gy"),
            P("gy", "col"),
            P("col", None),
        ),
        check_vma=False,
    )
```

```python
import functools

import jax
import jax.numpy as jnp
from jax import lax
from jax.experimental import pallas as pl
from jax.experimental.pallas import tpu as pltpu
from jax.sharding import PartitionSpec as P

CLASSES = 14
CLASS_ROWS = 16
TAPS = 27
VMEM_LIMIT = 48 * 1024 * 1024
STEPS = (-1, 0, 1)


def exchange(x, axis):
    return lax.all_to_all(x, axis, split_axis=0, concat_axis=0, tiled=False)


def spread(x, axis):
    size = lax.axis_size(axis)
    return exchange(jnp.broadcast_to(x[None], (size,) + x.shape), axis)


def behind(x, *others):
    return lax.optimization_barrier((x,) + others)[0]


def neighbour(x, depth, height):
    nx, ny = lax.axis_size("gx"), lax.axis_size("gy")
    pairs = [
        (i * ny + j, (i + depth) * ny + j + height)
        for i in range(nx)
        for j in range(ny)
        if 0 <= i + depth < nx and 0 <= j + height < ny
    ]
    return lax.ppermute(x, ("gx", "gy"), pairs)


def bits_of(axis):
    return [1 << k for k in reversed(range(lax.axis_size(axis).bit_length() - 1))]


def swap(x, axis, bit):
    return lax.ppermute(x, axis, [(i, i ^ bit) for i in range(lax.axis_size(axis))])


def mine_and_other(x, axis, bit, dim):
    own = lax.axis_index(axis) // bit % 2
    take = functools.partial(lax.dynamic_index_in_dim, x, axis=dim, keepdims=False)
    return take(own), take(1 - own)


def summed_by_pairs(x, axis, bits):
    names = bits_of(axis)
    x = x.reshape((2,) * len(names) + x.shape[1:])
    left = list(names)
    steps = []
    for bit in bits:
        own, other = mine_and_other(x, axis, bit, left.index(bit))
        left.remove(bit)
        x = own.astype(jnp.float32) + swap(other.astype(jnp.bfloat16), axis, bit).astype(jnp.float32)
        steps.append(x)
    return x, steps


def dot_nn(a, b):
    return lax.dot_general(a, b, (((1,), (0,)), ((), ())), preferred_element_type=jnp.float32)


def dot_tn(a, b):
    return lax.dot_general(a, b, (((0,), (0,)), ((), ())), preferred_element_type=jnp.float32)


def dot_nt(a, b):
    return lax.dot_general(a, b, (((1,), (1,)), ((), ())), preferred_element_type=jnp.float32)


def moved(x, step, period):
    if step == 0:
        return x
    rows = x.shape[0]
    place = lax.rem(lax.broadcasted_iota(jnp.int32, x.shape, 0), period)
    edge = 0 if step == 1 else period - 1
    return jnp.where(place == edge, 0.0, pltpu.roll(x, step % rows, 0))


def local_call(body, out_shapes, scratch, flops, moved_bytes, *args, stay=None):
    return pl.pallas_call(
        body,
        out_shape=list(out_shapes),
        in_specs=[
            pl.BlockSpec(
                memory_space=pl.ANY if k == stay else pltpu.SMEM if a.ndim == 1 else pltpu.VMEM
            )
            for k, a in enumerate(args)
        ],
        out_specs=[pl.BlockSpec(memory_space=pltpu.VMEM)] * len(out_shapes),
        scratch_shapes=scratch,
        cost_estimate=pl.CostEstimate(flops=flops, bytes_accessed=moved_bytes, transcendentals=0),
        compiler_params=pltpu.CompilerParams(vmem_limit_bytes=VMEM_LIMIT),
    )(*args)


def class_kernel(gathered_ref, own_ref, label_ref, *out_refs):
    plane_refs, aux_ref = out_refs[:-1], out_refs[-1]
    groups, rows, inner = gathered_ref.shape[0], own_ref.shape[0], own_ref.shape[1]
    logits = jnp.zeros((CLASS_ROWS, rows), jnp.float32)
    for c in range(groups):
        weight = gathered_ref[c, 2 * rows : 2 * rows + CLASS_ROWS]
        logits += dot_nt(weight, jnp.maximum(gathered_ref[c, :rows], 0))
    place = lax.broadcasted_iota(jnp.int32, logits.shape, 0)
    real = place < CLASSES
    logits = jnp.where(real, logits, -jnp.inf)
    powers = jnp.exp(logits - jnp.max(logits, axis=0, keepdims=True))
    probabilities = powers / jnp.sum(powers, axis=0, keepdims=True)
    onehot = jnp.where(place == label_ref[...], 1.0, 0.0)
    logit_grad = jnp.where(real, probabilities - onehot, 0.0).astype(jnp.bfloat16)
    for c in range(groups):
        weight = gathered_ref[c, 2 * rows : 2 * rows + CLASS_ROWS]
        total = gathered_ref[c, rows : 2 * rows].astype(jnp.float32) + dot_tn(logit_grad, weight)
        active = gathered_ref[c, :rows].astype(jnp.float32) > 0
        grad = jnp.where(active, total, 0.0).astype(jnp.bfloat16)
        size = rows // len(plane_refs)
        for d, plane_ref in enumerate(plane_refs):
            plane_ref[:, c * inner : (c + 1) * inner] = grad[d * size : (d + 1) * size]
    aux_ref[...] = dot_nn(logit_grad, jnp.maximum(own_ref[...], 0)).astype(jnp.bfloat16)


def conv_kernel(*refs):
    side_ref, planes, (low_ref, high_ref, input_ref, weight_hbm) = refs[0], refs[1:-12], refs[-12:-8]
    far_ref, out_ref, part_ref, send_ref, acc_ref, pool_ref, weight_ref, sems = refs[-8:]
    far_d, far_h, width, full = far_ref.shape
    depth, height = far_d - 2, far_h - 2
    inner = out_ref.shape[1]
    rows = depth * height * width
    copies = []
    for k in range(9):
        span = pl.ds(3 * k * full, 3 * full)
        copies.append(
            pltpu.make_async_copy(weight_hbm.at[:, span], weight_ref.at[:, span], sems.at[k])
        )
        copies[k].start()
    for d, plane_ref in enumerate(planes):
        far_ref[d, 1 : 1 + height] = plane_ref[...].reshape(height, width, full)
    far_ref[:, 0] = low_ref[...]
    far_ref[:, far_h - 1] = high_ref[...]
    sent = far_d // 2
    send_ref[: sent * far_h * width] = far_ref[pl.ds(sent * side_ref[0], sent)].reshape(-1, full)
    piece_rows = rows * inner // full
    for c in range(full // inner):
        send_ref[sent * far_h * width :, c * inner : (c + 1) * inner] = input_ref[
            c * piece_rows : (c + 1) * piece_rows
        ]
    total = jnp.zeros((rows, inner), jnp.float32)
    terms = [total] * 3
    for a in STEPS:
        for b in STEPS:
            piece = far_ref[1 - a : 1 - a + depth, 1 - b : 1 - b + height].reshape(rows, full)
            copies[3 * (a + 1) + b + 1].wait()
            for c in STEPS:
                tap = 9 * (a + 1) + 3 * (b + 1) + c + 1
                terms[c + 1] += dot_nt(piece, weight_ref[:, tap * full : (tap + 1) * full])
    for c in STEPS:
        total += moved(terms[c + 1], c, width)
    out_ref[...] = total.astype(jnp.bfloat16)

    half_d, half_h, half_w = depth // 2, height // 2, width // 2
    nc = part_ref.shape[0]
    block = half_w // nc
    window = part_ref.shape[1] // (half_d * half_h)
    pool_ref[...] = jnp.zeros_like(pool_ref)
    lines = total.reshape(depth, height, width, inner)
    for d in range(half_d):
        for h in range(half_h):
            acc_ref[...] = (
                lines[2 * d, 2 * h]
                + lines[2 * d, 2 * h + 1]
                + lines[2 * d + 1, 2 * h]
                + lines[2 * d + 1, 2 * h + 1]
            )
            pool_ref[d, h, 8 : 8 + half_w] = (
                acc_ref[pl.ds(0, half_w, stride=2)] + acc_ref[pl.ds(1, half_w, stride=2)]
            )
    for c in range(nc):
        start = 7 + c * block
        part_ref[c] = jnp.concatenate(
            [pool_ref[d, h, start : start + window] for d in range(half_d) for h in range(half_h)],
            axis=0,
        ).astype(jnp.bfloat16)


def kernel_grad_kernel(chunk, place_ref, far_ref, input_ref, got_ref, *refs):
    out_refs, (all_ref, flat_ref, pair_ref, turn_ref, wide_ref) = refs[:-5], refs[-5:]
    far_d, far_h, width, full = far_ref.shape
    depth, height = far_d - 2, far_h - 2
    rows, inner = input_ref.shape
    by_height, by_depth, window, _ = all_ref.shape
    lanes = height * width
    side, at_y = place_ref[0], place_ref[1]
    sent = far_d // 2
    pair_ref[pl.ds(depth * side, far_d)] = far_ref[...]
    pair_ref[pl.ds(far_d * (1 - side), depth)] = got_ref[: sent * far_h * width].reshape(
        sent, far_h, width, full
    )
    piece_rows = rows * inner // full
    other = jnp.concatenate(
        [
            got_ref[sent * far_h * width :, c * inner : (c + 1) * inner]
            for c in range(full // inner)
        ],
        axis=0,
    )
    for c in STEPS:
        wide_ref[c + 1, side] = moved(input_ref[...].astype(jnp.float32), -c, width).astype(jnp.bfloat16)
        wide_ref[c + 1, 1 - side] = moved(other.astype(jnp.float32), -c, width).astype(jnp.bfloat16)
    for d in range(far_d + depth):
        for b in range(3):
            turn_ref[d, b] = pair_ref[d, b : b + height].reshape(lanes, full).T
    half = full // 2
    for step in range(TAPS // 2 + 1):
        tap = TAPS // 2 * side + step
        a, b, c = tap // 9, lax.rem(tap // 3, 3), lax.rem(tap, 3)
        turned = jnp.concatenate([turn_ref[2 - a + d, 2 - b] for d in range(2 * depth)], axis=1)
        terms = dot_nn(turned, wide_ref[c].reshape(2 * rows, inner))
        first = pl.multiple_of(step * full + half - half * side, half)
        flat_ref[pl.ds(first, full)] = terms.astype(jnp.bfloat16)
    for owner in range(by_depth * by_height):
        start = half + owner * chunk // 16 * 16
        all_ref[owner % by_height, owner // by_height] = flat_ref[start : start + window]
    for k, out_ref in enumerate(out_refs):
        out_ref[...] = all_ref[at_y ^ k]


def bottom_kernel(
    down_ref,
    up_ref,
    before_ref,
    pre_ref,
    after_ref,
    source_ref,
    weight_hbm,
    part_ref,
    both_ref,
    shift_ref,
    weight_ref,
    sem,
):
    copy = pltpu.make_async_copy(weight_hbm, weight_ref, sem)
    copy.start()
    _, far_d, far_w, height, filters = shift_ref.shape
    depth, width = far_d - 2, far_w - 2
    rows = depth * width * height
    channels = source_ref.shape[1]
    groups = both_ref.shape[0]
    thin = channels // groups
    full = down_ref.shape[1]
    inner = full // groups
    back = dot_nt(down_ref[...], up_ref[...])
    own_saved = pre_ref[...].reshape(rows, filters)
    saved = jnp.concatenate([before_ref[...], pre_ref[...], after_ref[...]], axis=1)
    saved = saved.reshape(depth * far_w * height, filters)
    grad = jnp.where(saved.astype(jnp.float32) > 0, back, 0.0)
    shift_ref[:, :1] = jnp.zeros((3, 1) + shift_ref.shape[2:], jnp.bfloat16)
    shift_ref[:, far_d - 1 :] = jnp.zeros((3, 1) + shift_ref.shape[2:], jnp.bfloat16)
    for b in STEPS:
        shift_ref[b + 1, 1 : 1 + depth] = (
            moved(grad, b, height).astype(jnp.bfloat16).reshape(depth, far_w, height, filters)
        )
    own_down = down_ref[...].reshape(depth, far_w, height, full)[:, 1 : 1 + width].reshape(rows, full)
    up_part = dot_tn(jnp.maximum(own_saved, 0), own_down).astype(jnp.bfloat16)
    for cc in range(groups):
        both_ref[cc, TAPS * thin :] = up_part[:, cc * inner : (cc + 1) * inner]
    turned = source_ref[...].T
    total = jnp.zeros((rows, channels), jnp.float32)
    copy.wait()
    for a in STEPS:
        for b in STEPS:
            tap = 9 * (a + 1) + 3 * (b + 1)
            piece = jnp.concatenate(
                [
                    shift_ref[b + 1, 1 - a : 1 - a + depth, 1 - c : 1 - c + width].reshape(rows, filters)
                    for c in STEPS
                ],
                axis=1,
            )
            weight = jnp.concatenate([weight_ref[tap + c] for c in range(3)], axis=1)
            total += dot_nt(piece, weight)
            terms = dot_nn(turned, piece).astype(jnp.bfloat16)
            for c in range(3):
                for cc in range(groups):
                    both_ref[cc, (tap + c) * thin : (tap + c + 1) * thin] = terms[
                        cc * thin : (cc + 1) * thin, c * filters : (c + 1) * filters
                    ]
    part_ref[...] = total.astype(jnp.bfloat16)


def per_device(
    pre_bottom,
    bottom_input,
    bottom_weight,
    up_weight,
    level_input,
    pre_level,
    level_cotangent,
    labels,
    level_weight,
    aux_weight,
):
    nx, ny, nc = (lax.axis_size(a) for a in ("gx", "gy", "col"))
    at_x, at_y = lax.axis_index("gx"), lax.axis_index("gy")
    depth, height, width, inner = level_input.shape
    full = inner * nc
    rows = depth * height * width
    far_d, far_h = depth + 2, height + 2
    half_d, half_h, half_w = depth // 2, height // 2, width // 2
    block = half_w // nc
    wide = block + 2
    bottom_d, bottom_h, _, filters = pre_bottom.shape
    bf16, f32 = jnp.bfloat16, jnp.float32
    struct = jax.ShapeDtypeStruct

    own_pre = pre_level.reshape(rows, inner)
    payload = jnp.concatenate(
        [
            own_pre,
            level_cotangent.reshape(rows, inner),
            jnp.pad(aux_weight.T, ((0, CLASS_ROWS - CLASSES), (0, 0))),
        ]
    )
    gathered = lax.all_gather(payload, "col")
    lanes = height * width
    *planes, aux_part = local_call(
        class_kernel,
        [struct((lanes, full), bf16)] * depth + [struct((CLASS_ROWS, inner), bf16)],
        [],
        6 * rows * full * CLASS_ROWS,
        2 * gathered.size,
        gathered,
        own_pre,
        labels.reshape(1, rows),
    )

    planes = [neighbour(planes[-1], 1, 0)] + planes + [neighbour(planes[0], -1, 0)]
    low = neighbour(jnp.stack([p[lanes - width :] for p in planes]), 0, 1)
    high = neighbour(jnp.stack([p[:width] for p in planes]), 0, -1)

    window = (wide + 7) // 8 * 8
    cells = half_d * half_h * window
    side = lax.rem(at_x, 2).astype(jnp.int32)
    flat_input = level_input.reshape(rows, inner)
    far, level_input_grad, parts, send = local_call(
        conv_kernel,
        (
            struct((far_d, far_h, width, full), bf16),
            struct((rows, inner), bf16),
            struct((nc, cells, inner), bf16),
            struct((far_d // 2 * far_h * width + rows * inner // full, full), bf16),
        ),
        [
            pltpu.VMEM((width, inner), f32),
            pltpu.VMEM((half_d, half_h, half_w + 24, inner), f32),
            pltpu.VMEM(level_weight.shape, bf16),
            pltpu.SemaphoreType.DMA((9,)),
        ],
        2 * rows * full * TAPS * inner,
        2 * level_weight.size,
        side.reshape(1),
        *planes,
        low,
        high,
        flat_input,
        level_weight,
        stay=len(planes) + 4,
    )
    got = swap(send, "gx", 1)
    level_input_grad = level_input_grad.reshape(level_input.shape)

    relayed = exchange(parts, "col").reshape(nc * cells, inner)

    chunk = TAPS * full // (nx * ny)
    span = chunk + 8 if chunk % 16 else chunk
    level_parts = local_call(
        functools.partial(kernel_grad_kernel, chunk),
        [struct((nx // 2, span, inner), bf16)] * ny,
        [
            pltpu.VMEM((ny, nx // 2, span, inner), bf16),
            pltpu.VMEM(((TAPS + 2) * full // 2, inner), bf16),
            pltpu.VMEM((far_d + depth, far_h, width, full), bf16),
            pltpu.VMEM((far_d + depth, 3, full, lanes), bf16),
            pltpu.VMEM((3, 2, rows, inner), bf16),
        ],
        2 * rows * full * TAPS * inner,
        2 * nx * ny * span * inner,
        jnp.stack([side, at_y.astype(jnp.int32)]),
        far,
        flat_input,
        got,
    )
    terms = [level_parts[0]] + [swap(level_parts[k], "gy", k) for k in range(1, ny)]
    relayed = behind(relayed, level_parts[0])

    turned_pre = pre_bottom.transpose(0, 2, 1, 3)
    edges = behind(turned_pre, parts)
    ups = [(i, i + 1) for i in range(nc - 1)]
    downs = [(j, i) for i, j in ups]
    pre_before = lax.ppermute(edges[:, -1:], "col", ups)
    pre_after = lax.ppermute(edges[:, :1], "col", downs)

    by_depth = spread(jnp.concatenate([relayed, aux_part]), "gx")
    aux_sum = by_depth[:, nc * cells :].astype(f32).sum(axis=0).astype(bf16)
    by_depth = behind(by_depth, *terms[1 : ny // 2])
    line = by_depth[:, : nc * cells].reshape(nx, nc, half_d * half_h, window, inner)[:, :, :, :wide]
    split = nx * nc * half_d * half_h * wide
    by_height = spread(jnp.concatenate([line.reshape(split, inner), aux_sum]), "gy")
    aux_weight_grad = by_height[:, split : split + CLASSES].astype(f32).sum(axis=0).T
    down_wide = (
        by_height[:, :split]
        .reshape(ny, nx, nc, half_d, half_h, wide, inner)
        .transpose(1, 3, 5, 0, 4, 2, 6)
        .reshape(bottom_d * wide * bottom_h, full)
    )

    level_part = sum(t.astype(f32) for t in terms).astype(bf16)
    down_wide = behind(down_wide, level_part)
    pairs = nx // 2
    level_sum = jnp.zeros((span, inner), f32)
    for step in range(pairs):
        chosen = lax.dynamic_index_in_dim(
            level_part, lax.rem(at_x // 2 + step, pairs), 0, keepdims=False
        )
        level_sum += lax.ppermute(
            chosen, "gx", [(i, i % 2 * pairs + (i // 2 + step) % pairs) for i in range(nx)]
        ).astype(f32)
    level_part = level_sum
    if span != chunk:
        odd = lax.rem(at_y + at_x * ny, 2)
        level_part = jnp.where(odd == 1, level_part[span - chunk :], level_part[:chunk])
    level_weight_grad = level_part.T

    bottom_rows = bottom_d * block * bottom_h
    channel_width = bottom_weight.shape[0]
    thin = channel_width // nc
    part, both = local_call(
        bottom_kernel,
        (
            struct((bottom_rows, channel_width), bf16),
            struct((nc, TAPS * thin + filters, inner), bf16),
        ),
        [
            pltpu.VMEM((3, bottom_d + 2, wide, bottom_h, filters), bf16),
            pltpu.VMEM((TAPS, channel_width, filters), bf16),
            pltpu.SemaphoreType.DMA(()),
        ],
        4 * bottom_rows * channel_width * TAPS * filters,
        2 * bottom_weight.size,
        down_wide,
        up_weight,
        pre_before,
        turned_pre,
        pre_after,
        bottom_input.transpose(0, 2, 1, 3).reshape(bottom_rows, channel_width),
        bottom_weight.transpose(1, 0, 2),
        stay=6,
    )
    share = bottom_d // ny
    bottom_input_grad = (
        exchange(part.reshape(ny, bottom_rows // ny, channel_width), "gy")
        .astype(f32)
        .sum(axis=0)
        .astype(bf16)
        .reshape(share, block, bottom_h, channel_width)
        .transpose(0, 2, 1, 3)
    )
    both, _ = summed_by_pairs(both, "col", bits_of("col")[::-1])
    bottom_weight_grad = both[: TAPS * thin].reshape(TAPS, thin, filters).transpose(1, 0, 2)
    up_weight_grad = both[TAPS * thin :]
    return (
        level_input_grad,
        bottom_input_grad,
        level_weight_grad,
        bottom_weight_grad,
        up_weight_grad,
        aux_weight_grad,
    )


def solution(mesh):
    return jax.shard_map(
        per_device,
        mesh=mesh,
        in_specs=(
            P(None, None, "col", "gy"),
            P(None, None, "col", "gx"),
            P("gx", None, "gy"),
            P("gy", None),
            P("gx", "gy", None, "col"),
            P("gx", "gy", None, "col"),
            P("gx", "gy", None, "col"),
            P("gx", "gy", None),
            P("col", None),
            P("col", None),
        ),
        out_specs=(
            P("gx", "gy", None, "col"),
            P("gy", None, "col", "gx"),
            P("col", ("gx", "gy")),
            P(("gx", "col"), None, "gy"),
            P("gy", "col"),
            P("col", None),
        ),
        check_vma=False,
    )
```

```python
import functools

import jax
import jax.numpy as jnp
from jax import lax
from jax.experimental import pallas as pl
from jax.experimental.pallas import tpu as pltpu
from jax.sharding import PartitionSpec as P

CLASSES = 14
CLASS_ROWS = 16
TAPS = 27
VMEM_LIMIT = 48 * 1024 * 1024
VMEM_MORE = 56 * 1024 * 1024
STEPS = (-1, 0, 1)


def exchange(x, axis):
    return lax.all_to_all(x, axis, split_axis=0, concat_axis=0, tiled=False)


def spread(x, axis):
    size = lax.axis_size(axis)
    return exchange(jnp.broadcast_to(x[None], (size,) + x.shape), axis)


def behind(x, *others):
    return lax.optimization_barrier((x,) + others)[0]


def neighbour(x, depth, height):
    nx, ny = lax.axis_size("gx"), lax.axis_size("gy")
    pairs = [
        (i * ny + j, (i + depth) * ny + j + height)
        for i in range(nx)
        for j in range(ny)
        if 0 <= i + depth < nx and 0 <= j + height < ny
    ]
    return lax.ppermute(x, ("gx", "gy"), pairs)


def bits_of(axis):
    return [1 << k for k in reversed(range(lax.axis_size(axis).bit_length() - 1))]


def swap(x, axis, bit):
    return lax.ppermute(x, axis, [(i, i ^ bit) for i in range(lax.axis_size(axis))])


def mine_and_other(x, axis, bit, dim):
    own = lax.axis_index(axis) // bit % 2
    take = functools.partial(lax.dynamic_index_in_dim, x, axis=dim, keepdims=False)
    return take(own), take(1 - own)


def summed_by_pairs(x, axis, bits, first):
    names = bits_of(axis)
    x = x.reshape((2,) * len(names) + x.shape[1:])
    left = list(names)
    steps = []
    for bit in bits:
        if bit == bits[-1]:
            x = behind(x, first)
        own, other = mine_and_other(x, axis, bit, left.index(bit))
        left.remove(bit)
        x = own.astype(jnp.float32) + swap(other.astype(jnp.bfloat16), axis, bit).astype(jnp.float32)
        steps.append(x)
    return x, steps


def dot_nn(a, b):
    return lax.dot_general(a, b, (((1,), (0,)), ((), ())), preferred_element_type=jnp.float32)


def dot_tn(a, b):
    return lax.dot_general(a, b, (((0,), (0,)), ((), ())), preferred_element_type=jnp.float32)


def dot_nt(a, b):
    return lax.dot_general(a, b, (((1,), (1,)), ((), ())), preferred_element_type=jnp.float32)


def moved(x, step, period):
    if step == 0:
        return x
    rows = x.shape[0]
    place = lax.rem(lax.broadcasted_iota(jnp.int32, x.shape, 0), period)
    edge = 0 if step == 1 else period - 1
    return jnp.where(place == edge, 0.0, pltpu.roll(x, step % rows, 0))


def local_call(body, out_shapes, scratch, flops, moved_bytes, *args, stay=None):
    return pl.pallas_call(
        body,
        out_shape=list(out_shapes),
        in_specs=[
            pl.BlockSpec(
                memory_space=pltpu.HBM if k == stay else pltpu.SMEM if a.ndim == 1 else pltpu.VMEM
            )
            for k, a in enumerate(args)
        ],
        out_specs=[pl.BlockSpec(memory_space=pltpu.VMEM)] * len(out_shapes),
        scratch_shapes=scratch,
        cost_estimate=pl.CostEstimate(flops=flops, bytes_accessed=moved_bytes, transcendentals=0),
        compiler_params=pltpu.CompilerParams(vmem_limit_bytes=VMEM_LIMIT if stay is None else VMEM_MORE),
    )(*args)


def class_kernel(gathered_ref, own_ref, label_ref, *out_refs):
    plane_refs, aux_ref = out_refs[:-1], out_refs[-1]
    groups, rows, inner = gathered_ref.shape[0], own_ref.shape[0], own_ref.shape[1]
    logits = jnp.zeros((CLASS_ROWS, rows), jnp.float32)
    for c in range(groups):
        weight = gathered_ref[c, 2 * rows : 2 * rows + CLASS_ROWS]
        logits += dot_nt(weight, jnp.maximum(gathered_ref[c, :rows], 0))
    place = lax.broadcasted_iota(jnp.int32, logits.shape, 0)
    real = place < CLASSES
    logits = jnp.where(real, logits, -jnp.inf)
    powers = jnp.exp(logits - jnp.max(logits, axis=0, keepdims=True))
    probabilities = powers / jnp.sum(powers, axis=0, keepdims=True)
    onehot = jnp.where(place == label_ref[...], 1.0, 0.0)
    logit_grad = jnp.where(real, probabilities - onehot, 0.0).astype(jnp.bfloat16)
    for c in range(groups):
        weight = gathered_ref[c, 2 * rows : 2 * rows + CLASS_ROWS]
        total = gathered_ref[c, rows : 2 * rows].astype(jnp.float32) + dot_tn(logit_grad, weight)
        active = gathered_ref[c, :rows].astype(jnp.float32) > 0
        grad = jnp.where(active, total, 0.0).astype(jnp.bfloat16)
        size = rows // len(plane_refs)
        for d, plane_ref in enumerate(plane_refs):
            plane_ref[:, c * inner : (c + 1) * inner] = grad[d * size : (d + 1) * size]
    aux_ref[...] = dot_nn(logit_grad, jnp.maximum(own_ref[...], 0)).astype(jnp.bfloat16)


def conv_kernel(*refs):
    side_ref, planes, (low_ref, high_ref, input_ref, weight_hbm) = refs[0], refs[1:-12], refs[-12:-8]
    far_ref, out_ref, part_ref, send_ref, acc_ref, pool_ref, weight_ref, sems = refs[-8:]
    far_d, far_h, width, full = far_ref.shape
    depth, height = far_d - 2, far_h - 2
    inner = out_ref.shape[1]
    rows = depth * height * width
    copies = []
    for k in range(9):
        span = pl.ds(3 * k * full, 3 * full)
        copies.append(
            pltpu.make_async_copy(weight_hbm.at[:, span], weight_ref.at[:, span], sems.at[k])
        )
        copies[k].start()
    for d, plane_ref in enumerate(planes):
        far_ref[d, 1 : 1 + height] = plane_ref[...].reshape(height, width, full)
    far_ref[:, 0] = low_ref[...]
    far_ref[:, far_h - 1] = high_ref[...]
    sent = far_d // 2
    send_ref[: sent * far_h * width] = far_ref[pl.ds(sent * side_ref[0], sent)].reshape(-1, full)
    piece_rows = rows * inner // full
    for c in range(full // inner):
        send_ref[sent * far_h * width :, c * inner : (c + 1) * inner] = input_ref[
            c * piece_rows : (c + 1) * piece_rows
        ]
    total = jnp.zeros((rows, inner), jnp.float32)
    terms = [total] * 3
    for a in STEPS:
        for b in STEPS:
            piece = far_ref[1 - a : 1 - a + depth, 1 - b : 1 - b + height].reshape(rows, full)
            copies[3 * (a + 1) + b + 1].wait()
            for c in STEPS:
                tap = 9 * (a + 1) + 3 * (b + 1) + c + 1
                terms[c + 1] += dot_nt(piece, weight_ref[:, tap * full : (tap + 1) * full])
    for c in STEPS:
        total += moved(terms[c + 1], c, width)
    out_ref[...] = total.astype(jnp.bfloat16)

    half_d, half_h, half_w = depth // 2, height // 2, width // 2
    nc = part_ref.shape[0]
    block = half_w // nc
    window = part_ref.shape[1] // (half_d * half_h)
    pool_ref[...] = jnp.zeros_like(pool_ref)
    lines = total.reshape(depth, height, width, inner)
    for d in range(half_d):
        for h in range(half_h):
            acc_ref[...] = (
                lines[2 * d, 2 * h]
                + lines[2 * d, 2 * h + 1]
                + lines[2 * d + 1, 2 * h]
                + lines[2 * d + 1, 2 * h + 1]
            )
            pool_ref[d, h, 8 : 8 + half_w] = (
                acc_ref[pl.ds(0, half_w, stride=2)] + acc_ref[pl.ds(1, half_w, stride=2)]
            )
    for c in range(nc):
        start = 7 + c * block
        part_ref[c] = jnp.concatenate(
            [pool_ref[d, h, start : start + window] for d in range(half_d) for h in range(half_h)],
            axis=0,
        ).astype(jnp.bfloat16)


def kernel_grad_kernel(chunk, place_ref, far_ref, input_ref, got_ref, *refs):
    out_refs, (all_ref, flat_ref, pair_ref, turn_ref, wide_ref) = refs[:-5], refs[-5:]
    far_d, far_h, width, full = far_ref.shape
    depth, height = far_d - 2, far_h - 2
    rows, inner = input_ref.shape
    by_height, by_depth, window, _ = all_ref.shape
    lanes = height * width
    side, at_y = place_ref[0], place_ref[1]
    sent = far_d // 2
    pair_ref[pl.ds(depth * side, far_d)] = far_ref[...]
    pair_ref[pl.ds(far_d * (1 - side), depth)] = got_ref[: sent * far_h * width].reshape(
        sent, far_h, width, full
    )
    piece_rows = rows * inner // full
    other = jnp.concatenate(
        [
            got_ref[sent * far_h * width :, c * inner : (c + 1) * inner]
            for c in range(full // inner)
        ],
        axis=0,
    )
    for c in STEPS:
        wide_ref[c + 1, side] = moved(input_ref[...].astype(jnp.float32), -c, width).astype(jnp.bfloat16)
        wide_ref[c + 1, 1 - side] = moved(other.astype(jnp.float32), -c, width).astype(jnp.bfloat16)
    for d in range(far_d + depth):
        for b in range(3):
            turn_ref[d, b] = pair_ref[d, b : b + height].reshape(lanes, full).T
    half = full // 2
    for step in range(TAPS // 2 + 1):
        tap = TAPS // 2 * side + step
        a, b, c = tap // 9, lax.rem(tap // 3, 3), lax.rem(tap, 3)
        turned = jnp.concatenate([turn_ref[2 - a + d, 2 - b] for d in range(2 * depth)], axis=1)
        terms = dot_nn(turned, wide_ref[c].reshape(2 * rows, inner))
        first = pl.multiple_of(step * full + half - half * side, half)
        flat_ref[pl.ds(first, full)] = terms.astype(jnp.bfloat16)
    for owner in range(by_depth * by_height):
        start = half + owner * chunk // 16 * 16
        all_ref[owner % by_height, owner // by_height] = flat_ref[start : start + window]
    for k, out_ref in enumerate(out_refs):
        out_ref[...] = all_ref[at_y ^ k]


def bottom_kernel(
    down_ref,
    up_ref,
    before_ref,
    pre_ref,
    after_ref,
    source_ref,
    weight_hbm,
    part_ref,
    both_ref,
    shift_ref,
    weight_ref,
    sem,
):
    copy = pltpu.make_async_copy(weight_hbm, weight_ref, sem)
    copy.start()
    _, far_d, far_w, height, filters = shift_ref.shape
    depth, width = far_d - 2, far_w - 2
    rows = depth * width * height
    channels = source_ref.shape[1]
    groups = both_ref.shape[0]
    thin = channels // groups
    full = down_ref.shape[1]
    inner = full // groups
    back = dot_nt(down_ref[...], up_ref[...])
    own_saved = pre_ref[...].reshape(rows, filters)
    saved = jnp.concatenate([before_ref[...], pre_ref[...], after_ref[...]], axis=1)
    saved = saved.reshape(depth * far_w * height, filters)
    grad = jnp.where(saved.astype(jnp.float32) > 0, back, 0.0)
    shift_ref[:, :1] = jnp.zeros((3, 1) + shift_ref.shape[2:], jnp.bfloat16)
    shift_ref[:, far_d - 1 :] = jnp.zeros((3, 1) + shift_ref.shape[2:], jnp.bfloat16)
    for b in STEPS:
        shift_ref[b + 1, 1 : 1 + depth] = (
            moved(grad, b, height).astype(jnp.bfloat16).reshape(depth, far_w, height, filters)
        )
    own_down = down_ref[...].reshape(depth, far_w, height, full)[:, 1 : 1 + width].reshape(rows, full)
    up_part = dot_tn(jnp.maximum(own_saved, 0), own_down).astype(jnp.bfloat16)
    for cc in range(groups):
        both_ref[cc, TAPS * thin :] = up_part[:, cc * inner : (cc + 1) * inner]
    turned = source_ref[...].T
    total = jnp.zeros((rows, channels), jnp.float32)
    copy.wait()
    for a in STEPS:
        for b in STEPS:
            tap = 9 * (a + 1) + 3 * (b + 1)
            piece = jnp.concatenate(
                [
                    shift_ref[b + 1, 1 - a : 1 - a + depth, 1 - c : 1 - c + width].reshape(rows, filters)
                    for c in STEPS
                ],
                axis=1,
            )
            weight = jnp.concatenate([weight_ref[tap + c] for c in range(3)], axis=1)
            total += dot_nt(piece, weight)
            terms = dot_nn(turned, piece).astype(jnp.bfloat16)
            for c in range(3):
                for cc in range(groups):
                    both_ref[cc, (tap + c) * thin : (tap + c + 1) * thin] = terms[
                        cc * thin : (cc + 1) * thin, c * filters : (c + 1) * filters
                    ]
    part_ref[...] = total.astype(jnp.bfloat16)


def per_device(
    pre_bottom,
    bottom_input,
    bottom_weight,
    up_weight,
    level_input,
    pre_level,
    level_cotangent,
    labels,
    level_weight,
    aux_weight,
):
    nx, ny, nc = (lax.axis_size(a) for a in ("gx", "gy", "col"))
    at_x, at_y = lax.axis_index("gx"), lax.axis_index("gy")
    depth, height, width, inner = level_input.shape
    full = inner * nc
    rows = depth * height * width
    far_d, far_h = depth + 2, height + 2
    half_d, half_h, half_w = depth // 2, height // 2, width // 2
    block = half_w // nc
    wide = block + 2
    bottom_d, bottom_h, _, filters = pre_bottom.shape
    bf16, f32 = jnp.bfloat16, jnp.float32
    struct = jax.ShapeDtypeStruct

    own_pre = pre_level.reshape(rows, inner)
    payload = jnp.concatenate(
        [
            own_pre,
            level_cotangent.reshape(rows, inner),
            jnp.pad(aux_weight.T, ((0, CLASS_ROWS - CLASSES), (0, 0))),
        ]
    )
    gathered = lax.all_gather(payload, "col")
    lanes = height * width
    *planes, aux_part = local_call(
        class_kernel,
        [struct((lanes, full), bf16)] * depth + [struct((CLASS_ROWS, inner), bf16)],
        [],
        6 * rows * full * CLASS_ROWS,
        2 * gathered.size,
        gathered,
        own_pre,
        labels.reshape(1, rows),
    )

    planes = [neighbour(planes[-1], 1, 0)] + planes + [neighbour(planes[0], -1, 0)]
    low = neighbour(jnp.stack([p[lanes - width :] for p in planes]), 0, 1)
    high = neighbour(jnp.stack([p[:width] for p in planes]), 0, -1)

    window = (wide + 7) // 8 * 8
    cells = half_d * half_h * window
    side = lax.rem(at_x, 2).astype(jnp.int32)
    flat_input = level_input.reshape(rows, inner)
    far, level_input_grad, parts, send = local_call(
        conv_kernel,
        (
            struct((far_d, far_h, width, full), bf16),
            struct((rows, inner), bf16),
            struct((nc, cells, inner), bf16),
            struct((far_d // 2 * far_h * width + rows * inner // full, full), bf16),
        ),
        [
            pltpu.VMEM((width, inner), f32),
            pltpu.VMEM((half_d, half_h, half_w + 24, inner), f32),
            pltpu.VMEM(level_weight.shape, bf16),
            pltpu.SemaphoreType.DMA((9,)),
        ],
        2 * rows * full * TAPS * inner,
        2 * level_weight.size,
        side.reshape(1),
        *planes,
        low,
        high,
        flat_input,
        level_weight,
        stay=len(planes) + 4,
    )
    got = swap(send, "gx", 1)
    level_input_grad = level_input_grad.reshape(level_input.shape)

    relayed = exchange(parts, "col").reshape(nc * cells, inner)

    chunk = TAPS * full // (nx * ny)
    span = chunk + 8 if chunk % 16 else chunk
    level_parts = local_call(
        functools.partial(kernel_grad_kernel, chunk),
        [struct((nx // 2, span, inner), bf16)] * ny,
        [
            pltpu.VMEM((ny, nx // 2, span, inner), bf16),
            pltpu.VMEM(((TAPS + 2) * full // 2, inner), bf16),
            pltpu.VMEM((far_d + depth, far_h, width, full), bf16),
            pltpu.VMEM((far_d + depth, 3, full, lanes), bf16),
            pltpu.VMEM((3, 2, rows, inner), bf16),
        ],
        2 * rows * full * TAPS * inner,
        2 * nx * ny * span * inner,
        jnp.stack([side, at_y.astype(jnp.int32)]),
        far,
        flat_input,
        got,
    )
    terms = [level_parts[0]] + [swap(level_parts[k], "gy", k) for k in range(1, ny)]
    relayed = behind(relayed, level_parts[0])

    turned_pre = pre_bottom.transpose(0, 2, 1, 3)
    edges = behind(turned_pre, parts)
    ups = [(i, i + 1) for i in range(nc - 1)]
    downs = [(j, i) for i, j in ups]
    pre_before = lax.ppermute(edges[:, -1:], "col", ups)
    pre_after = lax.ppermute(edges[:, :1], "col", downs)

    by_depth = spread(jnp.concatenate([relayed, aux_part]), "gx")
    aux_sum = by_depth[:, nc * cells :].astype(f32).sum(axis=0).astype(bf16)
    by_depth = behind(by_depth, *terms[1 : ny // 2])
    line = by_depth[:, : nc * cells].reshape(nx, nc, half_d * half_h, window, inner)[:, :, :, :wide]
    split = nx * nc * half_d * half_h * wide
    by_height = spread(jnp.concatenate([line.reshape(split, inner), aux_sum]), "gy")
    aux_weight_grad = by_height[:, split : split + CLASSES].astype(f32).sum(axis=0).T
    down_wide = (
        by_height[:, :split]
        .reshape(ny, nx, nc, half_d, half_h, wide, inner)
        .transpose(1, 3, 5, 0, 4, 2, 6)
        .reshape(bottom_d * wide * bottom_h, full)
    )

    level_part = sum(t.astype(f32) for t in terms).astype(bf16)
    down_wide = behind(down_wide, terms[ny // 2])

    bottom_rows = bottom_d * block * bottom_h
    channel_width = bottom_weight.shape[0]
    thin = channel_width // nc
    part, both = local_call(
        bottom_kernel,
        (
            struct((bottom_rows, channel_width), bf16),
            struct((nc, TAPS * thin + filters, inner), bf16),
        ),
        [
            pltpu.VMEM((3, bottom_d + 2, wide, bottom_h, filters), bf16),
            pltpu.VMEM((TAPS, channel_width, filters), bf16),
            pltpu.SemaphoreType.DMA(()),
        ],
        4 * bottom_rows * channel_width * TAPS * filters,
        2 * bottom_weight.size,
        down_wide,
        up_weight,
        pre_before,
        turned_pre,
        pre_after,
        bottom_input.transpose(0, 2, 1, 3).reshape(bottom_rows, channel_width),
        bottom_weight.transpose(1, 0, 2),
        stay=6,
    )
    part = exchange(part.reshape(ny, bottom_rows // ny, channel_width), "gy")
    pairs = nx // 2
    level_sum = jnp.zeros((span, inner), f32)
    for step in range(pairs):
        if step == pairs // 2:
            level_part = behind(level_part, part)
        chosen = lax.dynamic_index_in_dim(
            level_part, lax.rem(at_x // 2 + step, pairs), 0, keepdims=False
        )
        level_sum += lax.ppermute(
            chosen, "gx", [(i, i % 2 * pairs + (i // 2 + step) % pairs) for i in range(nx)]
        ).astype(f32)
    level_part = level_sum
    if span != chunk:
        odd = lax.rem(at_y + at_x * ny, 2)
        level_part = jnp.where(odd == 1, level_part[span - chunk :], level_part[:chunk])
    level_weight_grad = level_part.T
    share = bottom_d // ny
    bottom_input_grad = (
        part.astype(f32)
        .sum(axis=0)
        .astype(bf16)
        .reshape(share, block, bottom_h, channel_width)
        .transpose(0, 2, 1, 3)
    )
    both, _ = summed_by_pairs(both, "col", bits_of("col")[::-1], part)
    bottom_weight_grad = both[: TAPS * thin].reshape(TAPS, thin, filters).transpose(1, 0, 2)
    up_weight_grad = both[TAPS * thin :]
    return (
        level_input_grad,
        bottom_input_grad,
        level_weight_grad,
        bottom_weight_grad,
        up_weight_grad,
        aux_weight_grad,
    )


def solution(mesh):
    return jax.shard_map(
        per_device,
        mesh=mesh,
        in_specs=(
            P(None, None, "col", "gy"),
            P(None, None, "col", "gx"),
            P("gx", None, "gy"),
            P("gy", None),
            P("gx", "gy", None, "col"),
            P("gx", "gy", None, "col"),
            P("gx", "gy", None, "col"),
            P("gx", "gy", None),
            P("col", None),
            P("col", None),
        ),
        out_specs=(
            P("gx", "gy", None, "col"),
            P("gy", None, "col", "gx"),
            P("col", ("gx", "gy")),
            P(("gx", "col"), None, "gy"),
            P("gy", "col"),
            P("col", None),
        ),
        check_vma=False,
    )
```

```python
import functools

import jax
import jax.numpy as jnp
from jax import lax
from jax.experimental import pallas as pl
from jax.experimental.pallas import tpu as pltpu
from jax.sharding import PartitionSpec as P

CLASSES = 14
CLASS_ROWS = 16
TAPS = 27
VMEM_LIMIT = 48 * 1024 * 1024
VMEM_MORE = 60 * 1024 * 1024
STEPS = (-1, 0, 1)


def exchange(x, axis):
    return lax.all_to_all(x, axis, split_axis=0, concat_axis=0, tiled=False)


def spread(x, axis):
    size = lax.axis_size(axis)
    return exchange(jnp.broadcast_to(x[None], (size,) + x.shape), axis)


def behind(x, *others):
    return lax.optimization_barrier((x,) + others)[0]


def bits_of(axis):
    return [1 << k for k in reversed(range(lax.axis_size(axis).bit_length() - 1))]


def swap(x, axis, bit):
    return lax.ppermute(x, axis, [(i, i ^ bit) for i in range(lax.axis_size(axis))])


def swap_odd(x, axis):
    last = lax.axis_size(axis) - 1
    return lax.ppermute(
        x, axis, [(i, i + 1 if i % 2 else i - 1) for i in range(1, last)]
    )


def mine_and_other(x, axis, bit, dim):
    own = lax.axis_index(axis) // bit % 2
    take = functools.partial(lax.dynamic_index_in_dim, x, axis=dim, keepdims=False)
    return take(own), take(1 - own)


def summed_by_pairs(x, axis, bits, first):
    names = bits_of(axis)
    x = x.reshape((2,) * len(names) + x.shape[1:])
    left = list(names)
    steps = []
    for bit in bits:
        if bit == bits[-1]:
            x = behind(x, first)
        own, other = mine_and_other(x, axis, bit, left.index(bit))
        left.remove(bit)
        x = own.astype(jnp.float32) + swap(other.astype(jnp.bfloat16), axis, bit).astype(jnp.float32)
        steps.append(x)
    return x, steps


def dot_nn(a, b):
    return lax.dot_general(a, b, (((1,), (0,)), ((), ())), preferred_element_type=jnp.float32)


def dot_tn(a, b):
    return lax.dot_general(a, b, (((0,), (0,)), ((), ())), preferred_element_type=jnp.float32)


def dot_nt(a, b):
    return lax.dot_general(a, b, (((1,), (1,)), ((), ())), preferred_element_type=jnp.float32)


def moved(x, step, period):
    if step == 0:
        return x
    rows = x.shape[0]
    place = lax.rem(lax.broadcasted_iota(jnp.int32, x.shape, 0), period)
    edge = 0 if step == 1 else period - 1
    return jnp.where(place == edge, 0.0, pltpu.roll(x, step % rows, 0))


def local_call(body, out_shapes, scratch, flops, moved_bytes, *args, stay=None):
    return pl.pallas_call(
        body,
        out_shape=list(out_shapes),
        in_specs=[
            pl.BlockSpec(
                memory_space=pltpu.HBM if k == stay else pltpu.SMEM if a.ndim == 1 else pltpu.VMEM
            )
            for k, a in enumerate(args)
        ],
        out_specs=[pl.BlockSpec(memory_space=pltpu.VMEM)] * len(out_shapes),
        scratch_shapes=scratch,
        cost_estimate=pl.CostEstimate(flops=flops, bytes_accessed=moved_bytes, transcendentals=0),
        compiler_params=pltpu.CompilerParams(vmem_limit_bytes=VMEM_LIMIT if stay is None else VMEM_MORE),
    )(*args)


def class_kernel(
    side_ref, gathered_ref, own_ref, label_ref, later_ref, grad_ref, even_ref, odd_ref, aux_ref
):
    del later_ref
    groups, rows, inner = gathered_ref.shape[0], own_ref.shape[0], own_ref.shape[1]
    logits = jnp.zeros((CLASS_ROWS, rows), jnp.float32)
    for c in range(groups):
        weight = gathered_ref[c, 2 * rows : 2 * rows + CLASS_ROWS]
        logits += dot_nt(weight, jnp.maximum(gathered_ref[c, :rows], 0))
    place = lax.broadcasted_iota(jnp.int32, logits.shape, 0)
    real = place < CLASSES
    logits = jnp.where(real, logits, -jnp.inf)
    powers = jnp.exp(logits - jnp.max(logits, axis=0, keepdims=True))
    probabilities = powers / jnp.sum(powers, axis=0, keepdims=True)
    onehot = jnp.where(place == label_ref[...], 1.0, 0.0)
    logit_grad = jnp.where(real, probabilities - onehot, 0.0).astype(jnp.bfloat16)
    for c in range(groups):
        weight = gathered_ref[c, 2 * rows : 2 * rows + CLASS_ROWS]
        total = gathered_ref[c, rows : 2 * rows].astype(jnp.float32) + dot_tn(logit_grad, weight)
        active = gathered_ref[c, :rows].astype(jnp.float32) > 0
        grad_ref[:, c * inner : (c + 1) * inner] = jnp.where(active, total, 0.0).astype(jnp.bfloat16)
    size = even_ref.shape[0]
    first = pl.multiple_of((rows - size) * side_ref[0], size)
    even_ref[...] = grad_ref[pl.ds(rows - size - first, size)]
    odd_ref[...] = grad_ref[pl.ds(first, size)]
    aux_ref[...] = dot_nn(logit_grad, jnp.maximum(own_ref[...], 0)).astype(jnp.bfloat16)


def conv_kernel(
    side_ref,
    grad_ref,
    even_x_ref,
    odd_x_ref,
    even_y_ref,
    odd_y_ref,
    input_ref,
    edge_ref,
    weight_ref,
    far_ref,
    out_ref,
    part_ref,
    send_ref,
    acc_ref,
    pool_ref,
):
    far_d, far_h, width, full = far_ref.shape
    depth, height = far_d - 2, far_h - 2
    inner = out_ref.shape[1]
    rows = depth * height * width
    side_x, side_y = side_ref[0], side_ref[1]
    far_ref[1 : 1 + depth, 1 : 1 + height] = grad_ref[...].reshape(depth, height, width, full)
    far_ref[(far_d - 1) * (1 - side_x), 1 : 1 + height] = even_x_ref[...].reshape(height, width, full)
    far_ref[(far_d - 1) * side_x, 1 : 1 + height] = odd_x_ref[...].reshape(height, width, full)
    far_ref[:, (far_h - 1) * (1 - side_y)] = even_y_ref[...]
    far_ref[:, (far_h - 1) * side_y] = odd_y_ref[...]
    sent = far_d // 2
    send_ref[: sent * far_h * width] = far_ref[pl.ds(sent * side_x, sent)].reshape(-1, full)
    piece_rows = rows * inner // full
    for c in range(full // inner):
        send_ref[sent * far_h * width :, c * inner : (c + 1) * inner] = input_ref[
            c * piece_rows : (c + 1) * piece_rows
        ]
    total = jnp.zeros((rows, inner), jnp.float32)
    terms = [total] * 3
    for a in STEPS:
        for b in STEPS:
            piece = far_ref[1 - a : 1 - a + depth, 1 - b : 1 - b + height].reshape(rows, full)
            for c in STEPS:
                tap = 9 * (a + 1) + 3 * (b + 1) + c + 1
                terms[c + 1] += dot_nt(piece, weight_ref[:, tap * full : (tap + 1) * full])
    for c in STEPS:
        total += moved(terms[c + 1], c, width)
    out_ref[...] = total.astype(jnp.bfloat16)

    half_d, half_h, half_w = depth // 2, height // 2, width // 2
    nc = part_ref.shape[0]
    block = half_w // nc
    cells = part_ref.shape[1] - edge_ref.shape[1]
    window = cells // (half_d * half_h)
    pool_ref[...] = jnp.zeros_like(pool_ref)
    lines = total.reshape(depth, height, width, inner)
    for d in range(half_d):
        for h in range(half_h):
            acc_ref[...] = (
                lines[2 * d, 2 * h]
                + lines[2 * d, 2 * h + 1]
                + lines[2 * d + 1, 2 * h]
                + lines[2 * d + 1, 2 * h + 1]
            )
            pool_ref[d, h, 8 : 8 + half_w] = (
                acc_ref[pl.ds(0, half_w, stride=2)] + acc_ref[pl.ds(1, half_w, stride=2)]
            )
    for c in range(nc):
        start = 7 + c * block
        part_ref[c, cells:] = edge_ref[c]
        part_ref[c, :cells] = jnp.concatenate(
            [pool_ref[d, h, start : start + window] for d in range(half_d) for h in range(half_h)],
            axis=0,
        ).astype(jnp.bfloat16)


def kernel_grad_kernel(chunk, place_ref, far_ref, input_ref, got_ref, *refs):
    out_refs, (all_ref, flat_ref, pair_ref, turn_ref, wide_ref) = refs[:-5], refs[-5:]
    far_d, far_h, width, full = far_ref.shape
    depth, height = far_d - 2, far_h - 2
    rows, inner = input_ref.shape
    by_height, by_depth, window, _ = all_ref.shape
    lanes = height * width
    side, at_y = place_ref[0], place_ref[1]
    sent = far_d // 2
    pair_ref[pl.ds(depth * side, far_d)] = far_ref[...]
    pair_ref[pl.ds(far_d * (1 - side), depth)] = got_ref[: sent * far_h * width].reshape(
        sent, far_h, width, full
    )
    piece_rows = rows * inner // full
    other = jnp.concatenate(
        [
            got_ref[sent * far_h * width :, c * inner : (c + 1) * inner]
            for c in range(full // inner)
        ],
        axis=0,
    )
    for c in STEPS:
        wide_ref[c + 1, side] = moved(input_ref[...].astype(jnp.float32), -c, width).astype(jnp.bfloat16)
        wide_ref[c + 1, 1 - side] = moved(other.astype(jnp.float32), -c, width).astype(jnp.bfloat16)
    for d in range(far_d + depth):
        for b in range(3):
            turn_ref[d, b] = pair_ref[d, b : b + height].reshape(lanes, full).T
    half = full // 2
    for step in range(TAPS // 2 + 1):
        tap = TAPS // 2 * side + step
        a, b, c = tap // 9, lax.rem(tap // 3, 3), lax.rem(tap, 3)
        turned = jnp.concatenate([turn_ref[2 - a + d, 2 - b] for d in range(2 * depth)], axis=1)
        terms = dot_nn(turned, wide_ref[c].reshape(2 * rows, inner))
        first = pl.multiple_of(step * full + half - half * side, half)
        flat_ref[pl.ds(first, full)] = terms.astype(jnp.bfloat16)
    for owner in range(by_depth * by_height):
        start = half + owner * chunk // 16 * 16
        all_ref[owner % by_height, owner // by_height] = flat_ref[start : start + window]
    for k, out_ref in enumerate(out_refs):
        out_ref[...] = all_ref[at_y ^ k]


def bottom_kernel(
    down_ref, up_ref, before_ref, pre_ref, after_ref, weight_ref, part_ref, shift_ref
):
    _, far_d, far_w, height, filters = shift_ref.shape
    depth, width = far_d - 2, far_w - 2
    rows = depth * width * height
    channels = part_ref.shape[1]
    back = dot_nt(down_ref[...], up_ref[...])
    saved = jnp.concatenate([before_ref[...], pre_ref[...], after_ref[...]], axis=1)
    saved = saved.reshape(depth * far_w * height, filters)
    grad = jnp.where(saved.astype(jnp.float32) > 0, back, 0.0)
    shift_ref[:, :1] = jnp.zeros((3, 1) + shift_ref.shape[2:], jnp.bfloat16)
    shift_ref[:, far_d - 1 :] = jnp.zeros((3, 1) + shift_ref.shape[2:], jnp.bfloat16)
    for b in STEPS:
        shift_ref[b + 1, 1 : 1 + depth] = (
            moved(grad, b, height).astype(jnp.bfloat16).reshape(depth, far_w, height, filters)
        )
    total = jnp.zeros((rows, channels), jnp.float32)
    for a in STEPS:
        for b in STEPS:
            tap = 9 * (a + 1) + 3 * (b + 1)
            piece = jnp.concatenate(
                [
                    shift_ref[b + 1, 1 - a : 1 - a + depth, 1 - c : 1 - c + width].reshape(rows, filters)
                    for c in STEPS
                ],
                axis=1,
            )
            weight = jnp.concatenate([weight_ref[tap + c] for c in range(3)], axis=1)
            total += dot_nt(piece, weight)
    part_ref[...] = total.astype(jnp.bfloat16)


def bottom_weight_kernel(down_ref, pre_ref, source_ref, shift_ref, both_ref):
    _, far_d, far_w, height, filters = shift_ref.shape
    depth, width = far_d - 2, far_w - 2
    rows, channels = source_ref.shape
    groups = both_ref.shape[0]
    thin = channels // groups
    full = down_ref.shape[1]
    inner = full // groups
    own_down = down_ref[...].reshape(depth, far_w, height, full)[:, 1 : 1 + width].reshape(rows, full)
    own_saved = pre_ref[...].reshape(rows, filters)
    up_part = dot_tn(jnp.maximum(own_saved, 0), own_down).astype(jnp.bfloat16)
    for cc in range(groups):
        both_ref[cc, TAPS * thin :] = up_part[:, cc * inner : (cc + 1) * inner]
    turned = source_ref[...].T
    for a in STEPS:
        for b in STEPS:
            tap = 9 * (a + 1) + 3 * (b + 1)
            piece = jnp.concatenate(
                [
                    shift_ref[b + 1, 1 - a : 1 - a + depth, 1 - c : 1 - c + width].reshape(rows, filters)
                    for c in STEPS
                ],
                axis=1,
            )
            terms = dot_nn(turned, piece).astype(jnp.bfloat16)
            for c in range(3):
                for cc in range(groups):
                    both_ref[cc, (tap + c) * thin : (tap + c + 1) * thin] = terms[
                        cc * thin : (cc + 1) * thin, c * filters : (c + 1) * filters
                    ]


def per_device(
    pre_bottom,
    bottom_input,
    bottom_weight,
    up_weight,
    level_input,
    pre_level,
    level_cotangent,
    labels,
    level_weight,
    aux_weight,
):
    nx, ny, nc = (lax.axis_size(a) for a in ("gx", "gy", "col"))
    at_x, at_y, at_c = (lax.axis_index(a) for a in ("gx", "gy", "col"))
    depth, height, width, inner = level_input.shape
    full = inner * nc
    rows = depth * height * width
    far_d, far_h = depth + 2, height + 2
    half_d, half_h, half_w = depth // 2, height // 2, width // 2
    block = half_w // nc
    wide = block + 2
    bottom_d, bottom_h, _, filters = pre_bottom.shape
    bf16, f32 = jnp.bfloat16, jnp.float32
    struct = jax.ShapeDtypeStruct

    own_pre = pre_level.reshape(rows, inner)
    payload = jnp.concatenate(
        [
            own_pre,
            level_cotangent.reshape(rows, inner),
            jnp.pad(aux_weight.T, ((0, CLASS_ROWS - CLASSES), (0, 0))),
        ]
    )
    gathered = lax.all_gather(payload, "col")
    lanes = height * width
    side_x, side_y = at_x % 2, at_y % 2
    sides = jnp.stack([side_x, side_y]).astype(jnp.int32)
    level_pre_grad, even_x, odd_x, aux_part = local_call(
        class_kernel,
        (
            struct((rows, full), bf16),
            struct((lanes, full), bf16),
            struct((lanes, full), bf16),
            struct((CLASS_ROWS, inner), bf16),
        ),
        [],
        6 * rows * full * CLASS_ROWS,
        2 * gathered.size,
        sides,
        gathered,
        own_pre,
        labels.reshape(1, rows),
        level_weight,
        stay=4,
    )

    even_x = swap(even_x, "gx", 1)
    odd_x = swap_odd(odd_x, "gx")

    def lines(start):
        take = lambda x: x[start : start + width]
        before = jnp.where(side_x == 1, take(even_x), take(odd_x))
        after = jnp.where(side_x == 1, take(odd_x), take(even_x))
        own = level_pre_grad.reshape(depth, lanes, full)
        return jnp.stack([before] + [take(own[d]) for d in range(depth)] + [after])

    first, last = lines(0), lines(lanes - width)
    even_y = swap(jnp.where(side_y == 1, first, last), "gy", 1)
    odd_y = swap_odd(jnp.where(side_y == 1, last, first), "gy")

    turned_pre = pre_bottom.transpose(0, 2, 1, 3)
    edges = jnp.stack(
        [
            jnp.where(at_c < c, turned_pre[:, -1], turned_pre[:, 0]).reshape(-1, filters)
            for c in range(nc)
        ]
    )

    window = (wide + 7) // 8 * 8
    cells = half_d * half_h * window
    flat_input = level_input.reshape(rows, inner)
    far, level_input_grad, parts, send = local_call(
        conv_kernel,
        (
            struct((far_d, far_h, width, full), bf16),
            struct((rows, inner), bf16),
            struct((nc, cells + edges.shape[1], inner), bf16),
            struct((far_d // 2 * far_h * width + rows * inner // full, full), bf16),
        ),
        [
            pltpu.VMEM((width, inner), f32),
            pltpu.VMEM((half_d, half_h, half_w + 24, inner), f32),
        ],
        2 * rows * full * TAPS * inner,
        2 * level_weight.size,
        sides,
        level_pre_grad,
        even_x,
        odd_x,
        even_y,
        odd_y,
        flat_input,
        edges,
        level_weight,
    )
    got = swap(send, "gx", 1)
    level_input_grad = level_input_grad.reshape(level_input.shape)

    relayed = exchange(parts, "col")
    edges = relayed[:, cells:].reshape(nc, bottom_d, 1, bottom_h, filters)
    relayed = relayed[:, :cells].reshape(nc * cells, inner)

    def edge_of(c):
        found = lax.dynamic_index_in_dim(edges, jnp.clip(c, 0, nc - 1), 0, keepdims=False)
        return jnp.where((c >= 0) & (c < nc), found, jnp.zeros_like(found))

    pre_before, pre_after = edge_of(at_c - 1), edge_of(at_c + 1)

    chunk = TAPS * full // (nx * ny)
    span = chunk + 8 if chunk % 16 else chunk
    level_parts = local_call(
        functools.partial(kernel_grad_kernel, chunk),
        [struct((nx // 2, span, inner), bf16)] * ny,
        [
            pltpu.VMEM((ny, nx // 2, span, inner), bf16),
            pltpu.VMEM(((TAPS + 2) * full // 2, inner), bf16),
            pltpu.VMEM((far_d + depth, far_h, width, full), bf16),
            pltpu.VMEM((far_d + depth, 3, full, lanes), bf16),
            pltpu.VMEM((3, 2, rows, inner), bf16),
        ],
        2 * rows * full * TAPS * inner,
        2 * nx * ny * span * inner,
        jnp.stack([side_x, at_y]).astype(jnp.int32),
        far,
        flat_input,
        got,
    )
    terms = [level_parts[0]] + [swap(level_parts[k], "gy", k) for k in range(1, ny)]
    relayed = behind(relayed, level_parts[0])

    by_depth = spread(jnp.concatenate([relayed, aux_part]), "gx")
    aux_sum = by_depth[:, nc * cells :].astype(f32).sum(axis=0).astype(bf16)
    by_depth = behind(by_depth, *terms[1 : ny // 2])
    line = by_depth[:, : nc * cells].reshape(nx, nc, half_d * half_h, window, inner)[:, :, :, :wide]
    split = nx * nc * half_d * half_h * wide
    by_height = spread(jnp.concatenate([line.reshape(split, inner), aux_sum]), "gy")
    aux_weight_grad = by_height[:, split : split + CLASSES].astype(f32).sum(axis=0).T
    down_wide = (
        by_height[:, :split]
        .reshape(ny, nx, nc, half_d, half_h, wide, inner)
        .transpose(1, 3, 5, 0, 4, 2, 6)
        .reshape(bottom_d * wide * bottom_h, full)
    )

    level_part = sum(t.astype(f32) for t in terms).astype(bf16)
    down_wide = behind(down_wide, terms[ny // 2])

    bottom_rows = bottom_d * block * bottom_h
    channel_width = bottom_weight.shape[0]
    thin = channel_width // nc
    part, shifts = local_call(
        bottom_kernel,
        (
            struct((bottom_rows, channel_width), bf16),
            struct((3, bottom_d + 2, wide, bottom_h, filters), bf16),
        ),
        [],
        2 * bottom_rows * channel_width * TAPS * filters,
        2 * bottom_weight.size,
        down_wide,
        up_weight,
        pre_before,
        turned_pre,
        pre_after,
        bottom_weight.transpose(1, 0, 2),
    )
    (both,) = local_call(
        bottom_weight_kernel,
        [struct((nc, TAPS * thin + filters, inner), bf16)],
        [],
        2 * bottom_rows * channel_width * TAPS * filters,
        2 * bottom_weight.size,
        down_wide,
        turned_pre,
        bottom_input.transpose(0, 2, 1, 3).reshape(bottom_rows, channel_width),
        shifts,
    )
    part = exchange(part.reshape(ny, bottom_rows // ny, channel_width), "gy")
    pairs = nx // 2
    level_sum = jnp.zeros((span, inner), f32)
    for step in range(pairs):
        if step == pairs // 2:
            level_part = behind(level_part, part)
        chosen = lax.dynamic_index_in_dim(
            level_part, lax.rem(at_x // 2 + step, pairs), 0, keepdims=False
        )
        level_sum += lax.ppermute(
            chosen, "gx", [(i, i % 2 * pairs + (i // 2 + step) % pairs) for i in range(nx)]
        ).astype(f32)
    level_part = level_sum
    if span != chunk:
        odd = lax.rem(at_y + at_x * ny, 2)
        level_part = jnp.where(odd == 1, level_part[span - chunk :], level_part[:chunk])
    level_weight_grad = level_part.T
    share = bottom_d // ny
    bottom_input_grad = (
        part.astype(f32)
        .sum(axis=0)
        .astype(bf16)
        .reshape(share, block, bottom_h, channel_width)
        .transpose(0, 2, 1, 3)
    )
    both, _ = summed_by_pairs(both, "col", bits_of("col")[::-1], part)
    bottom_weight_grad = both[: TAPS * thin].reshape(TAPS, thin, filters).transpose(1, 0, 2)
    up_weight_grad = both[TAPS * thin :]
    return (
        level_input_grad,
        bottom_input_grad,
        level_weight_grad,
        bottom_weight_grad,
        up_weight_grad,
        aux_weight_grad,
    )


def solution(mesh):
    return jax.shard_map(
        per_device,
        mesh=mesh,
        in_specs=(
            P(None, None, "col", "gy"),
            P(None, None, "col", "gx"),
            P("gx", None, "gy"),
            P("gy", None),
            P("gx", "gy", None, "col"),
            P("gx", "gy", None, "col"),
            P("gx", "gy", None, "col"),
            P("gx", "gy", None),
            P("col", None),
            P("col", None),
        ),
        out_specs=(
            P("gx", "gy", None, "col"),
            P("gy", None, "col", "gx"),
            P("col", ("gx", "gy")),
            P(("gx", "col"), None, "gy"),
            P("gy", "col"),
            P("col", None),
        ),
        check_vma=False,
    )
```

```python
import functools

import jax
import jax.numpy as jnp
from jax import lax
from jax.experimental import pallas as pl
from jax.experimental.pallas import tpu as pltpu
from jax.sharding import PartitionSpec as P

CLASSES = 14
CLASS_ROWS = 16
TAPS = 27
VMEM_LIMIT = 48 * 1024 * 1024
VMEM_MORE = 60 * 1024 * 1024
STEPS = (-1, 0, 1)


def exchange(x, axis):
    return lax.all_to_all(x, axis, split_axis=0, concat_axis=0, tiled=False)


def spread(x, axis):
    size = lax.axis_size(axis)
    return exchange(jnp.broadcast_to(x[None], (size,) + x.shape), axis)


def behind(x, *others):
    return lax.optimization_barrier((x,) + others)[0]


def bits_of(axis):
    return [1 << k for k in reversed(range(lax.axis_size(axis).bit_length() - 1))]


def swap(x, axis, bit):
    return lax.ppermute(x, axis, [(i, i ^ bit) for i in range(lax.axis_size(axis))])


def swap_odd(x, axis):
    last = lax.axis_size(axis) - 1
    return lax.ppermute(
        x, axis, [(i, i + 1 if i % 2 else i - 1) for i in range(1, last)]
    )


def mine_and_other(x, axis, bit, dim):
    own = lax.axis_index(axis) // bit % 2
    take = functools.partial(lax.dynamic_index_in_dim, x, axis=dim, keepdims=False)
    return take(own), take(1 - own)


def summed_by_pairs(x, axis, bits, order, first=None):
    x = x.reshape((2,) * len(bits) + x.shape[1:])
    left = list(bits)
    for bit in order:
        if bit == order[-1] and first is not None:
            x = behind(x, first)
        own, other = mine_and_other(x, axis, bit, left.index(bit))
        left.remove(bit)
        x = own.astype(jnp.float32) + swap(other.astype(jnp.bfloat16), axis, bit).astype(jnp.float32)
    return x


def dot_nn(a, b):
    return lax.dot_general(a, b, (((1,), (0,)), ((), ())), preferred_element_type=jnp.float32)


def dot_tn(a, b):
    return lax.dot_general(a, b, (((0,), (0,)), ((), ())), preferred_element_type=jnp.float32)


def dot_nt(a, b):
    return lax.dot_general(a, b, (((1,), (1,)), ((), ())), preferred_element_type=jnp.float32)


def moved(x, step, period):
    if step == 0:
        return x
    rows = x.shape[0]
    place = lax.rem(lax.broadcasted_iota(jnp.int32, x.shape, 0), period)
    edge = 0 if step == 1 else period - 1
    return jnp.where(place == edge, 0.0, pltpu.roll(x, step % rows, 0))


def local_call(body, out_shapes, scratch, flops, moved_bytes, *args, stay=None):
    return pl.pallas_call(
        body,
        out_shape=list(out_shapes),
        in_specs=[
            pl.BlockSpec(
                memory_space=pltpu.HBM if k == stay else pltpu.SMEM if a.ndim == 1 else pltpu.VMEM
            )
            for k, a in enumerate(args)
        ],
        out_specs=[pl.BlockSpec(memory_space=pltpu.VMEM)] * len(out_shapes),
        scratch_shapes=scratch,
        cost_estimate=pl.CostEstimate(flops=flops, bytes_accessed=moved_bytes, transcendentals=0),
        compiler_params=pltpu.CompilerParams(vmem_limit_bytes=VMEM_LIMIT if stay is None else VMEM_MORE),
    )(*args)


def pack_kernel(saved_ref, cotangent_ref, weight_ref, later_ref, out_ref):
    del later_ref
    rows, inner = saved_ref.shape
    out_ref[:rows] = saved_ref[...]
    out_ref[rows : 2 * rows] = cotangent_ref[...]
    spare = CLASS_ROWS - weight_ref.shape[0]
    out_ref[2 * rows :] = jnp.concatenate(
        [weight_ref[...].astype(jnp.float32), jnp.zeros((spare, inner), jnp.float32)], axis=0
    ).astype(jnp.bfloat16)


def class_kernel(gathered_ref, own_ref, label_ref, grad_ref, even_ref, odd_ref, aux_ref):
    side = lax.rem(lax.axis_index("gx"), 2)
    groups, rows, inner = gathered_ref.shape[0], own_ref.shape[0], own_ref.shape[1]
    logits = jnp.zeros((CLASS_ROWS, rows), jnp.float32)
    for c in range(groups):
        weight = gathered_ref[c, 2 * rows : 2 * rows + CLASS_ROWS]
        logits += dot_nt(weight, jnp.maximum(gathered_ref[c, :rows], 0))
    place = lax.broadcasted_iota(jnp.int32, logits.shape, 0)
    real = place < CLASSES
    logits = jnp.where(real, logits, -jnp.inf)
    powers = jnp.exp(logits - jnp.max(logits, axis=0, keepdims=True))
    probabilities = powers / jnp.sum(powers, axis=0, keepdims=True)
    labels = jnp.concatenate(
        [
            label_ref[d, h : h + 1]
            for d in range(label_ref.shape[0])
            for h in range(label_ref.shape[1])
        ],
        axis=1,
    )
    onehot = jnp.where(place == labels, 1.0, 0.0)
    logit_grad = jnp.where(real, probabilities - onehot, 0.0).astype(jnp.bfloat16)
    for c in range(groups):
        weight = gathered_ref[c, 2 * rows : 2 * rows + CLASS_ROWS]
        total = gathered_ref[c, rows : 2 * rows].astype(jnp.float32) + dot_tn(logit_grad, weight)
        active = gathered_ref[c, :rows].astype(jnp.float32) > 0
        grad_ref[:, c * inner : (c + 1) * inner] = jnp.where(active, total, 0.0).astype(jnp.bfloat16)
    size = even_ref.shape[0]
    first = pl.multiple_of((rows - size) * side, size)
    even_ref[...] = grad_ref[pl.ds(rows - size - first, size)]
    odd_ref[...] = grad_ref[pl.ds(first, size)]
    aux_ref[...] = dot_nn(logit_grad, jnp.maximum(own_ref[...], 0)).astype(jnp.bfloat16)


def conv_kernel(
    grad_ref,
    even_x_ref,
    odd_x_ref,
    even_y_ref,
    odd_y_ref,
    input_ref,
    edge_ref,
    weight_ref,
    far_ref,
    out_ref,
    part_ref,
    send_ref,
    acc_ref,
    pool_ref,
):
    far_d, far_h, width, full = far_ref.shape
    depth, height = far_d - 2, far_h - 2
    inner = out_ref.shape[1]
    rows = depth * height * width
    side_x, side_y = (lax.rem(lax.axis_index(a), 2) for a in ("gx", "gy"))
    far_ref[1 : 1 + depth, 1 : 1 + height] = grad_ref[...].reshape(depth, height, width, full)
    far_ref[(far_d - 1) * (1 - side_x), 1 : 1 + height] = even_x_ref[...].reshape(height, width, full)
    far_ref[(far_d - 1) * side_x, 1 : 1 + height] = odd_x_ref[...].reshape(height, width, full)
    far_ref[:, (far_h - 1) * (1 - side_y)] = even_y_ref[...]
    far_ref[:, (far_h - 1) * side_y] = odd_y_ref[...]
    sent = far_d // 2
    send_ref[: sent * far_h * width] = far_ref[pl.ds(sent * side_x, sent)].reshape(-1, full)
    piece_rows = rows * inner // full
    for c in range(full // inner):
        send_ref[sent * far_h * width :, c * inner : (c + 1) * inner] = input_ref[
            c * piece_rows : (c + 1) * piece_rows
        ]
    total = jnp.zeros((rows, inner), jnp.float32)
    terms = [total] * 3
    for a in STEPS:
        for b in STEPS:
            piece = far_ref[1 - a : 1 - a + depth, 1 - b : 1 - b + height].reshape(rows, full)
            for c in STEPS:
                tap = 9 * (a + 1) + 3 * (b + 1) + c + 1
                terms[c + 1] += dot_nt(piece, weight_ref[:, tap * full : (tap + 1) * full])
    for c in STEPS:
        total += moved(terms[c + 1], c, width)
    out_ref[...] = total.astype(jnp.bfloat16)

    half_d, half_h, half_w = depth // 2, height // 2, width // 2
    nc = part_ref.shape[0]
    block = half_w // nc
    cells = part_ref.shape[1] - edge_ref.shape[1]
    window = cells // (half_d * half_h)
    pool_ref[...] = jnp.zeros_like(pool_ref)
    lines = total.reshape(depth, height, width, inner)
    for d in range(half_d):
        for h in range(half_h):
            acc_ref[...] = (
                lines[2 * d, 2 * h]
                + lines[2 * d, 2 * h + 1]
                + lines[2 * d + 1, 2 * h]
                + lines[2 * d + 1, 2 * h + 1]
            )
            pool_ref[d, h, 8 : 8 + half_w] = (
                acc_ref[pl.ds(0, half_w, stride=2)] + acc_ref[pl.ds(1, half_w, stride=2)]
            )
    for c in range(nc):
        start = 7 + c * block
        part_ref[c, cells:] = edge_ref[c]
        part_ref[c, :cells] = jnp.concatenate(
            [pool_ref[d, h, start : start + window] for d in range(half_d) for h in range(half_h)],
            axis=0,
        ).astype(jnp.bfloat16)


def kernel_grad_kernel(chunk, far_ref, input_ref, got_ref, *refs):
    out_refs, (all_ref, flat_ref, pair_ref, turn_ref, wide_ref) = refs[:-5], refs[-5:]
    far_d, far_h, width, full = far_ref.shape
    depth, height = far_d - 2, far_h - 2
    rows, inner = input_ref.shape
    by_height, by_depth, window, _ = all_ref.shape
    lanes = height * width
    side, at_y = lax.rem(lax.axis_index("gx"), 2), lax.axis_index("gy")
    sent = far_d // 2
    pair_ref[pl.ds(depth * side, far_d)] = far_ref[...]
    pair_ref[pl.ds(far_d * (1 - side), depth)] = got_ref[: sent * far_h * width].reshape(
        sent, far_h, width, full
    )
    piece_rows = rows * inner // full
    other = jnp.concatenate(
        [
            got_ref[sent * far_h * width :, c * inner : (c + 1) * inner]
            for c in range(full // inner)
        ],
        axis=0,
    )
    for c in STEPS:
        wide_ref[c + 1, side] = moved(input_ref[...].astype(jnp.float32), -c, width).astype(jnp.bfloat16)
        wide_ref[c + 1, 1 - side] = moved(other.astype(jnp.float32), -c, width).astype(jnp.bfloat16)
    for d in range(far_d + depth):
        for b in range(3):
            turn_ref[d, b] = pair_ref[d, b : b + height].reshape(lanes, full).T
    span = chunk * by_height
    grain = 16
    for m in range(by_depth):
        begin = span * (2 * m + side)
        for step in range((span - 1) // full + 2):
            tap = begin // full + step

            @pl.when(tap * full < begin + span)
            def _():
                a, b, c = tap // 9, lax.rem(tap // 3, 3), lax.rem(tap, 3)
                turned = jnp.concatenate([turn_ref[2 - a + d, 2 - b] for d in range(2 * depth)], axis=1)
                terms = dot_nn(turned, wide_ref[c].reshape(2 * rows, inner))
                first = pl.multiple_of(tap * full - begin + full, grain)
                flat_ref[m, pl.ds(first, full)] = terms.astype(jnp.bfloat16)

        for j in range(by_height):
            start = full + j * chunk // grain * grain
            all_ref[j, m] = flat_ref[m, start : start + window]
    for k, out_ref in enumerate(out_refs):
        out_ref[...] = all_ref[pl.ds(2 * (at_y // 2 ^ k), 2)]


def bottom_kernel(
    down_ref, up_ref, before_ref, pre_ref, after_ref, weight_ref, part_ref, shift_ref
):
    _, far_d, far_w, height, filters = shift_ref.shape
    depth, width = far_d - 2, far_w - 2
    rows = depth * width * height
    channels = part_ref.shape[1]
    back = dot_nt(down_ref[...], up_ref[...])
    saved = jnp.concatenate([before_ref[...], pre_ref[...], after_ref[...]], axis=1)
    saved = saved.reshape(depth * far_w * height, filters)
    grad = jnp.where(saved.astype(jnp.float32) > 0, back, 0.0)
    shift_ref[:, :1] = jnp.zeros((3, 1) + shift_ref.shape[2:], jnp.bfloat16)
    shift_ref[:, far_d - 1 :] = jnp.zeros((3, 1) + shift_ref.shape[2:], jnp.bfloat16)
    for b in STEPS:
        shift_ref[b + 1, 1 : 1 + depth] = (
            moved(grad, b, height).astype(jnp.bfloat16).reshape(depth, far_w, height, filters)
        )
    total = jnp.zeros((rows, channels), jnp.float32)
    for a in STEPS:
        for b in STEPS:
            tap = 9 * (a + 1) + 3 * (b + 1)
            piece = jnp.concatenate(
                [
                    shift_ref[b + 1, 1 - a : 1 - a + depth, 1 - c : 1 - c + width].reshape(rows, filters)
                    for c in STEPS
                ],
                axis=1,
            )
            weight = jnp.concatenate([weight_ref[tap + c] for c in range(3)], axis=1)
            total += dot_nt(piece, weight)
    part_ref[...] = total.astype(jnp.bfloat16)


def bottom_weight_kernel(down_ref, pre_ref, source_ref, shift_ref, both_ref):
    _, far_d, far_w, height, filters = shift_ref.shape
    depth, width = far_d - 2, far_w - 2
    rows, channels = source_ref.shape
    groups = both_ref.shape[0]
    thin = channels // groups
    full = down_ref.shape[1]
    inner = full // groups
    own_down = down_ref[...].reshape(depth, far_w, height, full)[:, 1 : 1 + width].reshape(rows, full)
    own_saved = pre_ref[...].reshape(rows, filters)
    up_part = dot_tn(jnp.maximum(own_saved, 0), own_down).astype(jnp.bfloat16)
    for cc in range(groups):
        both_ref[cc, TAPS * thin :] = up_part[:, cc * inner : (cc + 1) * inner]
    turned = source_ref[...].T
    for a in STEPS:
        for b in STEPS:
            tap = 9 * (a + 1) + 3 * (b + 1)
            piece = jnp.concatenate(
                [
                    shift_ref[b + 1, 1 - a : 1 - a + depth, 1 - c : 1 - c + width].reshape(rows, filters)
                    for c in STEPS
                ],
                axis=1,
            )
            terms = dot_nn(turned, piece).astype(jnp.bfloat16)
            for c in range(3):
                for cc in range(groups):
                    both_ref[cc, (tap + c) * thin : (tap + c + 1) * thin] = terms[
                        cc * thin : (cc + 1) * thin, c * filters : (c + 1) * filters
                    ]


def per_device(
    pre_bottom,
    bottom_input,
    bottom_weight,
    up_weight,
    level_input,
    pre_level,
    level_cotangent,
    labels,
    level_weight,
    aux_weight,
):
    nx, ny, nc = (lax.axis_size(a) for a in ("gx", "gy", "col"))
    at_x, at_y, at_c = (lax.axis_index(a) for a in ("gx", "gy", "col"))
    depth, height, width, inner = level_input.shape
    full = inner * nc
    rows = depth * height * width
    far_d, far_h = depth + 2, height + 2
    half_d, half_h, half_w = depth // 2, height // 2, width // 2
    block = half_w // nc
    wide = block + 2
    bottom_d, bottom_h, _, filters = pre_bottom.shape
    bf16, f32 = jnp.bfloat16, jnp.float32
    struct = jax.ShapeDtypeStruct

    own_pre = pre_level.reshape(rows, inner)
    (payload,) = local_call(
        pack_kernel,
        [struct((2 * rows + CLASS_ROWS, inner), bf16)],
        [],
        0,
        2 * pre_level.size,
        own_pre,
        level_cotangent.reshape(rows, inner),
        aux_weight.T,
        level_weight,
        stay=3,
    )
    gathered = lax.all_gather(payload, "col")
    lanes = height * width
    side_x, side_y = at_x % 2, at_y % 2
    level_pre_grad, even_x, odd_x, aux_part = local_call(
        class_kernel,
        (
            struct((rows, full), bf16),
            struct((lanes, full), bf16),
            struct((lanes, full), bf16),
            struct((CLASS_ROWS, inner), bf16),
        ),
        [],
        6 * rows * full * CLASS_ROWS,
        2 * gathered.size,
        gathered,
        own_pre,
        labels,
    )

    even_x = swap(even_x, "gx", 1)
    odd_x = swap_odd(odd_x, "gx")

    def lines(start):
        take = lambda x: x[start : start + width]
        before = jnp.where(side_x == 1, take(even_x), take(odd_x))
        after = jnp.where(side_x == 1, take(odd_x), take(even_x))
        own = level_pre_grad.reshape(depth, lanes, full)
        return jnp.stack([before] + [take(own[d]) for d in range(depth)] + [after])

    first, last = lines(0), lines(lanes - width)
    even_y = swap(jnp.where(side_y == 1, first, last), "gy", 1)
    odd_y = swap_odd(jnp.where(side_y == 1, last, first), "gy")

    turned_pre = pre_bottom.transpose(0, 2, 1, 3)
    edges = jnp.stack(
        [
            jnp.where(at_c < c, turned_pre[:, -1], turned_pre[:, 0]).reshape(-1, filters)
            for c in range(nc)
        ]
    )

    window = (wide + 7) // 8 * 8
    cells = half_d * half_h * window
    flat_input = level_input.reshape(rows, inner)
    far, level_input_grad, parts, send = local_call(
        conv_kernel,
        (
            struct((far_d, far_h, width, full), bf16),
            struct((rows, inner), bf16),
            struct((nc, cells + edges.shape[1], inner), bf16),
            struct((far_d // 2 * far_h * width + rows * inner // full, full), bf16),
        ),
        [
            pltpu.VMEM((width, inner), f32),
            pltpu.VMEM((half_d, half_h, half_w + 24, inner), f32),
        ],
        2 * rows * full * TAPS * inner,
        2 * level_weight.size,
        level_pre_grad,
        even_x,
        odd_x,
        even_y,
        odd_y,
        flat_input,
        edges,
        level_weight,
    )
    got = swap(send, "gx", 1)
    level_input_grad = level_input_grad.reshape(level_input.shape)

    relayed = exchange(parts, "col")
    edges = relayed[:, cells:].reshape(nc, bottom_d, 1, bottom_h, filters)
    relayed = relayed[:, :cells].reshape(nc * cells, inner)

    def edge_of(c):
        found = lax.dynamic_index_in_dim(edges, jnp.clip(c, 0, nc - 1), 0, keepdims=False)
        return jnp.where((c >= 0) & (c < nc), found, jnp.zeros_like(found))

    pre_before, pre_after = edge_of(at_c - 1), edge_of(at_c + 1)

    chunk = TAPS * full // (nx * ny)
    span = chunk + 8 if chunk % 16 else chunk
    level_parts = local_call(
        functools.partial(kernel_grad_kernel, chunk),
        [struct((2, nx // 2, span, inner), bf16)] * (ny // 2),
        [
            pltpu.VMEM((ny, nx // 2, span, inner), bf16),
            pltpu.VMEM((nx // 2, (chunk * ny - 1) // full * full + 4 * full, inner), bf16),
            pltpu.VMEM((far_d + depth, far_h, width, full), bf16),
            pltpu.VMEM((far_d + depth, 3, full, lanes), bf16),
            pltpu.VMEM((3, 2, rows, inner), bf16),
        ],
        2 * rows * full * TAPS * inner,
        2 * nx * ny * span * inner,
        far,
        flat_input,
        got,
    )
    terms = [level_parts[0]] + [swap(level_parts[k], "gy", 2 * k) for k in range(1, ny // 2)]
    relayed = behind(relayed, level_parts[0])

    by_depth = spread(jnp.concatenate([relayed, aux_part]), "gx")
    aux_sum = by_depth[:, nc * cells :].astype(f32).sum(axis=0).astype(bf16)
    by_depth = behind(by_depth, terms[1], terms[-1])
    line = by_depth[:, : nc * cells].reshape(nx, nc, half_d * half_h, window, inner)[:, :, :, :wide]
    split = nx * nc * half_d * half_h * wide
    by_height = spread(jnp.concatenate([line.reshape(split, inner), aux_sum]), "gy")
    aux_weight_grad = by_height[:, split : split + CLASSES].astype(f32).sum(axis=0).T
    down_wide = (
        by_height[:, :split]
        .reshape(ny, nx, nc, half_d, half_h, wide, inner)
        .transpose(1, 3, 5, 0, 4, 2, 6)
        .reshape(bottom_d * wide * bottom_h, full)
    )

    down_wide = behind(down_wide, terms[ny // 4])
    level_part = sum(t.astype(f32) for t in terms)
    level_part = summed_by_pairs(level_part, "gy", [1], [1])

    bottom_rows = bottom_d * block * bottom_h
    channel_width = bottom_weight.shape[0]
    thin = channel_width // nc
    part, shifts = local_call(
        bottom_kernel,
        (
            struct((bottom_rows, channel_width), bf16),
            struct((3, bottom_d + 2, wide, bottom_h, filters), bf16),
        ),
        [],
        2 * bottom_rows * channel_width * TAPS * filters,
        2 * bottom_weight.size,
        down_wide,
        up_weight,
        pre_before,
        turned_pre,
        pre_after,
        bottom_weight.transpose(1, 0, 2),
    )
    (both,) = local_call(
        bottom_weight_kernel,
        [struct((nc, TAPS * thin + filters, inner), bf16)],
        [],
        2 * bottom_rows * channel_width * TAPS * filters,
        2 * bottom_weight.size,
        down_wide,
        turned_pre,
        bottom_input.transpose(0, 2, 1, 3).reshape(bottom_rows, channel_width),
        shifts,
    )
    part = exchange(part.reshape(ny, bottom_rows // ny, channel_width), "gy")
    level_part = summed_by_pairs(level_part, "gx", bits_of("gx")[:-1], bits_of("gx")[-2::-1], part)
    if span != chunk:
        odd = lax.rem(at_y + at_x * ny, 2)
        level_part = jnp.where(odd == 1, level_part[span - chunk :], level_part[:chunk])
    level_weight_grad = level_part.T
    share = bottom_d // ny
    bottom_input_grad = (
        part.astype(f32)
        .sum(axis=0)
        .astype(bf16)
        .reshape(share, block, bottom_h, channel_width)
        .transpose(0, 2, 1, 3)
    )
    both = summed_by_pairs(both, "col", bits_of("col"), bits_of("col")[::-1], part)
    bottom_weight_grad = both[: TAPS * thin].reshape(TAPS, thin, filters).transpose(1, 0, 2)
    up_weight_grad = both[TAPS * thin :]
    return (
        level_input_grad,
        bottom_input_grad,
        level_weight_grad,
        bottom_weight_grad,
        up_weight_grad,
        aux_weight_grad,
    )


def solution(mesh):
    return jax.shard_map(
        per_device,
        mesh=mesh,
        in_specs=(
            P(None, None, "col", "gy"),
            P(None, None, "col", "gx"),
            P("gx", None, "gy"),
            P("gy", None),
            P("gx", "gy", None, "col"),
            P("gx", "gy", None, "col"),
            P("gx", "gy", None, "col"),
            P("gx", "gy", None),
            P("col", None),
            P("col", None),
        ),
        out_specs=(
            P("gx", "gy", None, "col"),
            P("gy", None, "col", "gx"),
            P("col", ("gx", "gy")),
            P(("gx", "col"), None, "gy"),
            P("gy", "col"),
            P("col", None),
        ),
        check_vma=False,
    )
```

```python
import functools

import jax
import jax.numpy as jnp
from jax import lax
from jax.experimental import pallas as pl
from jax.experimental.pallas import tpu as pltpu
from jax.sharding import PartitionSpec as P

CLASSES = 14
CLASS_ROWS = 16
TAPS = 27
VMEM_LIMIT = 24 * 1024 * 1024
VMEM_MORE = 60 * 1024 * 1024
STEPS = (-1, 0, 1)


def exchange(x, axis):
    return lax.all_to_all(x, axis, split_axis=0, concat_axis=0, tiled=False)


def spread(x, axis):
    size = lax.axis_size(axis)
    return exchange(jnp.broadcast_to(x[None], (size,) + x.shape), axis)


def behind(x, *others):
    return lax.optimization_barrier((x,) + others)[0]


def bits_of(axis):
    return [1 << k for k in reversed(range(lax.axis_size(axis).bit_length() - 1))]


def swap(x, axis, bit):
    return lax.ppermute(x, axis, [(i, i ^ bit) for i in range(lax.axis_size(axis))])


def swap_odd(x, axis):
    last = lax.axis_size(axis) - 1
    return lax.ppermute(
        x, axis, [(i, i + 1 if i % 2 else i - 1) for i in range(1, last)]
    )


def mine_and_other(x, axis, bit, dim):
    own = lax.axis_index(axis) // bit % 2
    take = functools.partial(lax.dynamic_index_in_dim, x, axis=dim, keepdims=False)
    return take(own), take(1 - own)


def summed_by_pairs(x, axis, bits, order, first=None):
    x = x.reshape((2,) * len(bits) + x.shape[1:])
    left = list(bits)
    for bit in order:
        if bit == order[-1] and first is not None:
            x = behind(x, first)
        own, other = mine_and_other(x, axis, bit, left.index(bit))
        left.remove(bit)
        x = own.astype(jnp.float32) + swap(other.astype(jnp.bfloat16), axis, bit).astype(jnp.float32)
    return x


def dot_nn(a, b):
    return lax.dot_general(a, b, (((1,), (0,)), ((), ())), preferred_element_type=jnp.float32)


def dot_tn(a, b):
    return lax.dot_general(a, b, (((0,), (0,)), ((), ())), preferred_element_type=jnp.float32)


def dot_nt(a, b):
    return lax.dot_general(a, b, (((1,), (1,)), ((), ())), preferred_element_type=jnp.float32)


def moved(x, step, period):
    if step == 0:
        return x
    rows = x.shape[0]
    place = lax.rem(lax.broadcasted_iota(jnp.int32, x.shape, 0), period)
    edge = 0 if step == 1 else period - 1
    return jnp.where(place == edge, 0.0, pltpu.roll(x, step % rows, 0))


def local_call(body, out_shapes, scratch, flops, moved_bytes, *args, stay=None):
    return pl.pallas_call(
        body,
        out_shape=list(out_shapes),
        in_specs=[
            pl.BlockSpec(
                memory_space=pltpu.HBM if k == stay else pltpu.SMEM if a.ndim == 1 else pltpu.VMEM
            )
            for k, a in enumerate(args)
        ],
        out_specs=[pl.BlockSpec(memory_space=pltpu.VMEM)] * len(out_shapes),
        scratch_shapes=scratch,
        cost_estimate=pl.CostEstimate(flops=flops, bytes_accessed=moved_bytes, transcendentals=0),
        compiler_params=pltpu.CompilerParams(vmem_limit_bytes=VMEM_LIMIT if stay is None else VMEM_MORE),
    )(*args)


def pack_kernel(saved_ref, cotangent_ref, weight_ref, later_ref, out_ref):
    del later_ref
    rows, inner = saved_ref.shape
    out_ref[:rows] = saved_ref[...]
    out_ref[rows : 2 * rows] = cotangent_ref[...]
    spare = CLASS_ROWS - weight_ref.shape[0]
    out_ref[2 * rows :] = jnp.concatenate(
        [weight_ref[...].astype(jnp.float32), jnp.zeros((spare, inner), jnp.float32)], axis=0
    ).astype(jnp.bfloat16)


def class_kernel(gathered_ref, own_ref, label_ref, grad_ref, even_ref, odd_ref, aux_ref):
    side = lax.rem(lax.axis_index("gx"), 2)
    groups, rows, inner = gathered_ref.shape[0], own_ref.shape[0], own_ref.shape[1]
    logits = jnp.zeros((CLASS_ROWS, rows), jnp.float32)
    for c in range(groups):
        weight = gathered_ref[c, 2 * rows : 2 * rows + CLASS_ROWS]
        logits += dot_nt(weight, jnp.maximum(gathered_ref[c, :rows], 0))
    place = lax.broadcasted_iota(jnp.int32, logits.shape, 0)
    real = place < CLASSES
    logits = jnp.where(real, logits, -jnp.inf)
    powers = jnp.exp(logits - jnp.max(logits, axis=0, keepdims=True))
    probabilities = powers / jnp.sum(powers, axis=0, keepdims=True)
    labels = jnp.concatenate(
        [
            label_ref[d, h : h + 1]
            for d in range(label_ref.shape[0])
            for h in range(label_ref.shape[1])
        ],
        axis=1,
    )
    onehot = jnp.where(place == labels, 1.0, 0.0)
    logit_grad = jnp.where(real, probabilities - onehot, 0.0).astype(jnp.bfloat16)
    for c in range(groups):
        weight = gathered_ref[c, 2 * rows : 2 * rows + CLASS_ROWS]
        total = gathered_ref[c, rows : 2 * rows].astype(jnp.float32) + dot_tn(logit_grad, weight)
        active = gathered_ref[c, :rows].astype(jnp.float32) > 0
        grad_ref[:, c * inner : (c + 1) * inner] = jnp.where(active, total, 0.0).astype(jnp.bfloat16)
    size = even_ref.shape[0]
    first = pl.multiple_of((rows - size) * side, size)
    even_ref[...] = grad_ref[pl.ds(rows - size - first, size)]
    odd_ref[...] = grad_ref[pl.ds(first, size)]
    aux_ref[...] = dot_nn(logit_grad, jnp.maximum(own_ref[...], 0)).astype(jnp.bfloat16)


def conv_kernel(
    grad_ref,
    even_x_ref,
    odd_x_ref,
    even_y_ref,
    odd_y_ref,
    input_ref,
    edge_ref,
    weight_ref,
    far_ref,
    out_ref,
    part_ref,
    send_ref,
    acc_ref,
    pool_ref,
):
    far_d, far_h, width, full = far_ref.shape
    depth, height = far_d - 2, far_h - 2
    inner = out_ref.shape[1]
    rows = depth * height * width
    side_x, side_y = (lax.rem(lax.axis_index(a), 2) for a in ("gx", "gy"))
    far_ref[1 : 1 + depth, 1 : 1 + height] = grad_ref[...].reshape(depth, height, width, full)
    far_ref[(far_d - 1) * (1 - side_x), 1 : 1 + height] = even_x_ref[...].reshape(height, width, full)
    far_ref[(far_d - 1) * side_x, 1 : 1 + height] = odd_x_ref[...].reshape(height, width, full)
    far_ref[:, (far_h - 1) * (1 - side_y)] = even_y_ref[...]
    far_ref[:, (far_h - 1) * side_y] = odd_y_ref[...]
    sent = far_d // 2
    send_ref[: sent * far_h * width] = far_ref[pl.ds(sent * side_x, sent)].reshape(-1, full)
    piece_rows = rows * inner // full
    for c in range(full // inner):
        send_ref[sent * far_h * width :, c * inner : (c + 1) * inner] = input_ref[
            c * piece_rows : (c + 1) * piece_rows
        ]
    total = jnp.zeros((rows, inner), jnp.float32)
    terms = [total] * 3
    for a in STEPS:
        for b in STEPS:
            piece = far_ref[1 - a : 1 - a + depth, 1 - b : 1 - b + height].reshape(rows, full)
            for c in STEPS:
                tap = 9 * (a + 1) + 3 * (b + 1) + c + 1
                terms[c + 1] += dot_nt(piece, weight_ref[:, tap * full : (tap + 1) * full])
    for c in STEPS:
        total += moved(terms[c + 1], c, width)
    out_ref[...] = total.astype(jnp.bfloat16)

    half_d, half_h, half_w = depth // 2, height // 2, width // 2
    nc = part_ref.shape[0]
    block = half_w // nc
    cells = part_ref.shape[1] - edge_ref.shape[1]
    window = cells // (half_d * half_h)
    pool_ref[...] = jnp.zeros_like(pool_ref)
    lines = total.reshape(depth, height, width, inner)
    for d in range(half_d):
        for h in range(half_h):
            acc_ref[...] = (
                lines[2 * d, 2 * h]
                + lines[2 * d, 2 * h + 1]
                + lines[2 * d + 1, 2 * h]
                + lines[2 * d + 1, 2 * h + 1]
            )
            pool_ref[d, h, 8 : 8 + half_w] = (
                acc_ref[pl.ds(0, half_w, stride=2)] + acc_ref[pl.ds(1, half_w, stride=2)]
            )
    for c in range(nc):
        start = 7 + c * block
        part_ref[c, cells:] = edge_ref[c]
        part_ref[c, :cells] = jnp.concatenate(
            [pool_ref[d, h, start : start + window] for d in range(half_d) for h in range(half_h)],
            axis=0,
        ).astype(jnp.bfloat16)


def kernel_grad_kernel(chunk, far_ref, input_ref, got_ref, *refs):
    out_refs, (all_ref, flat_ref, pair_ref, turn_ref, wide_ref) = refs[:-5], refs[-5:]
    far_d, far_h, width, full = far_ref.shape
    depth, height = far_d - 2, far_h - 2
    rows, inner = input_ref.shape
    by_height, by_depth, window, _ = all_ref.shape
    lanes = height * width
    side, at_y = lax.rem(lax.axis_index("gx"), 2), lax.axis_index("gy")
    sent = far_d // 2
    pair_ref[pl.ds(depth * side, far_d)] = far_ref[...]
    pair_ref[pl.ds(far_d * (1 - side), depth)] = got_ref[: sent * far_h * width].reshape(
        sent, far_h, width, full
    )
    piece_rows = rows * inner // full
    other = jnp.concatenate(
        [
            got_ref[sent * far_h * width :, c * inner : (c + 1) * inner]
            for c in range(full // inner)
        ],
        axis=0,
    )
    for c in STEPS:
        wide_ref[c + 1, side] = moved(input_ref[...].astype(jnp.float32), -c, width).astype(jnp.bfloat16)
        wide_ref[c + 1, 1 - side] = moved(other.astype(jnp.float32), -c, width).astype(jnp.bfloat16)
    for d in range(far_d + depth):
        for b in range(3):
            turn_ref[d, b] = pair_ref[d, b : b + height].reshape(lanes, full).T
    span = chunk * by_height
    grain = 16
    for m in range(by_depth):
        begin = span * (2 * m + side)
        for step in range((span - 1) // full + 2):
            tap = begin // full + step

            @pl.when(tap * full < begin + span)
            def _():
                a, b, c = tap // 9, lax.rem(tap // 3, 3), lax.rem(tap, 3)
                turned = jnp.concatenate([turn_ref[2 - a + d, 2 - b] for d in range(2 * depth)], axis=1)
                terms = dot_nn(turned, wide_ref[c].reshape(2 * rows, inner))
                first = pl.multiple_of(tap * full - begin + full, grain)
                flat_ref[m, pl.ds(first, full)] = terms.astype(jnp.bfloat16)

        for j in range(by_height):
            start = full + j * chunk // grain * grain
            all_ref[j, m] = flat_ref[m, start : start + window]
    for k, out_ref in enumerate(out_refs):
        out_ref[...] = all_ref[pl.ds(2 * (at_y // 2 ^ k), 2)]


def bottom_kernel(
    down_ref, up_ref, before_ref, pre_ref, after_ref, weight_ref, part_ref, shift_ref
):
    _, far_d, far_w, height, filters = shift_ref.shape
    depth, width = far_d - 2, far_w - 2
    rows = depth * width * height
    channels = part_ref.shape[1]
    back = dot_nt(down_ref[...], up_ref[...])
    saved = jnp.concatenate([before_ref[...], pre_ref[...], after_ref[...]], axis=1)
    saved = saved.reshape(depth * far_w * height, filters)
    grad = jnp.where(saved.astype(jnp.float32) > 0, back, 0.0)
    shift_ref[:, :1] = jnp.zeros((3, 1) + shift_ref.shape[2:], jnp.bfloat16)
    shift_ref[:, far_d - 1 :] = jnp.zeros((3, 1) + shift_ref.shape[2:], jnp.bfloat16)
    for b in STEPS:
        shift_ref[b + 1, 1 : 1 + depth] = (
            moved(grad, b, height).astype(jnp.bfloat16).reshape(depth, far_w, height, filters)
        )
    total = jnp.zeros((rows, channels), jnp.float32)
    for a in STEPS:
        for b in STEPS:
            tap = 9 * (a + 1) + 3 * (b + 1)
            piece = jnp.concatenate(
                [
                    shift_ref[b + 1, 1 - a : 1 - a + depth, 1 - c : 1 - c + width].reshape(rows, filters)
                    for c in STEPS
                ],
                axis=1,
            )
            weight = jnp.concatenate([weight_ref[tap + c] for c in range(3)], axis=1)
            total += dot_nt(piece, weight)
    part_ref[...] = total.astype(jnp.bfloat16)


def bottom_weight_kernel(down_ref, pre_ref, source_ref, shift_ref, both_ref):
    _, far_d, far_w, height, filters = shift_ref.shape
    depth, width = far_d - 2, far_w - 2
    rows, channels = source_ref.shape
    groups = both_ref.shape[0]
    thin = channels // groups
    full = down_ref.shape[1]
    inner = full // groups
    own_down = down_ref[...].reshape(depth, far_w, height, full)[:, 1 : 1 + width].reshape(rows, full)
    own_saved = pre_ref[...].reshape(rows, filters)
    up_part = dot_tn(jnp.maximum(own_saved, 0), own_down).astype(jnp.bfloat16)
    for cc in range(groups):
        both_ref[cc, TAPS * thin :] = up_part[:, cc * inner : (cc + 1) * inner]
    turned = source_ref[...].T
    for a in STEPS:
        for b in STEPS:
            tap = 9 * (a + 1) + 3 * (b + 1)
            piece = jnp.concatenate(
                [
                    shift_ref[b + 1, 1 - a : 1 - a + depth, 1 - c : 1 - c + width].reshape(rows, filters)
                    for c in STEPS
                ],
                axis=1,
            )
            terms = dot_nn(turned, piece).astype(jnp.bfloat16)
            for c in range(3):
                for cc in range(groups):
                    both_ref[cc, (tap + c) * thin : (tap + c + 1) * thin] = terms[
                        cc * thin : (cc + 1) * thin, c * filters : (c + 1) * filters
                    ]


def per_device(
    pre_bottom,
    bottom_input,
    bottom_weight,
    up_weight,
    level_input,
    pre_level,
    level_cotangent,
    labels,
    level_weight,
    aux_weight,
):
    nx, ny, nc = (lax.axis_size(a) for a in ("gx", "gy", "col"))
    at_x, at_y, at_c = (lax.axis_index(a) for a in ("gx", "gy", "col"))
    depth, height, width, inner = level_input.shape
    full = inner * nc
    rows = depth * height * width
    far_d, far_h = depth + 2, height + 2
    half_d, half_h, half_w = depth // 2, height // 2, width // 2
    block = half_w // nc
    wide = block + 2
    bottom_d, bottom_h, _, filters = pre_bottom.shape
    bf16, f32 = jnp.bfloat16, jnp.float32
    struct = jax.ShapeDtypeStruct

    own_pre = pre_level.reshape(rows, inner)
    (payload,) = local_call(
        pack_kernel,
        [struct((2 * rows + CLASS_ROWS, inner), bf16)],
        [],
        0,
        2 * pre_level.size,
        own_pre,
        level_cotangent.reshape(rows, inner),
        aux_weight.T,
        level_weight,
        stay=3,
    )
    gathered = lax.all_gather(payload, "col")
    lanes = height * width
    side_x, side_y = at_x % 2, at_y % 2
    level_pre_grad, even_x, odd_x, aux_part = local_call(
        class_kernel,
        (
            struct((rows, full), bf16),
            struct((lanes, full), bf16),
            struct((lanes, full), bf16),
            struct((CLASS_ROWS, inner), bf16),
        ),
        [],
        6 * rows * full * CLASS_ROWS,
        2 * gathered.size,
        gathered,
        own_pre,
        labels,
    )

    even_x = swap(even_x, "gx", 1)
    odd_x = swap_odd(odd_x, "gx")

    def lines(start):
        take = lambda x: x[start : start + width]
        before = jnp.where(side_x == 1, take(even_x), take(odd_x))
        after = jnp.where(side_x == 1, take(odd_x), take(even_x))
        own = level_pre_grad.reshape(depth, lanes, full)
        return jnp.stack([before] + [take(own[d]) for d in range(depth)] + [after])

    first, last = lines(0), lines(lanes - width)
    even_y = swap(jnp.where(side_y == 1, first, last), "gy", 1)
    odd_y = swap_odd(jnp.where(side_y == 1, last, first), "gy")

    turned_pre = pre_bottom.transpose(0, 2, 1, 3)
    edges = jnp.stack(
        [
            jnp.where(at_c < c, turned_pre[:, -1], turned_pre[:, 0]).reshape(-1, filters)
            for c in range(nc)
        ]
    )

    window = (wide + 7) // 8 * 8
    cells = half_d * half_h * window
    flat_input = level_input.reshape(rows, inner)
    far, level_input_grad, parts, send = local_call(
        conv_kernel,
        (
            struct((far_d, far_h, width, full), bf16),
            struct((rows, inner), bf16),
            struct((nc, cells + edges.shape[1], inner), bf16),
            struct((far_d // 2 * far_h * width + rows * inner // full, full), bf16),
        ),
        [
            pltpu.VMEM((width, inner), f32),
            pltpu.VMEM((half_d, half_h, half_w + 24, inner), f32),
        ],
        2 * rows * full * TAPS * inner,
        2 * level_weight.size,
        level_pre_grad,
        even_x,
        odd_x,
        even_y,
        odd_y,
        flat_input,
        edges,
        level_weight,
    )
    got = swap(send, "gx", 1)
    level_input_grad = level_input_grad.reshape(level_input.shape)

    relayed = exchange(parts, "col")
    edges = relayed[:, cells:].reshape(nc, bottom_d, 1, bottom_h, filters)
    relayed = relayed[:, :cells].reshape(nc * cells, inner)

    def edge_of(c):
        found = lax.dynamic_index_in_dim(edges, jnp.clip(c, 0, nc - 1), 0, keepdims=False)
        return jnp.where((c >= 0) & (c < nc), found, jnp.zeros_like(found))

    pre_before, pre_after = edge_of(at_c - 1), edge_of(at_c + 1)

    chunk = TAPS * full // (nx * ny)
    span = chunk + 8 if chunk % 16 else chunk
    level_parts = local_call(
        functools.partial(kernel_grad_kernel, chunk),
        [struct((2, nx // 2, span, inner), bf16)] * (ny // 2),
        [
            pltpu.VMEM((ny, nx // 2, span, inner), bf16),
            pltpu.VMEM((nx // 2, (chunk * ny - 1) // full * full + 4 * full, inner), bf16),
            pltpu.VMEM((far_d + depth, far_h, width, full), bf16),
            pltpu.VMEM((far_d + depth, 3, full, lanes), bf16),
            pltpu.VMEM((3, 2, rows, inner), bf16),
        ],
        2 * rows * full * TAPS * inner,
        2 * nx * ny * span * inner,
        far,
        flat_input,
        got,
    )
    terms = [level_parts[0]] + [swap(level_parts[k], "gy", 2 * k) for k in range(1, ny // 2)]

    by_depth = spread(jnp.concatenate([relayed, aux_part]), "gx")
    aux_sum = by_depth[:, nc * cells :].astype(f32).sum(axis=0).astype(bf16)
    by_depth = behind(by_depth, level_parts[0])
    line = by_depth[:, : nc * cells].reshape(nx, nc, half_d * half_h, window, inner)[:, :, :, :wide]
    split = nx * nc * half_d * half_h * wide
    by_height = spread(jnp.concatenate([line.reshape(split, inner), aux_sum]), "gy")
    aux_weight_grad = by_height[:, split : split + CLASSES].astype(f32).sum(axis=0).T
    down_wide = (
        by_height[:, :split]
        .reshape(ny, nx, nc, half_d, half_h, wide, inner)
        .transpose(1, 3, 5, 0, 4, 2, 6)
        .reshape(bottom_d * wide * bottom_h, full)
    )

    down_wide = behind(down_wide, terms[1], terms[-1])
    level_part = sum(t.astype(f32) for t in terms)
    level_part = summed_by_pairs(level_part, "gy", [1], [1])

    bottom_rows = bottom_d * block * bottom_h
    channel_width = bottom_weight.shape[0]
    thin = channel_width // nc
    part, shifts = local_call(
        bottom_kernel,
        (
            struct((bottom_rows, channel_width), bf16),
            struct((3, bottom_d + 2, wide, bottom_h, filters), bf16),
        ),
        [],
        2 * bottom_rows * channel_width * TAPS * filters,
        2 * bottom_weight.size,
        down_wide,
        up_weight,
        pre_before,
        turned_pre,
        pre_after,
        bottom_weight.transpose(1, 0, 2),
    )
    (both,) = local_call(
        bottom_weight_kernel,
        [struct((nc, TAPS * thin + filters, inner), bf16)],
        [],
        2 * bottom_rows * channel_width * TAPS * filters,
        2 * bottom_weight.size,
        down_wide,
        turned_pre,
        bottom_input.transpose(0, 2, 1, 3).reshape(bottom_rows, channel_width),
        shifts,
    )
    part = exchange(part.reshape(ny, bottom_rows // ny, channel_width), "gy")
    level_part = summed_by_pairs(level_part, "gx", bits_of("gx")[:-1], bits_of("gx")[-2::-1], part)
    if span != chunk:
        odd = lax.rem(at_y + at_x * ny, 2)
        level_part = jnp.where(odd == 1, level_part[span - chunk :], level_part[:chunk])
    level_weight_grad = level_part.T
    share = bottom_d // ny
    bottom_input_grad = (
        part.astype(f32)
        .sum(axis=0)
        .astype(bf16)
        .reshape(share, block, bottom_h, channel_width)
        .transpose(0, 2, 1, 3)
    )
    both = summed_by_pairs(behind(both, part), "col", bits_of("col"), bits_of("col")[::-1])
    bottom_weight_grad = both[: TAPS * thin].reshape(TAPS, thin, filters).transpose(1, 0, 2)
    up_weight_grad = both[TAPS * thin :]
    return (
        level_input_grad,
        bottom_input_grad,
        level_weight_grad,
        bottom_weight_grad,
        up_weight_grad,
        aux_weight_grad,
    )


def solution(mesh):
    return jax.shard_map(
        per_device,
        mesh=mesh,
        in_specs=(
            P(None, None, "col", "gy"),
            P(None, None, "col", "gx"),
            P("gx", None, "gy"),
            P("gy", None),
            P("gx", "gy", None, "col"),
            P("gx", "gy", None, "col"),
            P("gx", "gy", None, "col"),
            P("gx", "gy", None),
            P("col", None),
            P("col", None),
        ),
        out_specs=(
            P("gx", "gy", None, "col"),
            P("gy", None, "col", "gx"),
            P("col", ("gx", "gy")),
            P(("gx", "col"), None, "gy"),
            P("gy", "col"),
            P("col", None),
        ),
        check_vma=False,
    )
```

```python
import functools

import jax
import jax.numpy as jnp
from jax import lax
from jax.experimental import pallas as pl
from jax.experimental.pallas import tpu as pltpu
from jax.sharding import PartitionSpec as P

CLASSES = 14
CLASS_ROWS = 16
TAPS = 27
VMEM_LIMIT = 24 * 1024 * 1024
VMEM_MORE = 60 * 1024 * 1024
STEPS = (-1, 0, 1)
HALVES = ((0, (0, 3)), (0, (1, 2)), (1, (0, 1)), (1, (3, 2)))


def exchange(x, axis):
    return lax.all_to_all(x, axis, split_axis=0, concat_axis=0, tiled=False)


def spread(x, axis):
    size = lax.axis_size(axis)
    return exchange(jnp.broadcast_to(x[None], (size,) + x.shape), axis)


def behind(x, *others):
    return lax.optimization_barrier((x,) + others)[0]


def bits_of(axis):
    return [1 << k for k in reversed(range(lax.axis_size(axis).bit_length() - 1))]


def swap(x, axis, bit):
    return lax.ppermute(x, axis, [(i, i ^ bit) for i in range(lax.axis_size(axis))])


def swap_odd(x, axis):
    last = lax.axis_size(axis) - 1
    return lax.ppermute(
        x, axis, [(i, i + 1 if i % 2 else i - 1) for i in range(1, last)]
    )


def mine_and_other(x, axis, bit, dim):
    own = lax.axis_index(axis) // bit % 2
    take = functools.partial(lax.dynamic_index_in_dim, x, axis=dim, keepdims=False)
    return take(own), take(1 - own)


def summed_by_pairs(x, axis, bits, order, first=None):
    x = x.reshape((2,) * len(bits) + x.shape[1:])
    left = list(bits)
    for bit in order:
        if bit == order[-1] and first is not None:
            x = behind(x, first)
        own, other = mine_and_other(x, axis, bit, left.index(bit))
        left.remove(bit)
        x = own.astype(jnp.float32) + swap(other.astype(jnp.bfloat16), axis, bit).astype(jnp.float32)
    return x


def dot_nn(a, b):
    return lax.dot_general(a, b, (((1,), (0,)), ((), ())), preferred_element_type=jnp.float32)


def dot_tn(a, b):
    return lax.dot_general(a, b, (((0,), (0,)), ((), ())), preferred_element_type=jnp.float32)


def dot_nt(a, b):
    return lax.dot_general(a, b, (((1,), (1,)), ((), ())), preferred_element_type=jnp.float32)


def moved(x, step, period):
    if step == 0:
        return x
    rows = x.shape[0]
    place = lax.rem(lax.broadcasted_iota(jnp.int32, x.shape, 0), period)
    edge = 0 if step == 1 else period - 1
    return jnp.where(place == edge, 0.0, pltpu.roll(x, step % rows, 0))


def local_call(body, out_shapes, scratch, flops, moved_bytes, *args, stay=None):
    return pl.pallas_call(
        body,
        out_shape=list(out_shapes),
        in_specs=[
            pl.BlockSpec(
                memory_space=pltpu.HBM if stay is not None and k >= stay else pltpu.SMEM if a.ndim == 1 else pltpu.VMEM
            )
            for k, a in enumerate(args)
        ],
        out_specs=[pl.BlockSpec(memory_space=pltpu.VMEM)] * len(out_shapes),
        scratch_shapes=scratch,
        cost_estimate=pl.CostEstimate(flops=flops, bytes_accessed=moved_bytes, transcendentals=0),
        compiler_params=pltpu.CompilerParams(vmem_limit_bytes=VMEM_LIMIT if stay is None else VMEM_MORE),
    )(*args)


def pack_kernel(saved_ref, cotangent_ref, weight_ref, *refs):
    out_ref = refs[-1]
    rows, inner = saved_ref.shape
    out_ref[:rows] = saved_ref[...]
    out_ref[rows : 2 * rows] = cotangent_ref[...]
    spare = CLASS_ROWS - weight_ref.shape[0]
    out_ref[2 * rows :] = jnp.concatenate(
        [weight_ref[...].astype(jnp.float32), jnp.zeros((spare, inner), jnp.float32)], axis=0
    ).astype(jnp.bfloat16)


def class_kernel(gathered_ref, own_ref, label_ref, grad_ref, even_ref, odd_ref, aux_ref):
    side = lax.rem(lax.axis_index("gx"), 2)
    groups, rows, inner = gathered_ref.shape[0], own_ref.shape[0], own_ref.shape[1]
    logits = jnp.zeros((CLASS_ROWS, rows), jnp.float32)
    for c in range(groups):
        weight = gathered_ref[c, 2 * rows : 2 * rows + CLASS_ROWS]
        logits += dot_nt(weight, jnp.maximum(gathered_ref[c, :rows], 0))
    place = lax.broadcasted_iota(jnp.int32, logits.shape, 0)
    real = place < CLASSES
    logits = jnp.where(real, logits, -jnp.inf)
    powers = jnp.exp(logits - jnp.max(logits, axis=0, keepdims=True))
    probabilities = powers / jnp.sum(powers, axis=0, keepdims=True)
    labels = jnp.concatenate(
        [
            label_ref[d, h : h + 1]
            for d in range(label_ref.shape[0])
            for h in range(label_ref.shape[1])
        ],
        axis=1,
    )
    onehot = jnp.where(place == labels, 1.0, 0.0)
    logit_grad = jnp.where(real, probabilities - onehot, 0.0).astype(jnp.bfloat16)
    for c in range(groups):
        weight = gathered_ref[c, 2 * rows : 2 * rows + CLASS_ROWS]
        total = gathered_ref[c, rows : 2 * rows].astype(jnp.float32) + dot_tn(logit_grad, weight)
        active = gathered_ref[c, :rows].astype(jnp.float32) > 0
        grad_ref[:, c * inner : (c + 1) * inner] = jnp.where(active, total, 0.0).astype(jnp.bfloat16)
    size = even_ref.shape[0]
    first = pl.multiple_of((rows - size) * side, size)
    even_ref[...] = grad_ref[pl.ds(rows - size - first, size)]
    odd_ref[...] = grad_ref[pl.ds(first, size)]
    aux_ref[...] = dot_nn(logit_grad, jnp.maximum(own_ref[...], 0)).astype(jnp.bfloat16)


def conv_kernel(
    grad_ref,
    even_x_ref,
    odd_x_ref,
    even_y_ref,
    odd_y_ref,
    input_ref,
    edge_ref,
    weight_ref,
    far_ref,
    out_ref,
    part_ref,
    send_ref,
    acc_ref,
    pool_ref,
):
    far_d, far_h, width, full = far_ref.shape
    depth, height = far_d - 2, far_h - 2
    inner = out_ref.shape[1]
    rows = depth * height * width
    side_x, side_y = (lax.rem(lax.axis_index(a), 2) for a in ("gx", "gy"))
    far_ref[1 : 1 + depth, 1 : 1 + height] = grad_ref[...].reshape(depth, height, width, full)
    far_ref[(far_d - 1) * (1 - side_x), 1 : 1 + height] = even_x_ref[...].reshape(height, width, full)
    far_ref[(far_d - 1) * side_x, 1 : 1 + height] = odd_x_ref[...].reshape(height, width, full)
    far_ref[:, (far_h - 1) * (1 - side_y)] = even_y_ref[...]
    far_ref[:, (far_h - 1) * side_y] = odd_y_ref[...]
    sent = far_d // 2
    send_ref[: sent * far_h * width] = far_ref[pl.ds(sent * side_x, sent)].reshape(-1, full)
    piece_rows = rows * inner // full
    for c in range(full // inner):
        send_ref[sent * far_h * width :, c * inner : (c + 1) * inner] = input_ref[
            c * piece_rows : (c + 1) * piece_rows
        ]
    total = jnp.zeros((rows, inner), jnp.float32)
    terms = [total] * 3
    for a in STEPS:
        for b in STEPS:
            piece = far_ref[1 - a : 1 - a + depth, 1 - b : 1 - b + height].reshape(rows, full)
            for c in STEPS:
                tap = 9 * (a + 1) + 3 * (b + 1) + c + 1
                terms[c + 1] += dot_nt(piece, weight_ref[:, tap * full : (tap + 1) * full])
    for c in STEPS:
        total += moved(terms[c + 1], c, width)
    out_ref[...] = total.astype(jnp.bfloat16)

    half_d, half_h, half_w = depth // 2, height // 2, width // 2
    nc = part_ref.shape[0]
    block = half_w // nc
    cells = part_ref.shape[1] - edge_ref.shape[1]
    window = cells // (half_d * half_h)
    pool_ref[...] = jnp.zeros_like(pool_ref)
    lines = total.reshape(depth, height, width, inner)
    for d in range(half_d):
        for h in range(half_h):
            acc_ref[...] = (
                lines[2 * d, 2 * h]
                + lines[2 * d, 2 * h + 1]
                + lines[2 * d + 1, 2 * h]
                + lines[2 * d + 1, 2 * h + 1]
            )
            pool_ref[d, h, 8 : 8 + half_w] = (
                acc_ref[pl.ds(0, half_w, stride=2)] + acc_ref[pl.ds(1, half_w, stride=2)]
            )
    for c in range(nc):
        start = 7 + c * block
        part_ref[c, cells:] = edge_ref[c]
        part_ref[c, :cells] = jnp.concatenate(
            [pool_ref[d, h, start : start + window] for d in range(half_d) for h in range(half_h)],
            axis=0,
        ).astype(jnp.bfloat16)


def kernel_grad_kernel(chunk, far_ref, input_ref, got_ref, *refs):
    out_refs, (all_ref, flat_ref, pair_ref, turn_ref, wide_ref) = refs[:-5], refs[-5:]
    far_d, far_h, width, full = far_ref.shape
    depth, height = far_d - 2, far_h - 2
    rows, inner = input_ref.shape
    by_height, by_depth, window, _ = all_ref.shape
    lanes = height * width
    side, at_y = lax.rem(lax.axis_index("gx"), 2), lax.axis_index("gy")
    sent = far_d // 2
    pair_ref[pl.ds(depth * side, far_d)] = far_ref[...]
    pair_ref[pl.ds(far_d * (1 - side), depth)] = got_ref[: sent * far_h * width].reshape(
        sent, far_h, width, full
    )
    piece_rows = rows * inner // full
    other = jnp.concatenate(
        [
            got_ref[sent * far_h * width :, c * inner : (c + 1) * inner]
            for c in range(full // inner)
        ],
        axis=0,
    )
    for c in STEPS:
        wide_ref[c + 1, side] = moved(input_ref[...].astype(jnp.float32), -c, width).astype(jnp.bfloat16)
        wide_ref[c + 1, 1 - side] = moved(other.astype(jnp.float32), -c, width).astype(jnp.bfloat16)
    for d in range(far_d + depth):
        for b in range(3):
            turn_ref[d, b] = pair_ref[d, b : b + height].reshape(lanes, full).T
    span = chunk * by_height
    grain = 16
    for m in range(by_depth):
        begin = span * (2 * m + side)
        for step in range((span - 1) // full + 2):
            tap = begin // full + step

            @pl.when(tap * full < begin + span)
            def _():
                a, b, c = tap // 9, lax.rem(tap // 3, 3), lax.rem(tap, 3)
                turned = jnp.concatenate([turn_ref[2 - a + d, 2 - b] for d in range(2 * depth)], axis=1)
                terms = dot_nn(turned, wide_ref[c].reshape(2 * rows, inner))
                first = pl.multiple_of(tap * full - begin + full, grain)
                flat_ref[m, pl.ds(first, full)] = terms.astype(jnp.bfloat16)

        for j in range(by_height):
            start = full + j * chunk // grain * grain
            all_ref[j, m] = flat_ref[m, start : start + window]
    for (q, pairs), out_ref in zip(HALVES, out_refs):
        for slot, k in enumerate(pairs):
            out_ref[slot] = all_ref[2 * (at_y // 2 ^ k) + q]


def bottom_kernel(
    down_ref, up_ref, before_ref, pre_ref, after_ref, weight_ref, part_ref, shift_ref
):
    _, far_d, far_w, height, filters = shift_ref.shape
    depth, width = far_d - 2, far_w - 2
    rows = depth * width * height
    channels = part_ref.shape[1]
    back = dot_nt(down_ref[...], up_ref[...])
    saved = jnp.concatenate([before_ref[...], pre_ref[...], after_ref[...]], axis=1)
    saved = saved.reshape(depth * far_w * height, filters)
    grad = jnp.where(saved.astype(jnp.float32) > 0, back, 0.0)
    shift_ref[:, :1] = jnp.zeros((3, 1) + shift_ref.shape[2:], jnp.bfloat16)
    shift_ref[:, far_d - 1 :] = jnp.zeros((3, 1) + shift_ref.shape[2:], jnp.bfloat16)
    for b in STEPS:
        shift_ref[b + 1, 1 : 1 + depth] = (
            moved(grad, b, height).astype(jnp.bfloat16).reshape(depth, far_w, height, filters)
        )
    total = jnp.zeros((rows, channels), jnp.float32)
    for a in STEPS:
        for b in STEPS:
            tap = 9 * (a + 1) + 3 * (b + 1)
            piece = jnp.concatenate(
                [
                    shift_ref[b + 1, 1 - a : 1 - a + depth, 1 - c : 1 - c + width].reshape(rows, filters)
                    for c in STEPS
                ],
                axis=1,
            )
            weight = jnp.concatenate([weight_ref[tap + c] for c in range(3)], axis=1)
            total += dot_nt(piece, weight)
    part_ref[...] = total.astype(jnp.bfloat16)


def bottom_weight_kernel(down_ref, pre_ref, source_ref, shift_ref, both_ref):
    _, far_d, far_w, height, filters = shift_ref.shape
    depth, width = far_d - 2, far_w - 2
    rows, channels = source_ref.shape
    groups = both_ref.shape[0]
    thin = channels // groups
    full = down_ref.shape[1]
    inner = full // groups
    own_down = down_ref[...].reshape(depth, far_w, height, full)[:, 1 : 1 + width].reshape(rows, full)
    own_saved = pre_ref[...].reshape(rows, filters)
    up_part = dot_tn(jnp.maximum(own_saved, 0), own_down).astype(jnp.bfloat16)
    for cc in range(groups):
        both_ref[cc, TAPS * thin :] = up_part[:, cc * inner : (cc + 1) * inner]
    turned = source_ref[...].T
    for a in STEPS:
        for b in STEPS:
            tap = 9 * (a + 1) + 3 * (b + 1)
            piece = jnp.concatenate(
                [
                    shift_ref[b + 1, 1 - a : 1 - a + depth, 1 - c : 1 - c + width].reshape(rows, filters)
                    for c in STEPS
                ],
                axis=1,
            )
            terms = dot_nn(turned, piece).astype(jnp.bfloat16)
            for c in range(3):
                for cc in range(groups):
                    both_ref[cc, (tap + c) * thin : (tap + c + 1) * thin] = terms[
                        cc * thin : (cc + 1) * thin, c * filters : (c + 1) * filters
                    ]


def per_device(
    pre_bottom,
    bottom_input,
    bottom_weight,
    up_weight,
    level_input,
    pre_level,
    level_cotangent,
    labels,
    level_weight,
    aux_weight,
):
    nx, ny, nc = (lax.axis_size(a) for a in ("gx", "gy", "col"))
    at_x, at_y, at_c = (lax.axis_index(a) for a in ("gx", "gy", "col"))
    depth, height, width, inner = level_input.shape
    full = inner * nc
    rows = depth * height * width
    far_d, far_h = depth + 2, height + 2
    half_d, half_h, half_w = depth // 2, height // 2, width // 2
    block = half_w // nc
    wide = block + 2
    bottom_d, bottom_h, _, filters = pre_bottom.shape
    bf16, f32 = jnp.bfloat16, jnp.float32
    struct = jax.ShapeDtypeStruct

    own_pre = pre_level.reshape(rows, inner)
    (payload,) = local_call(
        pack_kernel,
        [struct((2 * rows + CLASS_ROWS, inner), bf16)],
        [],
        0,
        2 * pre_level.size,
        own_pre,
        level_cotangent.reshape(rows, inner),
        aux_weight.T,
        level_weight,
        level_input.reshape(rows, inner),
        up_weight,
        bottom_weight.transpose(1, 0, 2),
        stay=3,
    )
    gathered = lax.all_gather(payload, "col")
    lanes = height * width
    side_x, side_y = at_x % 2, at_y % 2
    level_pre_grad, even_x, odd_x, aux_part = local_call(
        class_kernel,
        (
            struct((rows, full), bf16),
            struct((lanes, full), bf16),
            struct((lanes, full), bf16),
            struct((CLASS_ROWS, inner), bf16),
        ),
        [],
        6 * rows * full * CLASS_ROWS,
        2 * gathered.size,
        gathered,
        own_pre,
        labels,
    )

    even_x = swap(even_x, "gx", 1)
    odd_x = swap_odd(odd_x, "gx")

    def lines(start):
        take = lambda x: x[start : start + width]
        before = jnp.where(side_x == 1, take(even_x), take(odd_x))
        after = jnp.where(side_x == 1, take(odd_x), take(even_x))
        own = level_pre_grad.reshape(depth, lanes, full)
        return jnp.stack([before] + [take(own[d]) for d in range(depth)] + [after])

    first, last = lines(0), lines(lanes - width)
    even_y = swap(jnp.where(side_y == 1, first, last), "gy", 1)
    odd_y = swap_odd(jnp.where(side_y == 1, last, first), "gy")

    turned_pre = pre_bottom.transpose(0, 2, 1, 3)
    edges = jnp.stack(
        [
            jnp.where(at_c < c, turned_pre[:, -1], turned_pre[:, 0]).reshape(-1, filters)
            for c in range(nc)
        ]
    )

    window = (wide + 7) // 8 * 8
    cells = half_d * half_h * window
    flat_input = level_input.reshape(rows, inner)
    far, level_input_grad, parts, send = local_call(
        conv_kernel,
        (
            struct((far_d, far_h, width, full), bf16),
            struct((rows, inner), bf16),
            struct((nc, cells + edges.shape[1], inner), bf16),
            struct((far_d // 2 * far_h * width + rows * inner // full, full), bf16),
        ),
        [
            pltpu.VMEM((width, inner), f32),
            pltpu.VMEM((half_d, half_h, half_w + 24, inner), f32),
        ],
        2 * rows * full * TAPS * inner,
        2 * level_weight.size,
        level_pre_grad,
        even_x,
        odd_x,
        even_y,
        odd_y,
        flat_input,
        edges,
        level_weight,
    )
    got = swap(send, "gx", 1)
    level_input_grad = level_input_grad.reshape(level_input.shape)

    relayed = exchange(parts, "col")
    edges = relayed[:, cells:].reshape(nc, bottom_d, 1, bottom_h, filters)
    relayed = relayed[:, :cells].reshape(nc * cells, inner)

    def edge_of(c):
        found = lax.dynamic_index_in_dim(edges, jnp.clip(c, 0, nc - 1), 0, keepdims=False)
        return jnp.where((c >= 0) & (c < nc), found, jnp.zeros_like(found))

    pre_before, pre_after = edge_of(at_c - 1), edge_of(at_c + 1)

    chunk = TAPS * full // (nx * ny)
    span = chunk + 8 if chunk % 16 else chunk
    level_parts = local_call(
        functools.partial(kernel_grad_kernel, chunk),
        [struct((2, nx // 2, span, inner), bf16)] * 4,
        [
            pltpu.VMEM((ny, nx // 2, span, inner), bf16),
            pltpu.VMEM((nx // 2, (chunk * ny - 1) // full * full + 4 * full, inner), bf16),
            pltpu.VMEM((far_d + depth, far_h, width, full), bf16),
            pltpu.VMEM((far_d + depth, 3, full, lanes), bf16),
            pltpu.VMEM((3, 2, rows, inner), bf16),
        ],
        2 * rows * full * TAPS * inner,
        2 * nx * ny * span * inner,
        far,
        flat_input,
        got,
    )
    def first_sum(kept, sent, bit):
        return kept.astype(f32) + swap(sent, "gy", bit).astype(f32)

    even_sum = first_sum(level_parts[0], level_parts[1], 2)
    odd_sum = first_sum(level_parts[2], level_parts[3], 6)
    relayed = behind(relayed, level_parts[0])

    by_depth = spread(jnp.concatenate([relayed, aux_part]), "gx")
    aux_sum = by_depth[:, nc * cells :].astype(f32).sum(axis=0).astype(bf16)
    by_depth = behind(by_depth, even_sum, odd_sum)
    line = by_depth[:, : nc * cells].reshape(nx, nc, half_d * half_h, window, inner)[:, :, :, :wide]
    split = nx * nc * half_d * half_h * wide
    by_height = spread(jnp.concatenate([line.reshape(split, inner), aux_sum]), "gy")
    aux_weight_grad = by_height[:, split : split + CLASSES].astype(f32).sum(axis=0).T
    down_wide = (
        by_height[:, :split]
        .reshape(ny, nx, nc, half_d, half_h, wide, inner)
        .transpose(1, 3, 5, 0, 4, 2, 6)
        .reshape(bottom_d * wide * bottom_h, full)
    )

    even_sum = first_sum(even_sum[0], even_sum[1].astype(bf16), 6)
    odd_sum = first_sum(odd_sum[0], odd_sum[1].astype(bf16), 2)
    level_part = summed_by_pairs(jnp.stack([even_sum, odd_sum]), "gy", [1], [1])
    down_wide = behind(down_wide, level_part)

    bottom_rows = bottom_d * block * bottom_h
    channel_width = bottom_weight.shape[0]
    thin = channel_width // nc
    part, shifts = local_call(
        bottom_kernel,
        (
            struct((bottom_rows, channel_width), bf16),
            struct((3, bottom_d + 2, wide, bottom_h, filters), bf16),
        ),
        [],
        2 * bottom_rows * channel_width * TAPS * filters,
        2 * bottom_weight.size,
        down_wide,
        up_weight,
        pre_before,
        turned_pre,
        pre_after,
        bottom_weight.transpose(1, 0, 2),
    )
    (both,) = local_call(
        bottom_weight_kernel,
        [struct((nc, TAPS * thin + filters, inner), bf16)],
        [],
        2 * bottom_rows * channel_width * TAPS * filters,
        2 * bottom_weight.size,
        down_wide,
        turned_pre,
        bottom_input.transpose(0, 2, 1, 3).reshape(bottom_rows, channel_width),
        shifts,
    )
    part = exchange(part.reshape(ny, bottom_rows // ny, channel_width), "gy")
    level_part = summed_by_pairs(level_part, "gx", bits_of("gx")[:-1], bits_of("gx")[-2::-1], part)
    if span != chunk:
        odd = lax.rem(at_y + at_x * ny, 2)
        level_part = jnp.where(odd == 1, level_part[span - chunk :], level_part[:chunk])
    level_weight_grad = level_part.T
    share = bottom_d // ny
    bottom_input_grad = (
        part.astype(f32)
        .sum(axis=0)
        .astype(bf16)
        .reshape(share, block, bottom_h, channel_width)
        .transpose(0, 2, 1, 3)
    )
    both = summed_by_pairs(behind(both, part), "col", bits_of("col"), bits_of("col")[::-1])
    bottom_weight_grad = both[: TAPS * thin].reshape(TAPS, thin, filters).transpose(1, 0, 2)
    up_weight_grad = both[TAPS * thin :]
    return (
        level_input_grad,
        bottom_input_grad,
        level_weight_grad,
        bottom_weight_grad,
        up_weight_grad,
        aux_weight_grad,
    )


def solution(mesh):
    return jax.shard_map(
        per_device,
        mesh=mesh,
        in_specs=(
            P(None, None, "col", "gy"),
            P(None, None, "col", "gx"),
            P("gx", None, "gy"),
            P("gy", None),
            P("gx", "gy", None, "col"),
            P("gx", "gy", None, "col"),
            P("gx", "gy", None, "col"),
            P("gx", "gy", None),
            P("col", None),
            P("col", None),
        ),
        out_specs=(
            P("gx", "gy", None, "col"),
            P("gy", None, "col", "gx"),
            P("col", ("gx", "gy")),
            P(("gx", "col"), None, "gy"),
            P("gy", "col"),
            P("col", None),
        ),
        check_vma=False,
    )
```

```python
import functools

import jax
import jax.numpy as jnp
from jax import lax
from jax.experimental import pallas as pl
from jax.experimental.pallas import tpu as pltpu
from jax.sharding import PartitionSpec as P

CLASSES = 14
CLASS_ROWS = 16
TAPS = 27
VMEM_LIMIT = 24 * 1024 * 1024
VMEM_MORE = 60 * 1024 * 1024
STEPS = (-1, 0, 1)
HALVES = ((0, (0, 3)), (0, (1, 2)), (1, (0, 1)), (1, (3, 2)))


def exchange(x, axis):
    return lax.all_to_all(x, axis, split_axis=0, concat_axis=0, tiled=False)


def spread(x, axis):
    size = lax.axis_size(axis)
    return exchange(jnp.broadcast_to(x[None], (size,) + x.shape), axis)


def behind(x, *others):
    return lax.optimization_barrier((x,) + others)[0]


def bits_of(axis):
    return [1 << k for k in reversed(range(lax.axis_size(axis).bit_length() - 1))]


def swap(x, axis, bit):
    return lax.ppermute(x, axis, [(i, i ^ bit) for i in range(lax.axis_size(axis))])


def swap_odd(x, axis):
    last = lax.axis_size(axis) - 1
    return lax.ppermute(
        x, axis, [(i, i + 1 if i % 2 else i - 1) for i in range(1, last)]
    )


def mine_and_other(x, axis, bit, dim):
    own = lax.axis_index(axis) // bit % 2
    take = functools.partial(lax.dynamic_index_in_dim, x, axis=dim, keepdims=False)
    return take(own), take(1 - own)


def summed_by_pairs(x, axis, bits, order, first=None):
    x = x.reshape((2,) * len(bits) + x.shape[1:])
    left = list(bits)
    for bit in order:
        if bit == order[-1] and first is not None:
            x = behind(x, first)
        own, other = mine_and_other(x, axis, bit, left.index(bit))
        left.remove(bit)
        x = own.astype(jnp.float32) + swap(other.astype(jnp.bfloat16), axis, bit).astype(jnp.float32)
    return x


def dot_nn(a, b):
    return lax.dot_general(a, b, (((1,), (0,)), ((), ())), preferred_element_type=jnp.float32)


def dot_tn(a, b):
    return lax.dot_general(a, b, (((0,), (0,)), ((), ())), preferred_element_type=jnp.float32)


def dot_nt(a, b):
    return lax.dot_general(a, b, (((1,), (1,)), ((), ())), preferred_element_type=jnp.float32)


def moved(x, step, period):
    if step == 0:
        return x
    rows = x.shape[0]
    place = lax.rem(lax.broadcasted_iota(jnp.int32, x.shape, 0), period)
    edge = 0 if step == 1 else period - 1
    return jnp.where(place == edge, 0.0, pltpu.roll(x, step % rows, 0))


def local_call(body, out_shapes, scratch, flops, moved_bytes, *args, stay=None):
    return pl.pallas_call(
        body,
        out_shape=list(out_shapes),
        in_specs=[
            pl.BlockSpec(
                memory_space=pltpu.HBM if stay is not None and k >= stay else pltpu.SMEM if a.ndim == 1 else pltpu.VMEM
            )
            for k, a in enumerate(args)
        ],
        out_specs=[pl.BlockSpec(memory_space=pltpu.VMEM)] * len(out_shapes),
        scratch_shapes=scratch,
        cost_estimate=pl.CostEstimate(flops=flops, bytes_accessed=moved_bytes, transcendentals=0),
        compiler_params=pltpu.CompilerParams(vmem_limit_bytes=VMEM_LIMIT if stay is None else VMEM_MORE),
    )(*args)


def pack_kernel(saved_ref, cotangent_ref, weight_ref, *refs):
    out_ref = refs[-1]
    rows, inner = saved_ref.shape
    out_ref[:rows] = saved_ref[...]
    out_ref[rows : 2 * rows] = cotangent_ref[...]
    spare = CLASS_ROWS - weight_ref.shape[0]
    out_ref[2 * rows :] = jnp.concatenate(
        [weight_ref[...].astype(jnp.float32), jnp.zeros((spare, inner), jnp.float32)], axis=0
    ).astype(jnp.bfloat16)


def class_kernel(gathered_ref, own_ref, label_ref, grad_ref, even_ref, odd_ref, aux_ref):
    side = lax.rem(lax.axis_index("gx"), 2)
    groups, rows, inner = gathered_ref.shape[0], own_ref.shape[0], own_ref.shape[1]
    logits = jnp.zeros((CLASS_ROWS, rows), jnp.float32)
    for c in range(groups):
        weight = gathered_ref[c, 2 * rows : 2 * rows + CLASS_ROWS]
        logits += dot_nt(weight, jnp.maximum(gathered_ref[c, :rows], 0))
    place = lax.broadcasted_iota(jnp.int32, logits.shape, 0)
    real = place < CLASSES
    logits = jnp.where(real, logits, -jnp.inf)
    powers = jnp.exp(logits - jnp.max(logits, axis=0, keepdims=True))
    probabilities = powers / jnp.sum(powers, axis=0, keepdims=True)
    labels = jnp.concatenate(
        [
            label_ref[d, h : h + 1]
            for d in range(label_ref.shape[0])
            for h in range(label_ref.shape[1])
        ],
        axis=1,
    )
    onehot = jnp.where(place == labels, 1.0, 0.0)
    logit_grad = jnp.where(real, probabilities - onehot, 0.0).astype(jnp.bfloat16)
    for c in range(groups):
        weight = gathered_ref[c, 2 * rows : 2 * rows + CLASS_ROWS]
        total = gathered_ref[c, rows : 2 * rows].astype(jnp.float32) + dot_tn(logit_grad, weight)
        active = gathered_ref[c, :rows].astype(jnp.float32) > 0
        grad_ref[:, c * inner : (c + 1) * inner] = jnp.where(active, total, 0.0).astype(jnp.bfloat16)
    size = even_ref.shape[0]
    first = pl.multiple_of((rows - size) * side, size)
    even_ref[...] = grad_ref[pl.ds(rows - size - first, size)]
    odd_ref[...] = grad_ref[pl.ds(first, size)]
    aux_ref[...] = dot_nn(logit_grad, jnp.maximum(own_ref[...], 0)).astype(jnp.bfloat16)


def conv_kernel(
    grad_ref,
    even_x_ref,
    odd_x_ref,
    even_y_ref,
    odd_y_ref,
    input_ref,
    edge_ref,
    weight_ref,
    far_ref,
    out_ref,
    part_ref,
    send_ref,
    acc_ref,
    pool_ref,
):
    far_d, far_h, width, full = far_ref.shape
    depth, height = far_d - 2, far_h - 2
    inner = out_ref.shape[1]
    rows = depth * height * width
    side_x, side_y = (lax.rem(lax.axis_index(a), 2) for a in ("gx", "gy"))
    far_ref[1 : 1 + depth, 1 : 1 + height] = grad_ref[...].reshape(depth, height, width, full)
    far_ref[(far_d - 1) * (1 - side_x), 1 : 1 + height] = even_x_ref[...].reshape(height, width, full)
    far_ref[(far_d - 1) * side_x, 1 : 1 + height] = odd_x_ref[...].reshape(height, width, full)
    far_ref[:, (far_h - 1) * (1 - side_y)] = even_y_ref[...]
    far_ref[:, (far_h - 1) * side_y] = odd_y_ref[...]
    sent = far_d // 2
    send_ref[: sent * far_h * width] = far_ref[pl.ds(sent * side_x, sent)].reshape(-1, full)
    piece_rows = rows * inner // full
    for c in range(full // inner):
        send_ref[sent * far_h * width :, c * inner : (c + 1) * inner] = input_ref[
            c * piece_rows : (c + 1) * piece_rows
        ]
    total = jnp.zeros((rows, inner), jnp.float32)
    terms = [total] * 3
    for a in STEPS:
        for b in STEPS:
            piece = far_ref[1 - a : 1 - a + depth, 1 - b : 1 - b + height].reshape(rows, full)
            for c in STEPS:
                tap = 9 * (a + 1) + 3 * (b + 1) + c + 1
                terms[c + 1] += dot_nt(piece, weight_ref[:, tap * full : (tap + 1) * full])
    for c in STEPS:
        total += moved(terms[c + 1], c, width)
    out_ref[...] = total.astype(jnp.bfloat16)

    half_d, half_h, half_w = depth // 2, height // 2, width // 2
    nc = part_ref.shape[0]
    block = half_w // nc
    cells = part_ref.shape[1] - edge_ref.shape[1]
    window = cells // (half_d * half_h)
    pool_ref[...] = jnp.zeros_like(pool_ref)
    lines = total.reshape(depth, height, width, inner)
    for d in range(half_d):
        for h in range(half_h):
            acc_ref[...] = (
                lines[2 * d, 2 * h]
                + lines[2 * d, 2 * h + 1]
                + lines[2 * d + 1, 2 * h]
                + lines[2 * d + 1, 2 * h + 1]
            )
            pool_ref[d, h, 8 : 8 + half_w] = (
                acc_ref[pl.ds(0, half_w, stride=2)] + acc_ref[pl.ds(1, half_w, stride=2)]
            )
    for c in range(nc):
        start = 7 + c * block
        part_ref[c, cells:] = edge_ref[c]
        part_ref[c, :cells] = jnp.concatenate(
            [pool_ref[d, h, start : start + window] for d in range(half_d) for h in range(half_h)],
            axis=0,
        ).astype(jnp.bfloat16)


def kernel_grad_kernel(chunk, far_ref, input_ref, got_ref, *refs):
    out_refs, (flat_ref, pair_ref, turn_ref, wide_ref) = refs[:-4], refs[-4:]
    far_d, far_h, width, full = far_ref.shape
    depth, height = far_d - 2, far_h - 2
    rows, inner = input_ref.shape
    by_height = lax.axis_size("gy")
    _, by_depth, window, _ = out_refs[0].shape
    lanes = height * width
    side, at_y = lax.rem(lax.axis_index("gx"), 2), lax.axis_index("gy")
    sent = far_d // 2
    pair_ref[pl.ds(depth * side, far_d)] = far_ref[...]
    pair_ref[pl.ds(far_d * (1 - side), depth)] = got_ref[: sent * far_h * width].reshape(
        sent, far_h, width, full
    )
    piece_rows = rows * inner // full
    other = jnp.concatenate(
        [
            got_ref[sent * far_h * width :, c * inner : (c + 1) * inner]
            for c in range(full // inner)
        ],
        axis=0,
    )
    for c in STEPS:
        wide_ref[c + 1, side] = moved(input_ref[...].astype(jnp.float32), -c, width).astype(jnp.bfloat16)
        wide_ref[c + 1, 1 - side] = moved(other.astype(jnp.float32), -c, width).astype(jnp.bfloat16)
    for d in range(far_d + depth):
        for b in range(3):
            turn_ref[d, b] = pair_ref[d, b : b + height].reshape(lanes, full).T
    span = chunk * by_height
    grain = 16
    for m in range(by_depth):
        begin = span * (2 * m + side)
        for step in range((span - 1) // full + 2):
            tap = begin // full + step

            @pl.when(tap * full < begin + span)
            def _():
                a, b, c = tap // 9, lax.rem(tap // 3, 3), lax.rem(tap, 3)
                turned = jnp.concatenate([turn_ref[2 - a + d, 2 - b] for d in range(2 * depth)], axis=1)
                terms = dot_nn(turned, wide_ref[c].reshape(2 * rows, inner))
                first = pl.multiple_of(tap * full - begin + full, grain)
                flat_ref[m, pl.ds(first, full)] = terms.astype(jnp.bfloat16)

        for (q, pairs), out_ref in zip(HALVES, out_refs):
            for slot, k in enumerate(pairs):
                owner = 2 * (at_y // 2 ^ k) + q
                start = pl.multiple_of(full + owner * chunk // grain * grain, grain)
                out_ref[slot, m] = flat_ref[m, pl.ds(start, window)]


def bottom_kernel(
    down_ref, up_ref, before_ref, pre_ref, after_ref, weight_ref, part_ref, shift_ref
):
    _, far_d, far_w, height, filters = shift_ref.shape
    depth, width = far_d - 2, far_w - 2
    rows = depth * width * height
    channels = part_ref.shape[1]
    back = dot_nt(down_ref[...], up_ref[...])
    saved = jnp.concatenate([before_ref[...], pre_ref[...], after_ref[...]], axis=1)
    saved = saved.reshape(depth * far_w * height, filters)
    grad = jnp.where(saved.astype(jnp.float32) > 0, back, 0.0)
    shift_ref[:, :1] = jnp.zeros((3, 1) + shift_ref.shape[2:], jnp.bfloat16)
    shift_ref[:, far_d - 1 :] = jnp.zeros((3, 1) + shift_ref.shape[2:], jnp.bfloat16)
    for b in STEPS:
        shift_ref[b + 1, 1 : 1 + depth] = (
            moved(grad, b, height).astype(jnp.bfloat16).reshape(depth, far_w, height, filters)
        )
    total = jnp.zeros((rows, channels), jnp.float32)
    for a in STEPS:
        for b in STEPS:
            tap = 9 * (a + 1) + 3 * (b + 1)
            piece = jnp.concatenate(
                [
                    shift_ref[b + 1, 1 - a : 1 - a + depth, 1 - c : 1 - c + width].reshape(rows, filters)
                    for c in STEPS
                ],
                axis=1,
            )
            weight = jnp.concatenate([weight_ref[tap + c] for c in range(3)], axis=1)
            total += dot_nt(piece, weight)
    part_ref[...] = total.astype(jnp.bfloat16)


def bottom_weight_kernel(down_ref, pre_ref, source_ref, shift_ref, *refs):
    out_refs, both_ref = refs[:-1], refs[-1]
    _, far_d, far_w, height, filters = shift_ref.shape
    depth, width = far_d - 2, far_w - 2
    rows, channels = source_ref.shape
    groups = both_ref.shape[0]
    thin = channels // groups
    full = down_ref.shape[1]
    inner = full // groups
    own_down = down_ref[...].reshape(depth, far_w, height, full)[:, 1 : 1 + width].reshape(rows, full)
    own_saved = pre_ref[...].reshape(rows, filters)
    up_part = dot_tn(jnp.maximum(own_saved, 0), own_down).astype(jnp.bfloat16)
    for cc in range(groups):
        both_ref[cc, TAPS * thin :] = up_part[:, cc * inner : (cc + 1) * inner]
    turned = source_ref[...].T
    for a in STEPS:
        for b in STEPS:
            tap = 9 * (a + 1) + 3 * (b + 1)
            piece = jnp.concatenate(
                [
                    shift_ref[b + 1, 1 - a : 1 - a + depth, 1 - c : 1 - c + width].reshape(rows, filters)
                    for c in STEPS
                ],
                axis=1,
            )
            terms = dot_nn(turned, piece).astype(jnp.bfloat16)
            for c in range(3):
                for cc in range(groups):
                    both_ref[cc, (tap + c) * thin : (tap + c + 1) * thin] = terms[
                        cc * thin : (cc + 1) * thin, c * filters : (c + 1) * filters
                    ]
    at_c = lax.axis_index("col")
    for k, out_ref in enumerate(out_refs):
        out_ref[...] = both_ref[at_c ^ k]


def per_device(
    pre_bottom,
    bottom_input,
    bottom_weight,
    up_weight,
    level_input,
    pre_level,
    level_cotangent,
    labels,
    level_weight,
    aux_weight,
):
    nx, ny, nc = (lax.axis_size(a) for a in ("gx", "gy", "col"))
    at_x, at_y, at_c = (lax.axis_index(a) for a in ("gx", "gy", "col"))
    depth, height, width, inner = level_input.shape
    full = inner * nc
    rows = depth * height * width
    far_d, far_h = depth + 2, height + 2
    half_d, half_h, half_w = depth // 2, height // 2, width // 2
    block = half_w // nc
    wide = block + 2
    bottom_d, bottom_h, _, filters = pre_bottom.shape
    bf16, f32 = jnp.bfloat16, jnp.float32
    struct = jax.ShapeDtypeStruct

    own_pre = pre_level.reshape(rows, inner)
    (payload,) = local_call(
        pack_kernel,
        [struct((2 * rows + CLASS_ROWS, inner), bf16)],
        [],
        0,
        2 * pre_level.size,
        own_pre,
        level_cotangent.reshape(rows, inner),
        aux_weight.T,
        level_weight,
        level_input.reshape(rows, inner),
        up_weight,
        bottom_weight.transpose(1, 0, 2),
        stay=3,
    )
    gathered = lax.all_gather(payload, "col")
    lanes = height * width
    side_x, side_y = at_x % 2, at_y % 2
    level_pre_grad, even_x, odd_x, aux_part = local_call(
        class_kernel,
        (
            struct((rows, full), bf16),
            struct((lanes, full), bf16),
            struct((lanes, full), bf16),
            struct((CLASS_ROWS, inner), bf16),
        ),
        [],
        6 * rows * full * CLASS_ROWS,
        2 * gathered.size,
        gathered,
        own_pre,
        labels,
    )

    even_x = swap(even_x, "gx", 1)
    odd_x = swap_odd(odd_x, "gx")

    def lines(start):
        take = lambda x: x[start : start + width]
        before = jnp.where(side_x == 1, take(even_x), take(odd_x))
        after = jnp.where(side_x == 1, take(odd_x), take(even_x))
        own = level_pre_grad.reshape(depth, lanes, full)
        return jnp.stack([before] + [take(own[d]) for d in range(depth)] + [after])

    first, last = lines(0), lines(lanes - width)
    even_y = swap(jnp.where(side_y == 1, first, last), "gy", 1)
    odd_y = swap_odd(jnp.where(side_y == 1, last, first), "gy")

    turned_pre = pre_bottom.transpose(0, 2, 1, 3)
    edges = jnp.stack(
        [
            jnp.where(at_c < c, turned_pre[:, -1], turned_pre[:, 0]).reshape(-1, filters)
            for c in range(nc)
        ]
    )

    window = (wide + 7) // 8 * 8
    cells = half_d * half_h * window
    flat_input = level_input.reshape(rows, inner)
    far, level_input_grad, parts, send = local_call(
        conv_kernel,
        (
            struct((far_d, far_h, width, full), bf16),
            struct((rows, inner), bf16),
            struct((nc, cells + edges.shape[1], inner), bf16),
            struct((far_d // 2 * far_h * width + rows * inner // full, full), bf16),
        ),
        [
            pltpu.VMEM((width, inner), f32),
            pltpu.VMEM((half_d, half_h, half_w + 24, inner), f32),
        ],
        2 * rows * full * TAPS * inner,
        2 * level_weight.size,
        level_pre_grad,
        even_x,
        odd_x,
        even_y,
        odd_y,
        flat_input,
        edges,
        level_weight,
    )
    got = swap(send, "gx", 1)
    level_input_grad = level_input_grad.reshape(level_input.shape)

    relayed = exchange(parts, "col")
    edges = relayed[:, cells:].reshape(nc, bottom_d, 1, bottom_h, filters)
    relayed = relayed[:, :cells].reshape(nc * cells, inner)

    def edge_of(c):
        found = lax.dynamic_index_in_dim(edges, jnp.clip(c, 0, nc - 1), 0, keepdims=False)
        return jnp.where((c >= 0) & (c < nc), found, jnp.zeros_like(found))

    pre_before, pre_after = edge_of(at_c - 1), edge_of(at_c + 1)

    chunk = TAPS * full // (nx * ny)
    span = chunk + 8 if chunk % 16 else chunk
    level_parts = local_call(
        functools.partial(kernel_grad_kernel, chunk),
        [struct((2, nx // 2, span, inner), bf16)] * 4,
        [
            pltpu.VMEM((nx // 2, (chunk * ny - 1) // full * full + 4 * full, inner), bf16),
            pltpu.VMEM((far_d + depth, far_h, width, full), bf16),
            pltpu.VMEM((far_d + depth, 3, full, lanes), bf16),
            pltpu.VMEM((3, 2, rows, inner), bf16),
        ],
        2 * rows * full * TAPS * inner,
        2 * nx * ny * span * inner,
        far,
        flat_input,
        got,
    )
    def first_sum(kept, sent, bit):
        return kept.astype(f32) + swap(sent, "gy", bit).astype(f32)

    even_sum = first_sum(level_parts[0], level_parts[1], 2)
    odd_sum = first_sum(level_parts[2], level_parts[3], 6)
    relayed = behind(relayed, level_parts[0])

    by_depth = spread(jnp.concatenate([relayed, aux_part]), "gx")
    aux_sum = by_depth[:, nc * cells :].astype(f32).sum(axis=0).astype(bf16)
    line = by_depth[:, : nc * cells].reshape(nx, nc, half_d * half_h, window, inner)[:, :, :, :wide]
    split = nx * nc * half_d * half_h * wide
    by_height = spread(jnp.concatenate([line.reshape(split, inner), aux_sum]), "gy")
    aux_weight_grad = by_height[:, split : split + CLASSES].astype(f32).sum(axis=0).T
    down_wide = (
        by_height[:, :split]
        .reshape(ny, nx, nc, half_d, half_h, wide, inner)
        .transpose(1, 3, 5, 0, 4, 2, 6)
        .reshape(bottom_d * wide * bottom_h, full)
    )

    even_sum = first_sum(even_sum[0], even_sum[1].astype(bf16), 6)
    odd_sum = first_sum(odd_sum[0], odd_sum[1].astype(bf16), 2)
    down_wide = behind(down_wide, even_sum, odd_sum)
    level_part = summed_by_pairs(jnp.stack([even_sum, odd_sum]), "gy", [1], [1])

    bottom_rows = bottom_d * block * bottom_h
    channel_width = bottom_weight.shape[0]
    thin = channel_width // nc
    part, shifts = local_call(
        bottom_kernel,
        (
            struct((bottom_rows, channel_width), bf16),
            struct((3, bottom_d + 2, wide, bottom_h, filters), bf16),
        ),
        [],
        2 * bottom_rows * channel_width * TAPS * filters,
        2 * bottom_weight.size,
        down_wide,
        up_weight,
        pre_before,
        turned_pre,
        pre_after,
        bottom_weight.transpose(1, 0, 2),
    )
    both = local_call(
        bottom_weight_kernel,
        [struct((TAPS * thin + filters, inner), bf16)] * nc,
        [pltpu.VMEM((nc, TAPS * thin + filters, inner), bf16)],
        2 * bottom_rows * channel_width * TAPS * filters,
        2 * bottom_weight.size,
        down_wide,
        turned_pre,
        bottom_input.transpose(0, 2, 1, 3).reshape(bottom_rows, channel_width),
        shifts,
    )
    part = exchange(part.reshape(ny, bottom_rows // ny, channel_width), "gy")
    level_part = summed_by_pairs(level_part, "gx", bits_of("gx")[:-1], bits_of("gx")[-2::-1], part)
    if span != chunk:
        odd = lax.rem(at_y + at_x * ny, 2)
        level_part = jnp.where(odd == 1, level_part[span - chunk :], level_part[:chunk])
    level_weight_grad = level_part.T
    share = bottom_d // ny
    bottom_input_grad = (
        part.astype(f32)
        .sum(axis=0)
        .astype(bf16)
        .reshape(share, block, bottom_h, channel_width)
        .transpose(0, 2, 1, 3)
    )
    both = sum(
        (both[k] if k == 0 else swap(both[k], "col", k)).astype(f32) for k in range(nc)
    )
    bottom_weight_grad = both[: TAPS * thin].reshape(TAPS, thin, filters).transpose(1, 0, 2)
    up_weight_grad = both[TAPS * thin :]
    return (
        level_input_grad,
        bottom_input_grad,
        level_weight_grad,
        bottom_weight_grad,
        up_weight_grad,
        aux_weight_grad,
    )


def solution(mesh):
    return jax.shard_map(
        per_device,
        mesh=mesh,
        in_specs=(
            P(None, None, "col", "gy"),
            P(None, None, "col", "gx"),
            P("gx", None, "gy"),
            P("gy", None),
            P("gx", "gy", None, "col"),
            P("gx", "gy", None, "col"),
            P("gx", "gy", None, "col"),
            P("gx", "gy", None),
            P("col", None),
            P("col", None),
        ),
        out_specs=(
            P("gx", "gy", None, "col"),
            P("gy", None, "col", "gx"),
            P("col", ("gx", "gy")),
            P(("gx", "col"), None, "gy"),
            P("gy", "col"),
            P("col", None),
        ),
        check_vma=False,
    )
```

```python
import functools

import jax
import jax.numpy as jnp
from jax import lax
from jax.experimental import pallas as pl
from jax.experimental.pallas import tpu as pltpu
from jax.sharding import PartitionSpec as P

CLASSES = 14
CLASS_ROWS = 16
TAPS = 27
VMEM_LIMIT = 24 * 1024 * 1024
VMEM_MORE = 60 * 1024 * 1024
STEPS = (-1, 0, 1)
HALVES = ((0, (0, 3)), (0, (1, 2)), (1, (0, 1)), (1, (3, 2)))


def exchange(x, axis):
    return lax.all_to_all(x, axis, split_axis=0, concat_axis=0, tiled=False)


def spread(x, axis):
    size = lax.axis_size(axis)
    return exchange(jnp.broadcast_to(x[None], (size,) + x.shape), axis)


def behind(x, *others):
    return lax.optimization_barrier((x,) + others)[0]


def bits_of(axis):
    return [1 << k for k in reversed(range(lax.axis_size(axis).bit_length() - 1))]


def swap(x, axis, bit):
    return lax.ppermute(x, axis, [(i, i ^ bit) for i in range(lax.axis_size(axis))])


def swap_odd(x, axis):
    last = lax.axis_size(axis) - 1
    return lax.ppermute(
        x, axis, [(i, i + 1 if i % 2 else i - 1) for i in range(1, last)]
    )


def mine_and_other(x, axis, bit, dim):
    own = lax.axis_index(axis) // bit % 2
    take = functools.partial(lax.dynamic_index_in_dim, x, axis=dim, keepdims=False)
    return take(own), take(1 - own)


def summed_by_pairs(x, axis, bits, order, first=None):
    x = x.reshape((2,) * len(bits) + x.shape[1:])
    left = list(bits)
    for bit in order:
        if bit == order[-1] and first is not None:
            x = behind(x, first)
        own, other = mine_and_other(x, axis, bit, left.index(bit))
        left.remove(bit)
        x = own.astype(jnp.float32) + swap(other.astype(jnp.bfloat16), axis, bit).astype(jnp.float32)
    return x


def dot_nn(a, b):
    return lax.dot_general(a, b, (((1,), (0,)), ((), ())), preferred_element_type=jnp.float32)


def dot_tn(a, b):
    return lax.dot_general(a, b, (((0,), (0,)), ((), ())), preferred_element_type=jnp.float32)


def dot_nt(a, b):
    return lax.dot_general(a, b, (((1,), (1,)), ((), ())), preferred_element_type=jnp.float32)


def moved(x, step, period):
    if step == 0:
        return x
    rows = x.shape[0]
    place = lax.rem(lax.broadcasted_iota(jnp.int32, x.shape, 0), period)
    edge = 0 if step == 1 else period - 1
    return jnp.where(place == edge, 0.0, pltpu.roll(x, step % rows, 0))


def local_call(body, out_shapes, scratch, flops, moved_bytes, *args, stay=None):
    return pl.pallas_call(
        body,
        out_shape=list(out_shapes),
        in_specs=[
            pl.BlockSpec(
                memory_space=pltpu.HBM if stay is not None and k >= stay else pltpu.SMEM if a.ndim == 1 else pltpu.VMEM
            )
            for k, a in enumerate(args)
        ],
        out_specs=[pl.BlockSpec(memory_space=pltpu.VMEM)] * len(out_shapes),
        scratch_shapes=scratch,
        cost_estimate=pl.CostEstimate(flops=flops, bytes_accessed=moved_bytes, transcendentals=0),
        compiler_params=pltpu.CompilerParams(vmem_limit_bytes=VMEM_LIMIT if stay is None else VMEM_MORE),
    )(*args)


def pack_kernel(saved_ref, cotangent_ref, weight_ref, *refs):
    out_ref = refs[-1]
    rows, inner = saved_ref.shape
    out_ref[:rows] = saved_ref[...]
    out_ref[rows : 2 * rows] = cotangent_ref[...]
    spare = CLASS_ROWS - weight_ref.shape[0]
    out_ref[2 * rows :] = jnp.concatenate(
        [weight_ref[...].astype(jnp.float32), jnp.zeros((spare, inner), jnp.float32)], axis=0
    ).astype(jnp.bfloat16)


def class_kernel(gathered_ref, own_ref, label_ref, grad_ref, even_ref, odd_ref, aux_ref):
    side = lax.rem(lax.axis_index("gx"), 2)
    groups, rows, inner = gathered_ref.shape[0], own_ref.shape[0], own_ref.shape[1]
    logits = jnp.zeros((CLASS_ROWS, rows), jnp.float32)
    for c in range(groups):
        weight = gathered_ref[c, 2 * rows : 2 * rows + CLASS_ROWS]
        logits += dot_nt(weight, jnp.maximum(gathered_ref[c, :rows], 0))
    place = lax.broadcasted_iota(jnp.int32, logits.shape, 0)
    real = place < CLASSES
    logits = jnp.where(real, logits, -jnp.inf)
    powers = jnp.exp(logits - jnp.max(logits, axis=0, keepdims=True))
    probabilities = powers / jnp.sum(powers, axis=0, keepdims=True)
    labels = jnp.concatenate(
        [
            label_ref[d, h : h + 1]
            for d in range(label_ref.shape[0])
            for h in range(label_ref.shape[1])
        ],
        axis=1,
    )
    onehot = jnp.where(place == labels, 1.0, 0.0)
    logit_grad = jnp.where(real, probabilities - onehot, 0.0).astype(jnp.bfloat16)
    for c in range(groups):
        weight = gathered_ref[c, 2 * rows : 2 * rows + CLASS_ROWS]
        total = gathered_ref[c, rows : 2 * rows].astype(jnp.float32) + dot_tn(logit_grad, weight)
        active = gathered_ref[c, :rows].astype(jnp.float32) > 0
        grad_ref[:, c * inner : (c + 1) * inner] = jnp.where(active, total, 0.0).astype(jnp.bfloat16)
    size = even_ref.shape[0]
    first = pl.multiple_of((rows - size) * side, size)
    even_ref[...] = grad_ref[pl.ds(rows - size - first, size)]
    odd_ref[...] = grad_ref[pl.ds(first, size)]
    aux_ref[...] = dot_nn(logit_grad, jnp.maximum(own_ref[...], 0)).astype(jnp.bfloat16)


def conv_kernel(
    grad_ref,
    even_x_ref,
    odd_x_ref,
    even_y_ref,
    odd_y_ref,
    input_ref,
    edge_ref,
    weight_ref,
    far_ref,
    out_ref,
    part_ref,
    send_ref,
    acc_ref,
    pool_ref,
):
    far_d, far_h, width, full = far_ref.shape
    depth, height = far_d - 2, far_h - 2
    inner = out_ref.shape[1]
    rows = depth * height * width
    side_x, side_y = (lax.rem(lax.axis_index(a), 2) for a in ("gx", "gy"))
    far_ref[1 : 1 + depth, 1 : 1 + height] = grad_ref[...].reshape(depth, height, width, full)
    far_ref[(far_d - 1) * (1 - side_x), 1 : 1 + height] = even_x_ref[...].reshape(height, width, full)
    far_ref[(far_d - 1) * side_x, 1 : 1 + height] = odd_x_ref[...].reshape(height, width, full)
    far_ref[:, (far_h - 1) * (1 - side_y)] = even_y_ref[...]
    far_ref[:, (far_h - 1) * side_y] = odd_y_ref[...]
    sent = far_d // 2
    send_ref[: sent * far_h * width] = far_ref[pl.ds(sent * side_x, sent)].reshape(-1, full)
    piece_rows = rows * inner // full
    for c in range(full // inner):
        send_ref[sent * far_h * width :, c * inner : (c + 1) * inner] = input_ref[
            c * piece_rows : (c + 1) * piece_rows
        ]
    total = jnp.zeros((rows, inner), jnp.float32)
    terms = [total] * 3
    for a in STEPS:
        for b in STEPS:
            piece = far_ref[1 - a : 1 - a + depth, 1 - b : 1 - b + height].reshape(rows, full)
            for c in STEPS:
                tap = 9 * (a + 1) + 3 * (b + 1) + c + 1
                terms[c + 1] += dot_nt(piece, weight_ref[:, tap * full : (tap + 1) * full])
    for c in STEPS:
        total += moved(terms[c + 1], c, width)
    out_ref[...] = total.astype(jnp.bfloat16)

    half_d, half_h, half_w = depth // 2, height // 2, width // 2
    nc = part_ref.shape[0]
    block = half_w // nc
    cells = part_ref.shape[1] - edge_ref.shape[1]
    window = cells // (half_d * half_h)
    pool_ref[...] = jnp.zeros_like(pool_ref)
    lines = total.reshape(depth, height, width, inner)
    for d in range(half_d):
        for h in range(half_h):
            acc_ref[...] = (
                lines[2 * d, 2 * h]
                + lines[2 * d, 2 * h + 1]
                + lines[2 * d + 1, 2 * h]
                + lines[2 * d + 1, 2 * h + 1]
            )
            pool_ref[d, h, 8 : 8 + half_w] = (
                acc_ref[pl.ds(0, half_w, stride=2)] + acc_ref[pl.ds(1, half_w, stride=2)]
            )
    for c in range(nc):
        start = 7 + c * block
        part_ref[c, cells:] = edge_ref[c]
        part_ref[c, :cells] = jnp.concatenate(
            [pool_ref[d, h, start : start + window] for d in range(half_d) for h in range(half_h)],
            axis=0,
        ).astype(jnp.bfloat16)


def kernel_grad_kernel(chunk, far_ref, input_ref, got_ref, *refs):
    out_refs, (flat_ref, pair_ref, turn_ref, wide_ref) = refs[:-4], refs[-4:]
    far_d, far_h, width, full = far_ref.shape
    depth, height = far_d - 2, far_h - 2
    rows, inner = input_ref.shape
    by_height = lax.axis_size("gy")
    _, by_depth, window, _ = out_refs[0].shape
    lanes = height * width
    side, at_y = lax.rem(lax.axis_index("gx"), 2), lax.axis_index("gy")
    sent = far_d // 2
    pair_ref[pl.ds(depth * side, far_d)] = far_ref[...]
    pair_ref[pl.ds(far_d * (1 - side), depth)] = got_ref[: sent * far_h * width].reshape(
        sent, far_h, width, full
    )
    piece_rows = rows * inner // full
    other = jnp.concatenate(
        [
            got_ref[sent * far_h * width :, c * inner : (c + 1) * inner]
            for c in range(full // inner)
        ],
        axis=0,
    )
    for c in STEPS:
        wide_ref[c + 1, side] = moved(input_ref[...].astype(jnp.float32), -c, width).astype(jnp.bfloat16)
        wide_ref[c + 1, 1 - side] = moved(other.astype(jnp.float32), -c, width).astype(jnp.bfloat16)
    for d in range(far_d + depth):
        for b in range(3):
            turn_ref[d, b] = pair_ref[d, b : b + height].reshape(lanes, full).T
    span = chunk * by_height
    grain = 16
    for m in range(by_depth):
        begin = span * (2 * m + side)
        for step in range((span - 1) // full + 2):
            tap = begin // full + step

            @pl.when(tap * full < begin + span)
            def _():
                a, b, c = tap // 9, lax.rem(tap // 3, 3), lax.rem(tap, 3)
                turned = jnp.concatenate([turn_ref[2 - a + d, 2 - b] for d in range(2 * depth)], axis=1)
                terms = dot_nn(turned, wide_ref[c].reshape(2 * rows, inner))
                first = pl.multiple_of(tap * full - begin + full, grain)
                flat_ref[m, pl.ds(first, full)] = terms.astype(jnp.bfloat16)

        for (q, pairs), out_ref in zip(HALVES, out_refs):
            for slot, k in enumerate(pairs):
                owner = 2 * (at_y // 2 ^ k) + q
                start = pl.multiple_of(full + owner * chunk // grain * grain, grain)
                out_ref[slot, m] = flat_ref[m, pl.ds(start, window)]


def bottom_kernel(
    down_ref, up_ref, before_ref, pre_ref, after_ref, weight_ref, aux_ref, part_ref, shift_ref
):
    _, far_d, far_w, height, filters = shift_ref.shape
    depth, width = far_d - 2, far_w - 2
    rows = depth * width * height
    channels = part_ref.shape[2]
    back = dot_nt(down_ref[...], up_ref[...])
    saved = jnp.concatenate([before_ref[...], pre_ref[...], after_ref[...]], axis=1)
    saved = saved.reshape(depth * far_w * height, filters)
    grad = jnp.where(saved.astype(jnp.float32) > 0, back, 0.0)
    shift_ref[:, :1] = jnp.zeros((3, 1) + shift_ref.shape[2:], jnp.bfloat16)
    shift_ref[:, far_d - 1 :] = jnp.zeros((3, 1) + shift_ref.shape[2:], jnp.bfloat16)
    for b in STEPS:
        shift_ref[b + 1, 1 : 1 + depth] = (
            moved(grad, b, height).astype(jnp.bfloat16).reshape(depth, far_w, height, filters)
        )
    total = jnp.zeros((rows, channels), jnp.float32)
    for a in STEPS:
        for b in STEPS:
            tap = 9 * (a + 1) + 3 * (b + 1)
            piece = jnp.concatenate(
                [
                    shift_ref[b + 1, 1 - a : 1 - a + depth, 1 - c : 1 - c + width].reshape(rows, filters)
                    for c in STEPS
                ],
                axis=1,
            )
            weight = jnp.concatenate([weight_ref[tap + c] for c in range(3)], axis=1)
            total += dot_nt(piece, weight)
    share = rows // part_ref.shape[0]
    for j in range(part_ref.shape[0]):
        part_ref[j, :share] = total[j * share : (j + 1) * share].astype(jnp.bfloat16)
        part_ref[j, share:] = aux_ref[...]


def bottom_weight_kernel(down_ref, pre_ref, source_ref, shift_ref, *refs):
    out_refs, both_ref = refs[:-1], refs[-1]
    _, far_d, far_w, height, filters = shift_ref.shape
    depth, width = far_d - 2, far_w - 2
    rows, channels = source_ref.shape
    groups = both_ref.shape[0]
    thin = channels // groups
    full = down_ref.shape[1]
    inner = full // groups
    own_down = down_ref[...].reshape(depth, far_w, height, full)[:, 1 : 1 + width].reshape(rows, full)
    own_saved = pre_ref[...].reshape(rows, filters)
    up_part = dot_tn(jnp.maximum(own_saved, 0), own_down).astype(jnp.bfloat16)
    for cc in range(groups):
        both_ref[cc, TAPS * thin :] = up_part[:, cc * inner : (cc + 1) * inner]
    turned = source_ref[...].T
    for a in STEPS:
        for b in STEPS:
            tap = 9 * (a + 1) + 3 * (b + 1)
            piece = jnp.concatenate(
                [
                    shift_ref[b + 1, 1 - a : 1 - a + depth, 1 - c : 1 - c + width].reshape(rows, filters)
                    for c in STEPS
                ],
                axis=1,
            )
            terms = dot_nn(turned, piece).astype(jnp.bfloat16)
            for c in range(3):
                for cc in range(groups):
                    both_ref[cc, (tap + c) * thin : (tap + c + 1) * thin] = terms[
                        cc * thin : (cc + 1) * thin, c * filters : (c + 1) * filters
                    ]
    at_c = lax.axis_index("col")
    for k, out_ref in enumerate(out_refs):
        out_ref[...] = both_ref[at_c ^ k]


def per_device(
    pre_bottom,
    bottom_input,
    bottom_weight,
    up_weight,
    level_input,
    pre_level,
    level_cotangent,
    labels,
    level_weight,
    aux_weight,
):
    nx, ny, nc = (lax.axis_size(a) for a in ("gx", "gy", "col"))
    at_x, at_y, at_c = (lax.axis_index(a) for a in ("gx", "gy", "col"))
    depth, height, width, inner = level_input.shape
    full = inner * nc
    rows = depth * height * width
    far_d, far_h = depth + 2, height + 2
    half_d, half_h, half_w = depth // 2, height // 2, width // 2
    block = half_w // nc
    wide = block + 2
    bottom_d, bottom_h, _, filters = pre_bottom.shape
    bf16, f32 = jnp.bfloat16, jnp.float32
    struct = jax.ShapeDtypeStruct

    own_pre = pre_level.reshape(rows, inner)
    (payload,) = local_call(
        pack_kernel,
        [struct((2 * rows + CLASS_ROWS, inner), bf16)],
        [],
        0,
        2 * pre_level.size,
        own_pre,
        level_cotangent.reshape(rows, inner),
        aux_weight.T,
        level_weight,
        level_input.reshape(rows, inner),
        up_weight,
        bottom_weight.transpose(1, 0, 2),
        stay=3,
    )
    gathered = lax.all_gather(payload, "col")
    lanes = height * width
    side_x, side_y = at_x % 2, at_y % 2
    level_pre_grad, even_x, odd_x, aux_part = local_call(
        class_kernel,
        (
            struct((rows, full), bf16),
            struct((lanes, full), bf16),
            struct((lanes, full), bf16),
            struct((CLASS_ROWS, inner), bf16),
        ),
        [],
        6 * rows * full * CLASS_ROWS,
        2 * gathered.size,
        gathered,
        own_pre,
        labels,
    )

    even_x = swap(even_x, "gx", 1)
    odd_x = swap_odd(odd_x, "gx")

    def lines(start):
        take = lambda x: x[start : start + width]
        before = jnp.where(side_x == 1, take(even_x), take(odd_x))
        after = jnp.where(side_x == 1, take(odd_x), take(even_x))
        own = level_pre_grad.reshape(depth, lanes, full)
        return jnp.stack([before] + [take(own[d]) for d in range(depth)] + [after])

    first, last = lines(0), lines(lanes - width)
    even_y = swap(jnp.where(side_y == 1, first, last), "gy", 1)
    odd_y = swap_odd(jnp.where(side_y == 1, last, first), "gy")

    turned_pre = pre_bottom.transpose(0, 2, 1, 3)
    edges = jnp.stack(
        [
            jnp.where(at_c < c, turned_pre[:, -1], turned_pre[:, 0]).reshape(-1, filters)
            for c in range(nc)
        ]
    )

    window = (wide + 7) // 8 * 8
    cells = half_d * half_h * window
    flat_input = level_input.reshape(rows, inner)
    far, level_input_grad, parts, send = local_call(
        conv_kernel,
        (
            struct((far_d, far_h, width, full), bf16),
            struct((rows, inner), bf16),
            struct((nc, cells + edges.shape[1], inner), bf16),
            struct((far_d // 2 * far_h * width + rows * inner // full, full), bf16),
        ),
        [
            pltpu.VMEM((width, inner), f32),
            pltpu.VMEM((half_d, half_h, half_w + 24, inner), f32),
        ],
        2 * rows * full * TAPS * inner,
        2 * level_weight.size,
        level_pre_grad,
        even_x,
        odd_x,
        even_y,
        odd_y,
        flat_input,
        edges,
        level_weight,
    )
    got = swap(send, "gx", 1)
    level_input_grad = level_input_grad.reshape(level_input.shape)

    relayed = exchange(parts, "col")
    edges = relayed[:, cells:].reshape(nc, bottom_d, 1, bottom_h, filters)
    relayed = relayed[:, :cells].reshape(nc * cells, inner)

    def edge_of(c):
        found = lax.dynamic_index_in_dim(edges, jnp.clip(c, 0, nc - 1), 0, keepdims=False)
        return jnp.where((c >= 0) & (c < nc), found, jnp.zeros_like(found))

    pre_before, pre_after = edge_of(at_c - 1), edge_of(at_c + 1)

    chunk = TAPS * full // (nx * ny)
    span = chunk + 8 if chunk % 16 else chunk
    level_parts = local_call(
        functools.partial(kernel_grad_kernel, chunk),
        [struct((2, nx // 2, span, inner), bf16)] * 4,
        [
            pltpu.VMEM((nx // 2, (chunk * ny - 1) // full * full + 4 * full, inner), bf16),
            pltpu.VMEM((far_d + depth, far_h, width, full), bf16),
            pltpu.VMEM((far_d + depth, 3, full, lanes), bf16),
            pltpu.VMEM((3, 2, rows, inner), bf16),
        ],
        2 * rows * full * TAPS * inner,
        2 * nx * ny * span * inner,
        far,
        flat_input,
        got,
    )
    def first_sum(kept, sent, bit):
        return kept.astype(f32) + swap(sent, "gy", bit).astype(f32)

    even_sum = first_sum(level_parts[0], level_parts[1], 2)
    odd_sum = first_sum(level_parts[2], level_parts[3], 6)
    relayed = behind(relayed, level_parts[0])

    by_depth = spread(jnp.concatenate([relayed, aux_part]), "gx")
    aux_sum = by_depth[:, nc * cells :].astype(f32).sum(axis=0).astype(bf16)
    line = by_depth[:, : nc * cells].reshape(nx, nc, half_d * half_h, window, inner)[:, :, :, :wide]
    split = nx * nc * half_d * half_h * wide
    down_wide = (
        spread(line.reshape(split, inner), "gy")
        .reshape(ny, nx, nc, half_d, half_h, wide, inner)
        .transpose(1, 3, 5, 0, 4, 2, 6)
        .reshape(bottom_d * wide * bottom_h, full)
    )

    even_sum = first_sum(even_sum[0], even_sum[1].astype(bf16), 6)
    odd_sum = first_sum(odd_sum[0], odd_sum[1].astype(bf16), 2)
    down_wide = behind(down_wide, even_sum, odd_sum)
    kept_sum, sent_sum = mine_and_other(jnp.stack([even_sum, odd_sum]), "gy", 1, 0)
    got_sum = swap(sent_sum.astype(bf16), "gy", 1)

    bottom_rows = bottom_d * block * bottom_h
    channel_width = bottom_weight.shape[0]
    thin = channel_width // nc
    part, shifts = local_call(
        bottom_kernel,
        (
            struct((ny, bottom_rows // ny + CLASS_ROWS, channel_width), bf16),
            struct((3, bottom_d + 2, wide, bottom_h, filters), bf16),
        ),
        [],
        2 * bottom_rows * channel_width * TAPS * filters,
        2 * bottom_weight.size,
        down_wide,
        up_weight,
        pre_before,
        turned_pre,
        pre_after,
        bottom_weight.transpose(1, 0, 2),
        aux_sum,
    )
    both = local_call(
        bottom_weight_kernel,
        [struct((TAPS * thin + filters, inner), bf16)] * nc,
        [pltpu.VMEM((nc, TAPS * thin + filters, inner), bf16)],
        2 * bottom_rows * channel_width * TAPS * filters,
        2 * bottom_weight.size,
        down_wide,
        turned_pre,
        bottom_input.transpose(0, 2, 1, 3).reshape(bottom_rows, channel_width),
        shifts,
    )
    level_part = kept_sum + behind(got_sum, part).astype(f32)
    part = exchange(part, "gy")
    share = bottom_rows // ny
    aux_weight_grad = part[:, share : share + CLASSES].astype(f32).sum(axis=0).T
    level_part = summed_by_pairs(level_part, "gx", bits_of("gx")[:-1], bits_of("gx")[-2::-1], part)
    if span != chunk:
        odd = lax.rem(at_y + at_x * ny, 2)
        level_part = jnp.where(odd == 1, level_part[span - chunk :], level_part[:chunk])
    level_weight_grad = level_part.T
    share = bottom_d // ny
    bottom_input_grad = (
        part[:, : bottom_rows // ny]
        .astype(f32)
        .sum(axis=0)
        .astype(bf16)
        .reshape(share, block, bottom_h, channel_width)
        .transpose(0, 2, 1, 3)
    )
    both = [both[k] if k == 0 else swap(both[k], "col", k) for k in range(nc)]
    bottom_weight_grad = sum(x[: TAPS * thin].astype(f32) for x in both)
    bottom_weight_grad = bottom_weight_grad.reshape(TAPS, thin, filters).transpose(1, 0, 2)
    up_weight_grad = sum(x[TAPS * thin :].astype(f32) for x in both)
    return (
        level_input_grad,
        bottom_input_grad,
        level_weight_grad,
        bottom_weight_grad,
        up_weight_grad,
        aux_weight_grad,
    )


def solution(mesh):
    return jax.shard_map(
        per_device,
        mesh=mesh,
        in_specs=(
            P(None, None, "col", "gy"),
            P(None, None, "col", "gx"),
            P("gx", None, "gy"),
            P("gy", None),
            P("gx", "gy", None, "col"),
            P("gx", "gy", None, "col"),
            P("gx", "gy", None, "col"),
            P("gx", "gy", None),
            P("col", None),
            P("col", None),
        ),
        out_specs=(
            P("gx", "gy", None, "col"),
            P("gy", None, "col", "gx"),
            P("col", ("gx", "gy")),
            P(("gx", "col"), None, "gy"),
            P("gy", "col"),
            P("col", None),
        ),
        check_vma=False,
    )
```

```python
import functools

import jax
import jax.numpy as jnp
from jax import lax
from jax.experimental import pallas as pl
from jax.experimental.pallas import tpu as pltpu
from jax.sharding import PartitionSpec as P

CLASSES = 14
CLASS_ROWS = 16
TAPS = 27
VMEM_LIMIT = 24 * 1024 * 1024
VMEM_MORE = 60 * 1024 * 1024
STEPS = (-1, 0, 1)
HALVES = ((0, (0, 3)), (0, (1, 2)), (1, (0, 1)), (1, (3, 2)))


def exchange(x, axis):
    return lax.all_to_all(x, axis, split_axis=0, concat_axis=0, tiled=False)


def spread(x, axis):
    size = lax.axis_size(axis)
    return exchange(jnp.broadcast_to(x[None], (size,) + x.shape), axis)


def behind(x, *others):
    return lax.optimization_barrier((x,) + others)[0]


def bits_of(axis):
    return [1 << k for k in reversed(range(lax.axis_size(axis).bit_length() - 1))]


def swap(x, axis, bit):
    return lax.ppermute(x, axis, [(i, i ^ bit) for i in range(lax.axis_size(axis))])


def swap_odd(x, axis):
    last = lax.axis_size(axis) - 1
    return lax.ppermute(
        x, axis, [(i, i + 1 if i % 2 else i - 1) for i in range(1, last)]
    )


def mine_and_other(x, axis, bit, dim):
    own = lax.axis_index(axis) // bit % 2
    take = functools.partial(lax.dynamic_index_in_dim, x, axis=dim, keepdims=False)
    return take(own), take(1 - own)


def summed_by_pairs(x, axis, bits, order, first=None):
    x = x.reshape((2,) * len(bits) + x.shape[1:])
    left = list(bits)
    for bit in order:
        if bit == order[-1] and first is not None:
            x = behind(x, first)
        own, other = mine_and_other(x, axis, bit, left.index(bit))
        left.remove(bit)
        x = own.astype(jnp.float32) + swap(other.astype(jnp.bfloat16), axis, bit).astype(jnp.float32)
    return x


def dot_nn(a, b):
    return lax.dot_general(a, b, (((1,), (0,)), ((), ())), preferred_element_type=jnp.float32)


def dot_tn(a, b):
    return lax.dot_general(a, b, (((0,), (0,)), ((), ())), preferred_element_type=jnp.float32)


def dot_nt(a, b):
    return lax.dot_general(a, b, (((1,), (1,)), ((), ())), preferred_element_type=jnp.float32)


def moved(x, step, period):
    if step == 0:
        return x
    rows = x.shape[0]
    place = lax.rem(lax.broadcasted_iota(jnp.int32, x.shape, 0), period)
    edge = 0 if step == 1 else period - 1
    return jnp.where(place == edge, 0.0, pltpu.roll(x, step % rows, 0))


def local_call(body, out_shapes, scratch, flops, moved_bytes, *args, stay=None):
    return pl.pallas_call(
        body,
        out_shape=list(out_shapes),
        in_specs=[
            pl.BlockSpec(
                memory_space=pltpu.HBM if stay is not None and k >= stay else pltpu.SMEM if a.ndim == 1 else pltpu.VMEM
            )
            for k, a in enumerate(args)
        ],
        out_specs=[pl.BlockSpec(memory_space=pltpu.VMEM)] * len(out_shapes),
        scratch_shapes=scratch,
        cost_estimate=pl.CostEstimate(flops=flops, bytes_accessed=moved_bytes, transcendentals=0),
        compiler_params=pltpu.CompilerParams(vmem_limit_bytes=VMEM_LIMIT if stay is None else VMEM_MORE),
    )(*args)


def pack_kernel(saved_ref, cotangent_ref, weight_ref, *refs):
    out_ref = refs[-1]
    rows, inner = saved_ref.shape
    out_ref[:rows] = saved_ref[...]
    out_ref[rows : 2 * rows] = cotangent_ref[...]
    spare = CLASS_ROWS - weight_ref.shape[0]
    out_ref[2 * rows :] = jnp.concatenate(
        [weight_ref[...].astype(jnp.float32), jnp.zeros((spare, inner), jnp.float32)], axis=0
    ).astype(jnp.bfloat16)


def class_kernel(gathered_ref, own_ref, label_ref, grad_ref, even_ref, odd_ref, aux_ref):
    side = lax.rem(lax.axis_index("gx"), 2)
    groups, rows, inner = gathered_ref.shape[0], own_ref.shape[0], own_ref.shape[1]
    logits = jnp.zeros((CLASS_ROWS, rows), jnp.float32)
    for c in range(groups):
        weight = gathered_ref[c, 2 * rows : 2 * rows + CLASS_ROWS]
        logits += dot_nt(weight, jnp.maximum(gathered_ref[c, :rows], 0))
    place = lax.broadcasted_iota(jnp.int32, logits.shape, 0)
    real = place < CLASSES
    logits = jnp.where(real, logits, -jnp.inf)
    powers = jnp.exp(logits - jnp.max(logits, axis=0, keepdims=True))
    probabilities = powers / jnp.sum(powers, axis=0, keepdims=True)
    labels = jnp.concatenate(
        [
            label_ref[d, h : h + 1]
            for d in range(label_ref.shape[0])
            for h in range(label_ref.shape[1])
        ],
        axis=1,
    )
    onehot = jnp.where(place == labels, 1.0, 0.0)
    logit_grad = jnp.where(real, probabilities - onehot, 0.0).astype(jnp.bfloat16)
    for c in range(groups):
        weight = gathered_ref[c, 2 * rows : 2 * rows + CLASS_ROWS]
        total = gathered_ref[c, rows : 2 * rows].astype(jnp.float32) + dot_tn(logit_grad, weight)
        active = gathered_ref[c, :rows].astype(jnp.float32) > 0
        grad_ref[:, c * inner : (c + 1) * inner] = jnp.where(active, total, 0.0).astype(jnp.bfloat16)
    size = even_ref.shape[0]
    first = pl.multiple_of((rows - size) * side, size)
    even_ref[...] = grad_ref[pl.ds(rows - size - first, size)]
    odd_ref[...] = grad_ref[pl.ds(first, size)]
    aux_ref[...] = dot_nn(logit_grad, jnp.maximum(own_ref[...], 0)).astype(jnp.bfloat16)


def conv_kernel(
    grad_ref,
    even_x_ref,
    odd_x_ref,
    even_y_ref,
    odd_y_ref,
    input_ref,
    edge_ref,
    weight_ref,
    far_ref,
    out_ref,
    part_ref,
    send_ref,
    acc_ref,
    pool_ref,
):
    far_d, far_h, width, full = far_ref.shape
    depth, height = far_d - 2, far_h - 2
    inner = out_ref.shape[1]
    rows = depth * height * width
    side_x, side_y = (lax.rem(lax.axis_index(a), 2) for a in ("gx", "gy"))
    far_ref[1 : 1 + depth, 1 : 1 + height] = grad_ref[...].reshape(depth, height, width, full)
    far_ref[(far_d - 1) * (1 - side_x), 1 : 1 + height] = even_x_ref[...].reshape(height, width, full)
    far_ref[(far_d - 1) * side_x, 1 : 1 + height] = odd_x_ref[...].reshape(height, width, full)
    far_ref[:, (far_h - 1) * (1 - side_y)] = even_y_ref[...]
    far_ref[:, (far_h - 1) * side_y] = odd_y_ref[...]
    sent = far_d // 2
    send_ref[: sent * far_h * width] = far_ref[pl.ds(sent * side_x, sent)].reshape(-1, full)
    piece_rows = rows * inner // full
    for c in range(full // inner):
        send_ref[sent * far_h * width :, c * inner : (c + 1) * inner] = input_ref[
            c * piece_rows : (c + 1) * piece_rows
        ]
    total = jnp.zeros((rows, inner), jnp.float32)
    terms = [total] * 3
    for a in STEPS:
        for b in STEPS:
            piece = far_ref[1 - a : 1 - a + depth, 1 - b : 1 - b + height].reshape(rows, full)
            for c in STEPS:
                tap = 9 * (a + 1) + 3 * (b + 1) + c + 1
                terms[c + 1] += dot_nt(piece, weight_ref[:, tap * full : (tap + 1) * full])
    for c in STEPS:
        total += moved(terms[c + 1], c, width)
    out_ref[...] = total.astype(jnp.bfloat16)

    half_d, half_h, half_w = depth // 2, height // 2, width // 2
    nc = part_ref.shape[0]
    block = half_w // nc
    cells = part_ref.shape[1] - edge_ref.shape[1]
    window = cells // (half_d * half_h)
    pool_ref[...] = jnp.zeros_like(pool_ref)
    lines = total.reshape(depth, height, width, inner)
    for d in range(half_d):
        for h in range(half_h):
            acc_ref[...] = (
                lines[2 * d, 2 * h]
                + lines[2 * d, 2 * h + 1]
                + lines[2 * d + 1, 2 * h]
                + lines[2 * d + 1, 2 * h + 1]
            )
            pool_ref[d, h, 8 : 8 + half_w] = (
                acc_ref[pl.ds(0, half_w, stride=2)] + acc_ref[pl.ds(1, half_w, stride=2)]
            )
    for c in range(nc):
        start = 7 + c * block
        part_ref[c, cells:] = edge_ref[c]
        part_ref[c, :cells] = jnp.concatenate(
            [pool_ref[d, h, start : start + window] for d in range(half_d) for h in range(half_h)],
            axis=0,
        ).astype(jnp.bfloat16)


def kernel_grad_kernel(chunk, far_ref, input_ref, got_ref, *refs):
    out_refs, (flat_ref, pair_ref, turn_ref, wide_ref) = refs[:-4], refs[-4:]
    far_d, far_h, width, full = far_ref.shape
    depth, height = far_d - 2, far_h - 2
    rows, inner = input_ref.shape
    by_height = lax.axis_size("gy")
    _, by_depth, window, _ = out_refs[0].shape
    lanes = height * width
    side, at_y = lax.rem(lax.axis_index("gx"), 2), lax.axis_index("gy")
    sent = far_d // 2
    pair_ref[pl.ds(depth * side, far_d)] = far_ref[...]
    pair_ref[pl.ds(far_d * (1 - side), depth)] = got_ref[: sent * far_h * width].reshape(
        sent, far_h, width, full
    )
    piece_rows = rows * inner // full
    other = jnp.concatenate(
        [
            got_ref[sent * far_h * width :, c * inner : (c + 1) * inner]
            for c in range(full // inner)
        ],
        axis=0,
    )
    for c in STEPS:
        wide_ref[c + 1, side] = moved(input_ref[...].astype(jnp.float32), -c, width).astype(jnp.bfloat16)
        wide_ref[c + 1, 1 - side] = moved(other.astype(jnp.float32), -c, width).astype(jnp.bfloat16)
    for d in range(far_d + depth):
        for b in range(3):
            turn_ref[d, b] = pair_ref[d, b : b + height].reshape(lanes, full).T
    span = chunk * by_height
    grain = 16
    for m in range(by_depth):
        begin = span * (2 * m + side)
        for step in range((span - 1) // full + 2):
            tap = begin // full + step

            @pl.when(tap * full < begin + span)
            def _():
                a, b, c = tap // 9, lax.rem(tap // 3, 3), lax.rem(tap, 3)
                turned = jnp.concatenate([turn_ref[2 - a + d, 2 - b] for d in range(2 * depth)], axis=1)
                terms = dot_nn(turned, wide_ref[c].reshape(2 * rows, inner))
                first = pl.multiple_of(tap * full - begin + full, grain)
                flat_ref[m, pl.ds(first, full)] = terms.astype(jnp.bfloat16)

        for (q, pairs), out_ref in zip(HALVES, out_refs):
            for slot, k in enumerate(pairs):
                owner = 2 * (at_y // 2 ^ k) + q
                start = pl.multiple_of(full + owner * chunk // grain * grain, grain)
                out_ref[slot, m] = flat_ref[m, pl.ds(start, window)]


def bottom_kernel(
    down_ref, up_ref, before_ref, pre_ref, after_ref, weight_ref, aux_ref, part_ref, shift_ref
):
    _, far_d, far_w, height, filters = shift_ref.shape
    depth, width = far_d - 2, far_w - 2
    rows = depth * width * height
    channels = part_ref.shape[2]
    back = dot_nt(down_ref[...], up_ref[...])
    saved = jnp.concatenate([before_ref[...], pre_ref[...], after_ref[...]], axis=1)
    saved = saved.reshape(depth * far_w * height, filters)
    grad = jnp.where(saved.astype(jnp.float32) > 0, back, 0.0)
    shift_ref[:, :1] = jnp.zeros((3, 1) + shift_ref.shape[2:], jnp.bfloat16)
    shift_ref[:, far_d - 1 :] = jnp.zeros((3, 1) + shift_ref.shape[2:], jnp.bfloat16)
    for b in STEPS:
        shift_ref[b + 1, 1 : 1 + depth] = (
            moved(grad, b, height).astype(jnp.bfloat16).reshape(depth, far_w, height, filters)
        )
    total = jnp.zeros((rows, channels), jnp.float32)
    for a in STEPS:
        for b in STEPS:
            tap = 9 * (a + 1) + 3 * (b + 1)
            piece = jnp.concatenate(
                [
                    shift_ref[b + 1, 1 - a : 1 - a + depth, 1 - c : 1 - c + width].reshape(rows, filters)
                    for c in STEPS
                ],
                axis=1,
            )
            weight = jnp.concatenate([weight_ref[tap + c] for c in range(3)], axis=1)
            total += dot_nt(piece, weight)
    share = rows // part_ref.shape[0]
    for j in range(part_ref.shape[0]):
        part_ref[j, :share] = total[j * share : (j + 1) * share].astype(jnp.bfloat16)
        part_ref[j, share:] = aux_ref[...]


def bottom_weight_kernel(down_ref, pre_ref, source_ref, shift_ref, *refs):
    out_refs, both_ref = refs[:-1], refs[-1]
    _, far_d, far_w, height, filters = shift_ref.shape
    depth, width = far_d - 2, far_w - 2
    rows, channels = source_ref.shape
    groups = both_ref.shape[0]
    thin = channels // groups
    full = down_ref.shape[1]
    inner = full // groups
    own_down = down_ref[...].reshape(depth, far_w, height, full)[:, 1 : 1 + width].reshape(rows, full)
    own_saved = pre_ref[...].reshape(rows, filters)
    up_part = dot_tn(jnp.maximum(own_saved, 0), own_down).astype(jnp.bfloat16)
    for cc in range(groups):
        both_ref[cc, TAPS * thin :] = up_part[:, cc * inner : (cc + 1) * inner]
    turned = source_ref[...].T
    for a in STEPS:
        for b in STEPS:
            tap = 9 * (a + 1) + 3 * (b + 1)
            piece = jnp.concatenate(
                [
                    shift_ref[b + 1, 1 - a : 1 - a + depth, 1 - c : 1 - c + width].reshape(rows, filters)
                    for c in STEPS
                ],
                axis=1,
            )
            terms = dot_nn(turned, piece).astype(jnp.bfloat16)
            for c in range(3):
                for cc in range(groups):
                    both_ref[cc, (tap + c) * thin : (tap + c + 1) * thin] = terms[
                        cc * thin : (cc + 1) * thin, c * filters : (c + 1) * filters
                    ]
    at_c = lax.axis_index("col")
    for k, out_ref in enumerate(out_refs):
        out_ref[...] = both_ref[at_c ^ k]


def per_device(
    pre_bottom,
    bottom_input,
    bottom_weight,
    up_weight,
    level_input,
    pre_level,
    level_cotangent,
    labels,
    level_weight,
    aux_weight,
):
    nx, ny, nc = (lax.axis_size(a) for a in ("gx", "gy", "col"))
    at_x, at_y, at_c = (lax.axis_index(a) for a in ("gx", "gy", "col"))
    depth, height, width, inner = level_input.shape
    full = inner * nc
    rows = depth * height * width
    far_d, far_h = depth + 2, height + 2
    half_d, half_h, half_w = depth // 2, height // 2, width // 2
    block = half_w // nc
    wide = block + 2
    bottom_d, bottom_h, _, filters = pre_bottom.shape
    bf16, f32 = jnp.bfloat16, jnp.float32
    struct = jax.ShapeDtypeStruct

    own_pre = pre_level.reshape(rows, inner)
    (payload,) = local_call(
        pack_kernel,
        [struct((2 * rows + CLASS_ROWS, inner), bf16)],
        [],
        0,
        2 * pre_level.size,
        own_pre,
        level_cotangent.reshape(rows, inner),
        aux_weight.T,
        level_weight,
        level_input.reshape(rows, inner),
        up_weight,
        bottom_weight.transpose(1, 0, 2),
        stay=3,
    )
    gathered = lax.all_gather(payload, "col")
    lanes = height * width
    side_x, side_y = at_x % 2, at_y % 2
    level_pre_grad, even_x, odd_x, aux_part = local_call(
        class_kernel,
        (
            struct((rows, full), bf16),
            struct((lanes, full), bf16),
            struct((lanes, full), bf16),
            struct((CLASS_ROWS, inner), bf16),
        ),
        [],
        6 * rows * full * CLASS_ROWS,
        2 * gathered.size,
        gathered,
        own_pre,
        labels,
    )

    even_x = swap(even_x, "gx", 1)
    odd_x = swap_odd(odd_x, "gx")

    def lines(start):
        take = lambda x: x[start : start + width]
        before = jnp.where(side_x == 1, take(even_x), take(odd_x))
        after = jnp.where(side_x == 1, take(odd_x), take(even_x))
        own = level_pre_grad.reshape(depth, lanes, full)
        return jnp.stack([before] + [take(own[d]) for d in range(depth)] + [after])

    first, last = lines(0), lines(lanes - width)
    even_y = swap(jnp.where(side_y == 1, first, last), "gy", 1)
    odd_y = swap_odd(jnp.where(side_y == 1, last, first), "gy")

    turned_pre = pre_bottom.transpose(0, 2, 1, 3)
    edges = jnp.stack(
        [
            jnp.where(at_c < c, turned_pre[:, -1], turned_pre[:, 0]).reshape(-1, filters)
            for c in range(nc)
        ]
    )

    window = (wide + 7) // 8 * 8
    cells = half_d * half_h * window
    flat_input = level_input.reshape(rows, inner)
    far, level_input_grad, parts, send = local_call(
        conv_kernel,
        (
            struct((far_d, far_h, width, full), bf16),
            struct((rows, inner), bf16),
            struct((nc, cells + edges.shape[1], inner), bf16),
            struct((far_d // 2 * far_h * width + rows * inner // full, full), bf16),
        ),
        [
            pltpu.VMEM((width, inner), f32),
            pltpu.VMEM((half_d, half_h, half_w + 24, inner), f32),
        ],
        2 * rows * full * TAPS * inner,
        2 * level_weight.size,
        level_pre_grad,
        even_x,
        odd_x,
        even_y,
        odd_y,
        flat_input,
        edges,
        level_weight,
    )
    got = swap(send, "gx", 1)
    level_input_grad = level_input_grad.reshape(level_input.shape)

    relayed = exchange(parts, "col")
    edges = relayed[:, cells:].reshape(nc, bottom_d, 1, bottom_h, filters)
    relayed = relayed[:, :cells].reshape(nc * cells, inner)

    def edge_of(c):
        found = lax.dynamic_index_in_dim(edges, jnp.clip(c, 0, nc - 1), 0, keepdims=False)
        return jnp.where((c >= 0) & (c < nc), found, jnp.zeros_like(found))

    pre_before, pre_after = edge_of(at_c - 1), edge_of(at_c + 1)

    chunk = TAPS * full // (nx * ny)
    span = chunk + 8 if chunk % 16 else chunk
    level_parts = local_call(
        functools.partial(kernel_grad_kernel, chunk),
        [struct((2, nx // 2, span, inner), bf16)] * 4,
        [
            pltpu.VMEM((nx // 2, (chunk * ny - 1) // full * full + 4 * full, inner), bf16),
            pltpu.VMEM((far_d + depth, far_h, width, full), bf16),
            pltpu.VMEM((far_d + depth, 3, full, lanes), bf16),
            pltpu.VMEM((3, 2, rows, inner), bf16),
        ],
        2 * rows * full * TAPS * inner,
        2 * nx * ny * span * inner,
        far,
        flat_input,
        got,
    )
    def first_sum(kept, sent, bit):
        return kept.astype(f32) + swap(sent, "gy", bit).astype(f32)

    even_sum = first_sum(level_parts[0], level_parts[1], 2)
    odd_sum = first_sum(level_parts[2], level_parts[3], 6)
    relayed = behind(relayed, level_parts[0])

    by_depth = spread(jnp.concatenate([relayed, aux_part]), "gx")
    aux_sum = by_depth[:, nc * cells :].astype(f32).sum(axis=0).astype(bf16)
    line = by_depth[:, : nc * cells].reshape(nx, nc, half_d * half_h, window, inner)[:, :, :, :wide]
    split = nx * nc * half_d * half_h * wide
    down_wide = (
        spread(line.reshape(split, inner), "gy")
        .reshape(ny, nx, nc, half_d, half_h, wide, inner)
        .transpose(1, 3, 5, 0, 4, 2, 6)
        .reshape(bottom_d * wide * bottom_h, full)
    )

    even_sum = first_sum(even_sum[0], even_sum[1].astype(bf16), 6)
    odd_sum = first_sum(odd_sum[0], odd_sum[1].astype(bf16), 2)
    down_wide = behind(down_wide, even_sum, odd_sum)
    kept_sum, sent_sum = mine_and_other(jnp.stack([even_sum, odd_sum]), "gy", 1, 0)
    got_sum = swap(sent_sum.astype(bf16), "gy", 1)

    bottom_rows = bottom_d * block * bottom_h
    channel_width = bottom_weight.shape[0]
    thin = channel_width // nc
    part, shifts = local_call(
        bottom_kernel,
        (
            struct((ny, bottom_rows // ny + CLASS_ROWS, channel_width), bf16),
            struct((3, bottom_d + 2, wide, bottom_h, filters), bf16),
        ),
        [],
        2 * bottom_rows * channel_width * TAPS * filters,
        2 * bottom_weight.size,
        down_wide,
        up_weight,
        pre_before,
        turned_pre,
        pre_after,
        bottom_weight.transpose(1, 0, 2),
        aux_sum,
    )
    both = local_call(
        bottom_weight_kernel,
        [struct((TAPS * thin + filters, inner), bf16)] * nc,
        [pltpu.VMEM((nc, TAPS * thin + filters, inner), bf16)],
        2 * bottom_rows * channel_width * TAPS * filters,
        2 * bottom_weight.size,
        down_wide,
        turned_pre,
        bottom_input.transpose(0, 2, 1, 3).reshape(bottom_rows, channel_width),
        shifts,
    )
    level_part = kept_sum + behind(got_sum, both[0]).astype(f32)
    part = exchange(behind(part, both[0]), "gy")
    share = bottom_rows // ny
    aux_weight_grad = part[:, share : share + CLASSES].astype(f32).sum(axis=0).T
    level_part = summed_by_pairs(level_part, "gx", bits_of("gx")[:-1], bits_of("gx")[-2::-1], part)
    if span != chunk:
        odd = lax.rem(at_y + at_x * ny, 2)
        level_part = jnp.where(odd == 1, level_part[span - chunk :], level_part[:chunk])
    level_weight_grad = level_part.T
    share = bottom_d // ny
    bottom_input_grad = (
        part[:, : bottom_rows // ny]
        .astype(f32)
        .sum(axis=0)
        .astype(bf16)
        .reshape(share, block, bottom_h, channel_width)
        .transpose(0, 2, 1, 3)
    )
    both = [both[k] if k == 0 else swap(both[k], "col", k) for k in range(nc)]
    bottom_weight_grad = sum(x[: TAPS * thin].astype(f32) for x in both)
    bottom_weight_grad = bottom_weight_grad.reshape(TAPS, thin, filters).transpose(1, 0, 2)
    up_weight_grad = sum(x[TAPS * thin :].astype(f32) for x in both)
    return (
        level_input_grad,
        bottom_input_grad,
        level_weight_grad,
        bottom_weight_grad,
        up_weight_grad,
        aux_weight_grad,
    )


def solution(mesh):
    return jax.shard_map(
        per_device,
        mesh=mesh,
        in_specs=(
            P(None, None, "col", "gy"),
            P(None, None, "col", "gx"),
            P("gx", None, "gy"),
            P("gy", None),
            P("gx", "gy", None, "col"),
            P("gx", "gy", None, "col"),
            P("gx", "gy", None, "col"),
            P("gx", "gy", None),
            P("col", None),
            P("col", None),
        ),
        out_specs=(
            P("gx", "gy", None, "col"),
            P("gy", None, "col", "gx"),
            P("col", ("gx", "gy")),
            P(("gx", "col"), None, "gy"),
            P("gy", "col"),
            P("col", None),
        ),
        check_vma=False,
    )
```
